128 devices in a mesh: dp: 32 (over z, x, core), tensor: 4 (over y).
Axes of the slice: x: 4, y: 4, z: 4, core: 2. Of those that a mesh axis runs over, the one named last changes fastest.
Arguments:
- tokens: bfloat16 [12288, 2048], P('dp'), may hold values from -6 to 6
- norm1_gain: bfloat16 [2048], replicated, may hold values from 0.25 to 1.75
- w_query: bfloat16 [2048, 2048], P(None, 'tensor'), may hold values from -0.125 to 0.125
- w_key: bfloat16 [2048, 512], P(None, 'tensor'), may hold values from -0.125 to 0.125
- w_value: bfloat16 [2048, 512], P(None, 'tensor'), may hold values from -0.125 to 0.125
- w_output: bfloat16 [2048, 2048], P('tensor'), may hold values from -0.375 to 0.375
- norm2_gain: bfloat16 [2048], replicated, may hold values from 0.25 to 1.75
- w_gate: bfloat16 [2048, 8192], P(None, 'tensor'), may hold values from -0.125 to 0.125
- w_up: bfloat16 [2048, 8192], P(None, 'tensor'), may hold values from -0.125 to 0.125
- w_down: bfloat16 [8192, 2048], P('tensor'), may hold values from -0.0625 to 0.0625
- cotangent: bfloat16 [12288, 2048], P('dp'), may hold values from -6 to 6
- first_len: int32 [64], P('dp'), may hold values from 96 to 192
- live_rows: int32 [32], P('dp'), may hold values from 1 to 2, as said below
Outputs:
- layer_out: bfloat16 [12288, 2048], P('dp')
- grad_tokens: float32 [12288, 2048], P('dp')
- grad_norm1: float32 [2048], P('dp')
- grad_query: float32 [2048, 2048], P('dp', 'tensor')
- grad_key: float32 [2048, 512], P('dp', 'tensor')
- grad_value: float32 [2048, 512], P('dp', 'tensor')
- grad_output: float32 [2048, 2048], P('tensor', 'dp')
- grad_norm2: float32 [2048], P('dp')
- grad_gate: float32 [2048, 8192], P('dp', 'tensor')
- grad_up: float32 [2048, 8192], P('dp', 'tensor')
- grad_down: float32 [8192, 2048], P('tensor', 'dp')
The draws below stay inside these ranges and needn't reach their ends.
Inputs may be any that keep to these rules, and one draw needn't show every extreme that they name: `live_rows`: each index of dp holds its live rows in its first slots; some index holds 2 live rows in every draw.
All inputs are finite; a program needn't handle non-finite values.
Results may differ from the reference program's by a relative error of at most 0.014.
Values sent between devices are 32-bit elements; how exact they have to be, the bound alone decides.
No kernel may reach another device: no remote copies, remote signals or barrier semaphores. Data moves between devices by JAX's collectives and lax.ppermute only.
A program may use at most 256 MiB of HBM per device.

```python
import math
import jax
import jax.numpy as jnp
from jax import lax

D = 2048
HEADS = 32
KV_HEADS = 8
HEAD_DIM = 64
FF = 8192
ROW = 192
ROWS_DEV = 2
GROUPS = 32
ROWS = 64
TOKENS = 12288


def draw_live_rows(key, part):
    key = jax.random.fold_in(key, 7)
    key_counts, key_busiest = jax.random.split(key)
    counts_drawn = jax.random.randint(key_counts, (GROUPS,), 1, ROWS_DEV + 1)
    busiest = jax.random.randint(key_busiest, (), 0, GROUPS)
    return jnp.where(jnp.arange(GROUPS) == busiest, ROWS_DEV, counts_drawn).astype(jnp.int32)


def with_ends(drawn, own_key, low, largest):
    spot = [jax.random.randint(jax.random.fold_in(own_key, axis), (), 0, length) for axis, length in enumerate(drawn.shape)]
    longest = drawn.shape.index(max(drawn.shape))
    neighbour = spot[:longest] + [(spot[longest] + 1) % drawn.shape[longest]] + spot[longest + 1:]
    return drawn.at[tuple(spot)].set(low).at[tuple(neighbour)].set(largest)


def with_spikes(array, key, source, target, parts, factor):
    def block_of(axis_at):
        return (jnp.arange(array.shape[axis_at]) // (array.shape[axis_at] // parts)).reshape((-1,) + (1,) * (array.ndim - 1 - axis_at))

    near = jax.random.permutation(key, parts)[block_of(target)]
    second = (block_of(target) + parts // 2) % parts
    return jnp.where((block_of(source) == near) | (block_of(source) == second), factor * array, array)


def block_scale(key, dims, cuts, smallest, high):
    factor_of, own = 1.0, jax.random.fold_in(key, 6)
    for dim, blocks in cuts:
        heights = jnp.exp(jax.random.uniform(jax.random.fold_in(own, dim), (blocks,), jnp.float32, smallest / len(cuts), high / len(cuts)))
        factor_of = factor_of * jnp.repeat(heights, dims[dim] // blocks).reshape([-1 if axis == dim else 1 for axis in range(len(dims))])
    return factor_of


def normal_values(rng, shape, deviation, most, shards=(), held_as=jnp.bfloat16):
    loudness = block_scale(rng, shape, shards, -0.22, 0.18) if shards else 1.0
    entries = jax.random.normal(rng, shape, jnp.float32) * deviation * loudness
    return jnp.minimum(jnp.maximum(entries, -most), most).astype(held_as)


def bell_draw_with(own_key, dims, spread, reach, shards, heavy, kind=jnp.bfloat16):
    drawn = spread * jax.random.normal(own_key, dims, jnp.float32)
    if shards:
        drawn = drawn * block_scale(own_key, dims, shards, -0.22, 0.18)
    return jnp.clip(with_spikes(drawn, jax.random.fold_in(own_key, 3), *heavy), -reach, reach).astype(kind)


def setup_inputs(seed: int = 0) -> dict:
    key_list = jax.random.split(jax.random.key(seed), 14)
    return {
        "tokens": normal_values(key_list[0], (TOKENS, D), 1.0, 6.0, ((0, 32),)),
        "norm1_gain": jnp.clip(1.0 + 0.15 * jax.random.normal(key_list[1], (D,), jnp.float32), 0.25, 1.75).astype(jnp.bfloat16),
        "w_query": normal_values(key_list[2], (D, HEADS * HEAD_DIM), D ** -0.5, 0.125, ((1, 4),)),
        "w_key": normal_values(key_list[3], (D, KV_HEADS * HEAD_DIM), D ** -0.5, 0.125, ((1, 4),)),
        "w_value": normal_values(key_list[4], (D, KV_HEADS * HEAD_DIM), D ** -0.5, 0.125, ((1, 4),)),
        "w_output": normal_values(key_list[5], (HEADS * HEAD_DIM, D), (HEADS * HEAD_DIM // 8) ** -0.5, 0.375, ((0, 4),)),
        "norm2_gain": jnp.clip(1.0 + 0.15 * jax.random.normal(key_list[6], (D,), jnp.float32), 0.25, 1.75).astype(jnp.bfloat16),
        "w_gate": normal_values(key_list[7], (D, FF), D ** -0.5, 0.125, ((1, 4),)),
        "w_up": normal_values(key_list[8], (D, FF), D ** -0.5, 0.125, ((1, 4),)),
        "w_down": normal_values(key_list[9], (FF, D), FF ** -0.5, 0.0625, ((0, 4),)),
        "cotangent": bell_draw_with(key_list[10], (TOKENS, D), 1.0, 6.0, ((0, 32),), (0, 1, 32, 2.75)),
        "first_len": with_ends(jax.random.randint(key_list[11], (ROWS,), ROW // 2, ROW + 1), jax.random.fold_in(key_list[11], 1), ROW // 2, ROW).astype(jnp.int32),
        "live_rows": draw_live_rows(jax.random.fold_in(key_list[13], 71), 0),
    }


THETA = 500000.0
EPS = 1e-05
NEGATIVE = -1e+30

@jax.custom_vjp
def low(v):
    return lax.optimization_barrier(v.astype(jnp.bfloat16)).astype(jnp.float32)

@jax.custom_vjp
def low_back(v):
    return v

def low_keep(v):
    return (low(v), None)

def low_pass(kept, grad):
    return (grad,)

def back_keep(v):
    return (v, None)

def back_low(kept, grad):
    return (low(grad),)
low.defvjp(low_keep, low_pass)
low_back.defvjp(back_keep, back_low)

def matmul(left, right):
    return jnp.dot(left, right, precision=lax.Precision.HIGHEST)

def rms_scale(values, gain):
    return values * lax.rsqrt(lax.optimization_barrier(jnp.mean(values * values, axis=-1, keepdims=True)) + EPS) * gain

def angles(position, head_dim):
    half_dim = head_dim // 2
    freq_tab = jnp.exp(jnp.arange(half_dim, dtype=jnp.float32) * (-2.0 * math.log(THETA) / head_dim))
    turned = position.astype(jnp.float32)[:, None] * freq_tab[None, :]
    return (jnp.cos(turned), jnp.sin(turned))

def rotate(vectors, cosine, sine_tab):
    half_dim = vectors.shape[-1] // 2
    first_half = vectors[..., :half_dim]
    second_half = vectors[..., half_dim:]
    cos_part = cosine[:, None, :]
    sin_part = sine_tab[:, None, :]
    return jnp.concatenate([first_half * cos_part - second_half * sin_part, second_half * cos_part + first_half * sin_part], axis=-1)

def reference(tokens, norm1_gain, w_query, w_key, w_value, w_output, norm2_gain, w_gate, w_up, w_down, cotangent, first_len, live_rows):
    index = jnp.arange(TOKENS, dtype=jnp.int32)
    global_row = index // ROW
    place = index - global_row * ROW
    first = first_len[global_row]
    second = (place >= first).astype(jnp.int32)
    segment = global_row * 2 + second
    position = place - second * first
    owner = global_row // ROWS_DEV
    live_mask = (global_row - owner * ROWS_DEV < live_rows[owner]).astype(jnp.float32)
    cosine, sine_tab = angles(position, HEAD_DIM)
    group_size = HEADS // KV_HEADS
    scale_factor = HEAD_DIM ** (-0.5)
    seg_rows = segment.reshape(ROWS, ROW)
    order = jnp.arange(ROW, dtype=jnp.int32)
    causal = order[None, :] <= order[:, None]

    @jax.checkpoint
    def attend_row(pieces):
        query_row, key_row, value_row, seg_row = pieces
        grouped = query_row.reshape(ROW, KV_HEADS, group_size, HEAD_DIM)
        raw = jnp.einsum('qkgd,tkd->kgqt', grouped, key_row, precision=lax.Precision.HIGHEST) * scale_factor
        raw = low_back(raw)
        allowed = (seg_row[:, None] == seg_row[None, :]) & causal
        masked = jnp.where(allowed[None, None], raw, NEGATIVE)
        top = lax.optimization_barrier(jnp.max(masked, axis=-1, keepdims=True))
        exp_terms = jnp.exp(masked - top)
        attn_prob = low(exp_terms / lax.optimization_barrier(jnp.sum(exp_terms, axis=-1, keepdims=True)))
        mixed = jnp.einsum('kgqt,tkd->qkgd', attn_prob, value_row, precision=lax.Precision.HIGHEST)
        return mixed.reshape(ROW, HEADS * HEAD_DIM)

    def forward(resid_in, gain_one, query_mat, key_mat, value_mat, output_mat, gain_two, gate_mat, up_mat, down_mat):
        normed_one = low(rms_scale(resid_in, gain_one))
        query_lin = low_back(matmul(normed_one, query_mat))
        key_lin = low_back(matmul(normed_one, key_mat))
        value_rows = low(low_back(matmul(normed_one, value_mat)))
        queries = low(rotate(query_lin.reshape(TOKENS, HEADS, HEAD_DIM), cosine, sine_tab))
        key_rows = low(rotate(key_lin.reshape(TOKENS, KV_HEADS, HEAD_DIM), cosine, sine_tab))
        attended = lax.map(attend_row, (queries.reshape(ROWS, ROW, HEADS, HEAD_DIM), key_rows.reshape(ROWS, ROW, KV_HEADS, HEAD_DIM), value_rows.reshape(ROWS, ROW, KV_HEADS, HEAD_DIM), seg_rows))
        attended = low(low_back(attended.reshape(TOKENS, HEADS * HEAD_DIM)))
        middle = resid_in + low_back(matmul(attended, output_mat))
        normed_two = low(rms_scale(middle, gain_two))
        gate_act = low_back(matmul(normed_two, gate_mat))
        up_act = low_back(matmul(normed_two, up_mat))
        hidden = low(gate_act * jax.nn.sigmoid(gate_act) * up_act)
        return live_mask[:, None] * (middle + low_back(matmul(hidden, down_mat)))
    result, pullback = jax.vjp(forward, tokens.astype(jnp.float32), norm1_gain.astype(jnp.float32), w_query.astype(jnp.float32), w_key.astype(jnp.float32), w_value.astype(jnp.float32), w_output.astype(jnp.float32), norm2_gain.astype(jnp.float32), w_gate.astype(jnp.float32), w_up.astype(jnp.float32), w_down.astype(jnp.float32))
    grads = pullback(cotangent.astype(jnp.float32))
    return (result.astype(jnp.bfloat16), grads[0], grads[1], grads[2], grads[3], grads[4], grads[5], grads[6], grads[7], grads[8], grads[9])
```

```python
import math

import jax
import jax.numpy as jnp
from jax import lax
from jax.experimental import pallas as pl
from jax.experimental.pallas import tpu as pltpu
from jax.sharding import PartitionSpec as P

HEAD_DIM = 64
THETA = 500000.0
EPS = 1e-05
NEGATIVE = -1e30
F32 = jnp.float32
BF16 = jnp.bfloat16
VMEM_BYTES = 56 * 1024 * 1024
AXES = ("dp", "tensor")


def pair_low(i):
    return i ^ 1


def pair_high(i):
    return 3 - i


def low_bit(v):
    return (v ^ (v >> 1)) & 1


def high_bit(v):
    return v >> 1


def from_bits(low, high):
    return jnp.where(high == 0, low, 3 - low)


def device_perm(move):
    pairs = []
    for dp in range(32):
        for y in range(4):
            z2, x2, c2, y2 = move(dp // 8, (dp // 2) % 4, dp % 2, y)
            pairs.append((dp * 4 + y, ((z2 * 4 + x2) * 2 + c2) * 4 + y2))
    return pairs


def first_pair(c, i):
    return pair_low(i) if c == 0 else pair_high(i)


def second_pair(c, i):
    return pair_high(i) if c == 0 else pair_low(i)


ALONG_Y = (
    device_perm(lambda z, x, c, y: (z, x, c, first_pair(c, y))),
    device_perm(lambda z, x, c, y: (z, x, c, second_pair(c, y))),
)
ALONG_X = (
    device_perm(lambda z, x, c, y: (z, first_pair(c, x), c, y)),
    device_perm(lambda z, x, c, y: (z, second_pair(c, x), c, y)),
)
ALONG_Z = (
    device_perm(lambda z, x, c, y: (first_pair(c, z), x, c, y)),
    device_perm(lambda z, x, c, y: (second_pair(c, z), x, c, y)),
)
OTHER_CORE = device_perm(lambda z, x, c, y: (z, x, 1 - c, y))
STREAMS = (ALONG_X + ALONG_Z, ALONG_Z + ALONG_X)


def swap(array, perm):
    return lax.ppermute(array, AXES, perm)


def block_order(stream, z, x, c):
    place = jnp.arange(16, dtype=jnp.int32)
    keep = [(place >> (3 - k)) & 1 for k in range(4)]

    def target(v, first, second):
        low = low_bit(v) ^ (1 - jnp.where(c == 0, first, second))
        high = high_bit(v) ^ (1 - jnp.where(c == 0, second, first))
        return from_bits(low, high)

    if stream == 0:
        return target(z, keep[2], keep[3]) * 4 + target(x, keep[0], keep[1])
    return target(z, keep[0], keep[1]) * 4 + target(x, keep[2], keep[3])


def angles(position, head_dim):
    half_dim = head_dim // 2
    freq_tab = jnp.exp(
        jnp.arange(half_dim, dtype=F32) * (-2.0 * math.log(THETA) / head_dim)
    )
    turned = position.astype(F32)[:, None] * freq_tab[None, :]
    return (jnp.cos(turned), jnp.sin(turned))


def rotate(vectors, cosine, sine_tab):
    half_dim = vectors.shape[-1] // 2
    first_half = vectors[..., :half_dim]
    second_half = vectors[..., half_dim:]
    cos_part = cosine[:, None, :]
    sin_part = sine_tab[:, None, :]
    return jnp.concatenate(
        [
            first_half * cos_part - second_half * sin_part,
            second_half * cos_part + first_half * sin_part,
        ],
        axis=-1,
    )


def times_transpose(left, right):
    return lax.dot_general(left, right, (((1,), (1,)), ((), ())), preferred_element_type=F32)


def mlp_kernel(n_ref, dy_ref, wg_ref, wu_ref, wd_ref, out_ref, grad_ref, act_ref):
    step = pl.program_id(0)
    n = n_ref[...]
    w_gate = wg_ref[...]
    w_up = wu_ref[...]
    w_down = wd_ref[...]
    gate = jnp.dot(n, w_gate, preferred_element_type=F32)
    up = jnp.dot(n, w_up, preferred_element_type=F32)
    grad_hidden = times_transpose(dy_ref[...], w_down)
    sig = 1.0 / (1.0 + jnp.exp(-gate))
    silu = gate * sig
    hidden = (silu * up).astype(BF16)
    d_gate = (grad_hidden * up * sig * (1.0 + gate * (1.0 - sig))).astype(BF16)
    d_up = (grad_hidden * silu).astype(BF16)
    act_ref[0] = hidden.astype(F32)
    act_ref[1] = d_gate.astype(F32)
    act_ref[2] = d_up.astype(F32)
    out_part = jnp.dot(hidden, w_down, preferred_element_type=F32)
    grad_part = times_transpose(d_gate, w_gate) + times_transpose(d_up, w_up)

    @pl.when(step == 0)
    def _():
        out_ref[...] = out_part
        grad_ref[...] = grad_part

    @pl.when(step > 0)
    def _():
        out_ref[...] += out_part
        grad_ref[...] += grad_part


def mlp(normed, dy, w_gate, w_up, w_down):
    tok, wide = normed.shape
    units = w_gate.shape[1]
    tile = 512
    return pl.pallas_call(
        mlp_kernel,
        grid=(units // tile,),
        in_specs=[
            pl.BlockSpec((tok, wide), lambda t: (0, 0)),
            pl.BlockSpec((tok, wide), lambda t: (0, 0)),
            pl.BlockSpec((wide, tile), lambda t: (0, t)),
            pl.BlockSpec((wide, tile), lambda t: (0, t)),
            pl.BlockSpec((tile, wide), lambda t: (t, 0)),
        ],
        out_specs=[
            pl.BlockSpec((tok, wide), lambda t: (0, 0)),
            pl.BlockSpec((tok, wide), lambda t: (0, 0)),
            pl.BlockSpec((3, tok, tile), lambda t: (0, 0, t)),
        ],
        out_shape=[
            jax.ShapeDtypeStruct((tok, wide), F32),
            jax.ShapeDtypeStruct((tok, wide), F32),
            jax.ShapeDtypeStruct((3, tok, units), F32),
        ],
        compiler_params=pltpu.CompilerParams(vmem_limit_bytes=VMEM_BYTES),
        cost_estimate=pl.CostEstimate(
            flops=12 * tok * wide * units,
            bytes_accessed=3 * wide * units * 2 + 5 * tok * wide * 4,
            transcendentals=tok * units,
        ),
        name="mlp",
    )(normed, dy, w_gate, w_up, w_down)


def weight_kernel(parts, order_ref, own_ref, other_ref, *refs):
    rhs_refs, (send_ref, keep_ref, lhs) = refs[:parts], refs[parts:]
    core = order_ref[16]
    tok = own_ref.shape[-1]

    @pl.when(pl.program_id(0) == 0)
    def _():
        for place in range(16):
            chip = order_ref[place]
            lhs[pl.ds(place * 64, 64), :tok] = own_ref[chip, core]
            lhs[pl.ds(place * 64, 64), tok:] = other_ref[chip].astype(BF16)

    rhs = jnp.concatenate([ref[...].reshape(ref.shape[-2:]).astype(BF16) for ref in rhs_refs], axis=0)
    half = send_ref.shape[0]
    send_ref[...] = jnp.dot(lhs[:half], rhs, preferred_element_type=F32)
    keep_ref[...] = jnp.dot(lhs[half:], rhs, preferred_element_type=F32)


def weight_grad(order, own, other, rhs, pick, start, columns):
    tile = min(512, columns)
    while columns % tile:
        tile -= 128
    offset = start // tile
    tok = own.shape[-1]
    rhs_specs = [
        pl.BlockSpec((1, r.shape[1], tile), lambda j, o, w=w: (w, 0, j + offset)) for r, w in zip(rhs, pick)
    ]
    return pl.pallas_call(
        lambda *refs: weight_kernel(len(rhs), *refs),
        grid_spec=pltpu.PrefetchScalarGridSpec(
            num_scalar_prefetch=1,
            grid=(columns // tile,),
            in_specs=[
                pl.BlockSpec(own.shape, lambda j, o: (0, 0, 0, 0)),
                pl.BlockSpec(other.shape, lambda j, o: (0, 0, 0)),
            ]
            + rhs_specs,
            out_specs=[
                pl.BlockSpec((512, tile), lambda j, o: (0, j)),
                pl.BlockSpec((512, tile), lambda j, o: (0, j)),
            ],
            scratch_shapes=[pltpu.VMEM((1024, 2 * tok), BF16)],
        ),
        out_shape=[jax.ShapeDtypeStruct((512, columns), F32)] * 2,
        compiler_params=pltpu.CompilerParams(vmem_limit_bytes=VMEM_BYTES),
        cost_estimate=pl.CostEstimate(
            flops=2 * 1024 * 2 * tok * columns,
            bytes_accessed=1024 * columns * 4 + 4 * tok * columns * 4 + 1024 * tok * 8,
            transcendentals=0,
        ),
        name="weight_grad",
    )(order, own, other, *rhs)


def scatter_sum(stream, send, keep):
    for perm in STREAMS[stream]:
        got = swap(send, perm)
        rows = keep.shape[0] // 2
        if perm is STREAMS[stream][3]:
            return keep + got
        send, keep = keep[:rows] + got[:rows], keep[rows:] + got[rows:]


def attend(normed, place, first, w_query, w_key, w_value, w_output):
    tok = normed.shape[0]
    heads = w_query.shape[1] // HEAD_DIM
    kv = w_key.shape[1] // HEAD_DIM
    group = heads // kv
    second = (place >= first).astype(jnp.int32)
    cosine, sine = angles(place - second * first, HEAD_DIM)
    allowed = (second[:, None] == second[None, :]) & (place[None, :] <= place[:, None])
    query_lin = jnp.dot(normed, w_query, preferred_element_type=F32)
    key_lin = jnp.dot(normed, w_key, preferred_element_type=F32)
    values = jnp.dot(normed, w_value, preferred_element_type=F32).astype(BF16).reshape(tok, kv, HEAD_DIM)
    queries = rotate(query_lin.reshape(tok, heads, HEAD_DIM), cosine, sine).astype(BF16)
    keys = rotate(key_lin.reshape(tok, kv, HEAD_DIM), cosine, sine).astype(BF16)
    grouped = queries.reshape(tok, kv, group, HEAD_DIM)
    raw = jnp.einsum("qkgd,tkd->kgqt", grouped, keys, preferred_element_type=F32) * HEAD_DIM**-0.5
    scores = jnp.where(allowed[None, None], raw, NEGATIVE)
    top = jnp.max(scores, axis=-1, keepdims=True)
    terms = jnp.exp(scores - top)
    prob = terms / jnp.sum(terms, axis=-1, keepdims=True)
    attended = jnp.einsum("kgqt,tkd->qkgd", prob.astype(BF16), values, preferred_element_type=F32)
    attended = attended.reshape(tok, heads * HEAD_DIM).astype(BF16)
    part = jnp.dot(attended, w_output, preferred_element_type=F32)
    return part, attended, (prob, grouped, keys, values, cosine, sine)


def attend_back(dm, kept, w_query, w_key, w_value, w_output):
    prob, grouped, keys, values, cosine, sine = kept
    tok, kv, group, _ = grouped.shape
    grad_att = times_transpose(dm, w_output).astype(BF16).reshape(grouped.shape)
    grad_values = jnp.einsum("kgqt,qkgd->tkd", prob.astype(BF16), grad_att, preferred_element_type=F32).astype(BF16)
    grad_prob = jnp.einsum("qkgd,tkd->kgqt", grad_att, values, preferred_element_type=F32)
    delta = jnp.sum(prob * grad_prob, axis=-1, keepdims=True)
    grad_score = (prob * (grad_prob - delta)).astype(BF16)
    scale = HEAD_DIM**-0.5
    grad_queries = jnp.einsum("kgqt,tkd->qkgd", grad_score, keys, preferred_element_type=F32) * scale
    grad_keys = jnp.einsum("kgqt,qkgd->tkd", grad_score, grouped, preferred_element_type=F32) * scale
    grad_q = rotate(grad_queries.reshape(tok, kv * group, HEAD_DIM), cosine, -sine).reshape(tok, -1).astype(BF16)
    grad_k = rotate(grad_keys, cosine, -sine).reshape(tok, -1).astype(BF16)
    grad_v = grad_values.reshape(tok, -1)
    part = (
        times_transpose(grad_q, w_query) + times_transpose(grad_k, w_key) + times_transpose(grad_v, w_value)
    )
    return part, jnp.concatenate([grad_q, grad_k, grad_v], axis=1)


def sum_over_tensor(sent, kept):
    got = swap(sent, ALONG_Y[0])
    rows = kept.shape[0] // 2
    more = swap(kept[rows:] + got[rows:], ALONG_Y[1])
    return kept[:rows] + got[:rows] + more


def spread_over_tensor(quarter):
    kept = jnp.concatenate([quarter, swap(quarter, ALONG_Y[1])], axis=0)
    return kept, swap(kept, ALONG_Y[0])


def unit_of(rows):
    inverse = lax.rsqrt(jnp.mean(rows * rows, axis=-1, keepdims=True) + EPS)
    return rows * inverse, inverse


def norm_back(grad, unit, inverse, gain):
    scaled = grad * gain
    return inverse * (scaled - unit * jnp.mean(scaled * unit, axis=-1, keepdims=True))


def on_device(
    tokens,
    norm1_gain,
    w_query,
    w_key,
    w_value,
    w_output,
    norm2_gain,
    w_gate,
    w_up,
    w_down,
    cotangent,
    first_len,
    live_rows,
):
    dp = lax.axis_index("dp")
    y = lax.axis_index("tensor")
    z, x, c = dp // 8, (dp // 2) % 4, dp % 2
    slot = jnp.where(c == 0, low_bit(y), high_bit(y))
    part = jnp.where(c == 0, high_bit(y), low_bit(y))
    orders = [block_order(s, z, x, c) for s in range(2)]
    orders_core = [jnp.concatenate([o, jnp.reshape(c, (1,))]).astype(jnp.int32) for o in orders]
    tok, wide = tokens.shape
    row = tok // 2
    quarter = row // 2
    gain_one = norm1_gain.astype(F32)
    gain_two = norm2_gain.astype(F32)

    def ordered(array, which):
        base = which * row
        return jnp.concatenate(
            [
                lax.dynamic_slice_in_dim(array, base + part * quarter, quarter, 0),
                lax.dynamic_slice_in_dim(array, base + (1 - part) * quarter, quarter, 0),
            ],
            axis=0,
        )

    steps = jnp.arange(quarter, dtype=jnp.int32)
    place = jnp.concatenate([steps + part * quarter, steps + (1 - part) * quarter])
    slots = (slot, 1 - slot)
    first = [lax.dynamic_index_in_dim(first_len, s, keepdims=False) for s in slots]
    live = [(s < live_rows[0]).astype(F32) for s in slots]
    x_in = [ordered(tokens, s).astype(F32) for s in slots]
    dy = [(ordered(cotangent, s).astype(F32) * l).astype(BF16) for s, l in zip(slots, live)]

    def by_block(rows):
        return jnp.transpose(rows).reshape(16, 2, 64, rows.shape[0])

    def for_other(blocks):
        return lax.dynamic_index_in_dim(blocks, 1 - c, axis=1, keepdims=False).astype(F32)

    unit_one, inv_one, normed_one = [], [], []
    for rows in x_in:
        unit, inverse = unit_of(rows)
        unit_one.append(unit)
        inv_one.append(inverse)
        normed_one.append((unit * gain_one).astype(BF16))

    weights = (w_query, w_key, w_value, w_output)
    part_n, attended_n, kept_n = attend(normed_one[1], place, first[1], *weights)
    part_k, attended_k, kept_k = attend(normed_one[0], place, first[0], *weights)
    own_sum = sum_over_tensor(part_n, part_k)

    dy_blocks = by_block(jnp.concatenate(dy, axis=0))
    one_blocks = by_block(jnp.concatenate(normed_one, axis=0))
    dy_other = swap(for_other(dy_blocks), OTHER_CORE)
    one_other = swap(for_other(one_blocks), OTHER_CORE)
    attended = jnp.concatenate([attended_k, attended_n], axis=0)
    attended_other = swap(attended.astype(F32), OTHER_CORE)

    middle_k, middle_n = spread_over_tensor(x_in[0][:quarter] + own_sum)
    unit_k, inv_k = unit_of(middle_k)
    two_k = (unit_k * gain_two).astype(BF16)
    out_k, grad_k, act_k = mlp(two_k, dy[0], w_gate, w_up, w_down)
    unit_n, inv_n = unit_of(middle_n)
    two_n = (unit_n * gain_two).astype(BF16)
    out_n, grad_n, act_n = mlp(two_n, dy[1], w_gate, w_up, w_down)
    act_k_other = swap(act_k, OTHER_CORE)
    two_blocks = by_block(jnp.concatenate([two_k, two_n], axis=0))
    two_other = swap(for_other(two_blocks), OTHER_CORE)
    act_n_other = swap(act_n, OTHER_CORE)

    grad_two_q = sum_over_tensor(grad_k, grad_n)
    gain_two_part = jnp.sum(grad_two_q * unit_n[:quarter], axis=0)
    grad_two_n, grad_two_k = spread_over_tensor(grad_two_q)

    acts = (act_k, act_n, act_k_other, act_n_other)
    down = [
        scatter_sum(s, *weight_grad(orders_core[s], dy_blocks, dy_other, acts, (0,) * 4, s * 1024, 1024))
        for s in range(2)
    ]
    gate = scatter_sum(0, *weight_grad(orders_core[0], two_blocks, two_other, acts, (1,) * 4, 0, 2048))
    up = scatter_sum(1, *weight_grad(orders_core[1], two_blocks, two_other, acts, (2,) * 4, 0, 2048))

    grad_middle_n = dy[1].astype(F32) + norm_back(grad_two_n, unit_n, inv_n, gain_two)
    grad_middle_k = dy[0].astype(F32) + norm_back(grad_two_k, unit_k, inv_k, gain_two)
    dm_n = grad_middle_n.astype(BF16)
    dm_k = grad_middle_k.astype(BF16)
    back_n, lin_n = attend_back(dm_n, kept_n, *weights)
    back_k, lin_k = attend_back(dm_k, kept_k, *weights)
    grad_one_q = sum_over_tensor(back_n, back_k)
    gain_one_part = jnp.sum(grad_one_q * unit_one[0][:quarter], axis=0)
    grad_one_k, grad_one_n = spread_over_tensor(grad_one_q)

    dm_blocks = by_block(jnp.concatenate([dm_k, dm_n], axis=0))
    dm_other = swap(for_other(dm_blocks), OTHER_CORE)
    lin = jnp.concatenate([lin_k, lin_n], axis=0)
    lin_other = swap(lin.astype(F32), OTHER_CORE)
    output = scatter_sum(
        1,
        *weight_grad(orders_core[1], dm_blocks, dm_other, (attended[None], attended_other[None]), (0, 0), 0, 512),
    )
    query_key_value = scatter_sum(
        0, *weight_grad(orders_core[0], one_blocks, one_other, (lin[None], lin_other[None]), (0, 0), 0, 768)
    )

    out_q = sum_over_tensor(out_n, out_k)
    sum_k, sum_n = spread_over_tensor(out_q)

    def in_place(first_slot, second_slot):
        whole = jnp.stack([first_slot, second_slot]).reshape(2, 2, quarter, wide)
        whole = jnp.where(part == 0, whole, whole[:, ::-1])
        whole = jnp.where(slot == 0, whole, whole[::-1])
        return whole.reshape(tok, wide)

    layer_out = in_place(
        (live[0] * (middle_k + sum_k)).astype(BF16), (live[1] * (middle_n + sum_n)).astype(BF16)
    )
    grad_tokens = in_place(
        grad_middle_k + norm_back(grad_one_k, unit_one[0], inv_one[0], gain_one),
        grad_middle_n + norm_back(grad_one_n, unit_one[1], inv_one[1], gain_one),
    )

    gains = jnp.stack([gain_one_part, gain_two_part]).reshape(2, 16, 2, 64)
    gains = jnp.transpose(gains, (2, 1, 0, 3)).reshape(2, 16, 128)
    mine = lax.dynamic_index_in_dim(gains, c, keepdims=False)
    theirs = lax.dynamic_index_in_dim(gains, 1 - c, keepdims=False)
    mine = mine + swap(theirs, OTHER_CORE)
    picks = orders[0][:, None] == jnp.arange(16, dtype=jnp.int32)[None, :]
    mine = jnp.sum(jnp.where(picks[:, :, None], mine[None], 0.0), axis=1)
    mine = scatter_sum(0, mine[:8], mine[8:])
    mine = mine + swap(mine, ALONG_Y[0])
    mine = mine + swap(mine, ALONG_Y[1])

    down = jnp.transpose(jnp.concatenate(down, axis=1))
    return (
        layer_out,
        grad_tokens,
        mine[0, :64],
        query_key_value[:, :512],
        query_key_value[:, 512:640],
        query_key_value[:, 640:],
        jnp.transpose(output),
        mine[0, 64:],
        gate,
        up,
        down,
    )


def solution(mesh):
    placed = (
        P("dp", None),
        P(),
        P(None, "tensor"),
        P(None, "tensor"),
        P(None, "tensor"),
        P("tensor", None),
        P(),
        P(None, "tensor"),
        P(None, "tensor"),
        P("tensor", None),
        P("dp", None),
        P("dp"),
        P("dp"),
    )
    return jax.shard_map(
        on_device,
        mesh=mesh,
        in_specs=placed,
        out_specs=(
            P("dp", None),
            P("dp", None),
            P("dp"),
            P("dp", "tensor"),
            P("dp", "tensor"),
            P("dp", "tensor"),
            P("tensor", "dp"),
            P("dp"),
            P("dp", "tensor"),
            P("dp", "tensor"),
            P("tensor", "dp"),
        ),
        check_vma=False,
    )
```

```python
import functools
import math

import jax
import jax.numpy as jnp
import numpy as np
from jax import lax
from jax.experimental import pallas as pl
from jax.experimental.pallas import tpu as pltpu
from jax.sharding import PartitionSpec as P

HEAD_DIM = 64
T1 = True
U2 = True
U3 = False
U4 = True
T7 = True
T8 = False
W1 = True
W2 = True
W4 = False
W5 = False
W6 = True
W7 = False
S_attend = 2.5
S_attend_back = 2.5
S_mlp = 2.5
S_mlp_weight_grad = 2.5
S_weight_grad = 8.0
S_by_block = 0.3
S_grad_tokens = 2.5
S_layer_out = 1.0
THETA = 500000.0
EPS = 1e-05
NEGATIVE = -1e30
F32 = jnp.float32
BF16 = jnp.bfloat16
ATTEND_VMEM = 58 * 1024 * 1024
MLP_VMEM = 58 * 1024 * 1024
WEIGHT_VMEM = 58 * 1024 * 1024
SMALL_VMEM = 58 * 1024 * 1024
AXES = ("dp", "tensor")


def pair_low(i):
    return i ^ 1


def pair_high(i):
    return 3 - i


def low_bit(v):
    return (v ^ (v >> 1)) & 1


def high_bit(v):
    return v >> 1


def from_bits(low, high):
    return jnp.where(high == 0, low, 3 - low)


def device_perm(move):
    pairs = []
    for dp in range(32):
        for y in range(4):
            z2, x2, c2, y2 = move(dp // 8, (dp // 2) % 4, dp % 2, y)
            pairs.append((dp * 4 + y, ((z2 * 4 + x2) * 2 + c2) * 4 + y2))
    return pairs


def first_pair(c, i):
    return pair_low(i) if c == 0 else pair_high(i)


def second_pair(c, i):
    return pair_high(i) if c == 0 else pair_low(i)


ALONG_Y = (
    device_perm(lambda z, x, c, y: (z, x, c, first_pair(c, y))),
    device_perm(lambda z, x, c, y: (z, x, c, second_pair(c, y))),
)
ALONG_X = (
    device_perm(lambda z, x, c, y: (z, first_pair(c, x), c, y)),
    device_perm(lambda z, x, c, y: (z, second_pair(c, x), c, y)),
)
ALONG_Z = (
    device_perm(lambda z, x, c, y: (first_pair(c, z), x, c, y)),
    device_perm(lambda z, x, c, y: (second_pair(c, z), x, c, y)),
)
OTHER_CORE = device_perm(lambda z, x, c, y: (z, x, 1 - c, y))
RING_X = [device_perm(lambda z, x, c, y, k=k: (z, (x + k) % 4, c, y)) for k in (1, 2, 3)]
RING_Z = [device_perm(lambda z, x, c, y, k=k: ((z + k) % 4, x, c, y)) for k in (1, 2, 3)]
STREAMS = (ALONG_X + ALONG_Z, ALONG_Z + ALONG_X)


def swap(array, perm):
    return lax.ppermute(array, AXES, perm)


def block_order(stream, z, x, c):
    place = jnp.arange(16, dtype=jnp.int32)
    keep = [(place >> (3 - k)) & 1 for k in range(4)]

    def target(v, first, second):
        low = low_bit(v) ^ (1 - jnp.where(c == 0, first, second))
        high = high_bit(v) ^ (1 - jnp.where(c == 0, second, first))
        return from_bits(low, high)

    if stream == 0:
        return target(z, keep[2], keep[3]) * 4 + target(x, keep[0], keep[1])
    return target(z, keep[0], keep[1]) * 4 + target(x, keep[2], keep[3])


def turn_tables(tok):
    half = HEAD_DIM // 2
    freq = np.exp(np.arange(half) * (-2.0 * math.log(THETA) / HEAD_DIM))
    turned = np.arange(tok)[:, None] * freq[None, :]
    cosine, sine = np.cos(turned), np.sin(turned)
    return (
        jnp.asarray(np.tile(cosine, (1, 4)), F32),
        jnp.asarray(np.concatenate([-sine, sine, -sine, sine], axis=1), F32),
    )


def cost(scale, flops, moved, transcendentals=0):
    return pl.CostEstimate(flops=int(flops * scale), bytes_accessed=int(moved * scale), transcendentals=int(transcendentals * scale))


def times_transpose(left, right):
    return lax.dot_general(left, right, (((1,), (1,)), ((), ())), preferred_element_type=F32)


def contract_rows(left, right):
    return lax.dot_general(left, right, (((0,), (0,)), ((), ())), preferred_element_type=F32)


def turn(vectors, cosine, sine):
    lane = lax.broadcasted_iota(jnp.int32, vectors.shape, 1)
    ahead = pltpu.roll(vectors, 96, 1)
    behind = pltpu.roll(vectors, 32, 1)
    return vectors * cosine + jnp.where(lane % 64 < 32, ahead, behind) * sine


def row_turns(first, cos_ref, sin_ref):
    place = lax.broadcasted_iota(jnp.int32, cos_ref.shape, 0)
    return [jnp.where(place >= first, pltpu.roll(ref[...], first, 0), ref[...]) for ref in (cos_ref, sin_ref)]


def allowed_pairs(first, tok, group):
    query = lax.broadcasted_iota(jnp.int32, (group * tok, tok), 0) % tok
    key = lax.broadcasted_iota(jnp.int32, (group * tok, tok), 1)
    same = jnp.logical_not(jnp.logical_xor(query >= first, key >= first))
    return jnp.logical_and(same, key <= query)


def softmax_rows(queries, keys, allowed):
    raw = times_transpose(queries, keys) * HEAD_DIM**-0.5
    scores = jnp.where(allowed, raw, NEGATIVE)
    terms = jnp.exp(scores - jnp.max(scores, axis=-1, keepdims=True))
    return terms / jnp.sum(terms, axis=-1, keepdims=True)


def head_rows(array, head, count):
    return jnp.concatenate(
        [array[:, (head + k) * HEAD_DIM : (head + k + 1) * HEAD_DIM] for k in range(count)], axis=0
    )


def attend_kernel(
    slot_ref, first_ref, x_ref, gain_ref, cos_ref, sin_ref, wq_hbm, wk_hbm, wv_hbm, wo_hbm, *refs
):
    part_ref, normed_ref, attended_ref, kept_ref, wq, wk, wv, wo, sems = refs[-9:]
    copies = [
        pltpu.make_async_copy(src, dst, sems.at[k])
        for k, (src, dst) in enumerate(((wq_hbm, wq), (wk_hbm, wk), (wv_hbm, wv), (wo_hbm, wo)))
    ]
    for copy in copies:
        copy.start()
    x = x_ref[...].astype(F32)
    inverse = lax.rsqrt(jnp.mean(x * x, axis=-1, keepdims=True) + EPS)
    normed = (x * inverse * gain_ref[...].astype(F32)).astype(BF16)
    normed_ref[...] = normed
    first = first_ref[slot_ref[0]]
    cosine, sine = row_turns(first, cos_ref, sin_ref)
    tok = x.shape[0]
    heads = wq.shape[1] // HEAD_DIM
    kv = wk.shape[1] // HEAD_DIM
    group = heads // kv
    copies[0].wait()
    lin = jnp.dot(normed, wq[...], preferred_element_type=F32)
    queries = jnp.concatenate(
        [turn(lin[:, k * 128 : (k + 1) * 128], cosine, sine).astype(BF16) for k in range(heads // 2)], axis=1
    )
    copies[1].wait()
    lin = jnp.dot(normed, wk[...], preferred_element_type=F32)
    keys = jnp.concatenate(
        [turn(lin[:, k * 128 : (k + 1) * 128], cosine, sine).astype(BF16) for k in range(kv // 2)], axis=1
    )
    copies[2].wait()
    values = jnp.dot(normed, wv[...], preferred_element_type=F32).astype(BF16)
    kept_ref[:, : heads * HEAD_DIM] = queries
    kept_ref[:, heads * HEAD_DIM : (heads + kv) * HEAD_DIM] = keys
    kept_ref[:, (heads + kv) * HEAD_DIM :] = values
    allowed = allowed_pairs(first, tok, group)
    mixed = []
    for k in range(kv):
        lanes = slice(k * HEAD_DIM, (k + 1) * HEAD_DIM)
        prob = softmax_rows(head_rows(queries, k * group, group), keys[:, lanes], allowed).astype(BF16)
        out = jnp.dot(prob, values[:, lanes], preferred_element_type=F32)
        mixed += [out[g * tok : (g + 1) * tok] for g in range(group)]
    attended = jnp.concatenate(mixed, axis=1).astype(BF16)
    attended_ref[0] = attended.astype(F32)
    copies[3].wait()
    part_ref[...] = jnp.dot(attended, wo[...], preferred_element_type=F32)


def attend(entry, slot, first_len, tokens, gain, tables, attended, w_query, w_key, w_value, w_output):
    tok, wide = tokens.shape[0] // 2, tokens.shape[1]
    cols = w_query.shape[1]
    kv_cols = w_key.shape[1]
    weights = (w_query, w_key, w_value, w_output)
    aliased = () if attended is None else (attended,)

    def whole(array):
        return pl.BlockSpec(array.shape, lambda j, s: (0,) * array.ndim)

    return pl.pallas_call(
        attend_kernel,
        grid_spec=pltpu.PrefetchScalarGridSpec(
            num_scalar_prefetch=1,
            grid=(1,),
            in_specs=[
                pl.BlockSpec(memory_space=pltpu.SMEM),
                pl.BlockSpec((tok, wide), lambda j, s: (s[0], 0)),
                whole(gain),
                whole(tables[0]),
                whole(tables[1]),
            ]
            + [pl.BlockSpec(memory_space=pl.ANY)] * (4 + len(aliased)),
            out_specs=[
                pl.BlockSpec((tok, wide), lambda j, s: (0, 0)),
                pl.BlockSpec((tok, wide), lambda j, s: (0, 0)),
                pl.BlockSpec((1, tok, cols), lambda j, s: (entry, 0, 0)),
                pl.BlockSpec((tok, cols + 2 * kv_cols), lambda j, s: (0, 0)),
            ],
            scratch_shapes=[pltpu.VMEM(w.shape, w.dtype) for w in weights] + [pltpu.SemaphoreType.DMA((4,))],
        ),
        out_shape=[
            jax.ShapeDtypeStruct((tok, wide), F32),
            jax.ShapeDtypeStruct((tok, wide), BF16),
            jax.ShapeDtypeStruct((2, tok, cols), F32),
            jax.ShapeDtypeStruct((tok, cols + 2 * kv_cols), BF16),
        ],
        input_output_aliases={10: 2} if aliased else {},
        compiler_params=pltpu.CompilerParams(vmem_limit_bytes=ATTEND_VMEM),
        cost_estimate=cost(S_attend,
            2 * tok * wide * (2 * cols + 2 * kv_cols) + 4 * tok * tok * cols,
            sum(w.size * 2 for w in weights) + tok * wide * 8,
            tok * tok * cols // HEAD_DIM,
        ),
        name="attend",
    )(slot, first_len, tokens, gain, *tables, *weights, *aliased)


def attend_back_kernel(
    slot_ref, first_ref, live_ref, grad_ref, more_ref, middle_ref, cot_ref, gain_ref, kept_ref, cos_ref, sin_ref,
    wq_hbm, wk_hbm, wv_hbm, wo_hbm, *refs
):
    part_ref, grad_mid_ref, dm_ref, lin_ref, gain_out_ref, wq, wk, wv, wo, sems = refs[-10:]
    copies = [
        pltpu.make_async_copy(src, dst, sems.at[k])
        for k, (src, dst) in enumerate(((wq_hbm, wq), (wk_hbm, wk), (wv_hbm, wv), (wo_hbm, wo)))
    ]
    for k in (3, 0, 1, 2):
        copies[k].start()
    grad = grad_ref[...]
    if more_ref is not None:
        grad = grad + more_ref[...]
    middle = middle_ref[...]
    inverse = lax.rsqrt(jnp.mean(middle * middle, axis=-1, keepdims=True) + EPS)
    unit = middle * inverse
    gain_out_ref[...] = jnp.sum(grad * unit, axis=0, keepdims=True)
    scaled = grad * gain_ref[...].astype(F32)
    grad_mid = cot_ref[...].astype(F32) * live_flag(slot_ref, live_ref) + inverse * (
        scaled - unit * jnp.mean(scaled * unit, axis=-1, keepdims=True)
    )
    grad_mid_ref[...] = grad_mid
    dm = grad_mid.astype(BF16)
    dm_ref[...] = dm
    tok = dm.shape[0]
    heads = wq.shape[1] // HEAD_DIM
    kv = wk.shape[1] // HEAD_DIM
    group = heads // kv
    first = first_ref[slot_ref[0]]
    cosine, sine = row_turns(first, cos_ref, sin_ref)
    sine = -sine
    allowed = allowed_pairs(first, tok, group)
    copies[3].wait()
    grad_att = times_transpose(dm, wo[...]).astype(BF16)
    grad_q, grad_k, grad_v = [], [], []
    scale = HEAD_DIM**-0.5
    for k in range(kv):
        q_rows = head_rows(kept_ref, k * group, group)
        keys = kept_ref[:, (heads + k) * HEAD_DIM : (heads + k + 1) * HEAD_DIM]
        values = kept_ref[:, (heads + kv + k) * HEAD_DIM : (heads + kv + k + 1) * HEAD_DIM]
        prob = softmax_rows(q_rows, keys, allowed)
        d_rows = head_rows(grad_att, k * group, group)
        grad_v.append(contract_rows(prob.astype(BF16), d_rows))
        grad_prob = times_transpose(d_rows, values)
        delta = jnp.sum(prob * grad_prob, axis=-1, keepdims=True)
        grad_score = (prob * (grad_prob - delta)).astype(BF16)
        rows = jnp.dot(grad_score, keys, preferred_element_type=F32) * scale
        grad_q += [rows[g * tok : (g + 1) * tok] for g in range(group)]
        grad_k.append(contract_rows(grad_score, q_rows) * scale)

    def turned_back(parts):
        pairs = [jnp.concatenate(parts[k : k + 2], axis=1) for k in range(0, len(parts), 2)]
        return jnp.concatenate([turn(p, cosine, sine).astype(BF16) for p in pairs], axis=1)

    lin_q = turned_back(grad_q)
    lin_k = turned_back(grad_k)
    lin_v = jnp.concatenate(grad_v, axis=1).astype(BF16)
    cols, kv_cols = heads * HEAD_DIM, kv * HEAD_DIM
    lin_ref[0, :, :cols] = lin_q.astype(F32)
    lin_ref[0, :, cols : cols + kv_cols] = lin_k.astype(F32)
    lin_ref[0, :, cols + kv_cols :] = lin_v.astype(F32)
    for k in range(3):
        copies[k].wait()
    part_ref[...] = (
        times_transpose(lin_q, wq[...]) + times_transpose(lin_k, wk[...]) + times_transpose(lin_v, wv[...])
    )


def attend_back(
    entry, slot, first_len, live_rows, grads, middle, cotangent, gain, kept, tables, lin, w_query, w_key, w_value, w_output
):
    tok, wide = middle.shape
    cols = w_query.shape[1]
    kv_cols = w_key.shape[1]
    weights = (w_query, w_key, w_value, w_output)
    aliased = () if lin is None else (lin,)
    rows = pl.BlockSpec((tok, wide), lambda j, s: (0, 0))

    def whole(array):
        return pl.BlockSpec(array.shape, lambda j, s: (0,) * array.ndim)

    def kernel(slot_ref, first_ref, live_ref, grad_ref, *refs):
        if len(grads) == 1:
            refs = (None, *refs)
        attend_back_kernel(slot_ref, first_ref, live_ref, grad_ref, *refs)

    return pl.pallas_call(
        kernel,
        grid_spec=pltpu.PrefetchScalarGridSpec(
            num_scalar_prefetch=1,
            grid=(1,),
            in_specs=[
                pl.BlockSpec(memory_space=pltpu.SMEM),
                pl.BlockSpec(memory_space=pltpu.SMEM),
                *[rows] * (len(grads) + 1),
                pl.BlockSpec((tok, wide), lambda j, s: (s[0], 0)),
                whole(gain),
                whole(kept),
                whole(tables[0]),
                whole(tables[1]),
            ]
            + [pl.BlockSpec(memory_space=pl.ANY)] * (4 + len(aliased)),
            out_specs=[
                rows,
                rows,
                rows,
                pl.BlockSpec((1, tok, cols + 2 * kv_cols), lambda j, s: (entry, 0, 0)),
                pl.BlockSpec((1, wide), lambda j, s: (0, 0)),
            ],
            scratch_shapes=[pltpu.VMEM(w.shape, w.dtype) for w in weights] + [pltpu.SemaphoreType.DMA((4,))],
        ),
        out_shape=[
            jax.ShapeDtypeStruct((tok, wide), F32),
            jax.ShapeDtypeStruct((tok, wide), F32),
            jax.ShapeDtypeStruct((tok, wide), BF16),
            jax.ShapeDtypeStruct((2, tok, cols + 2 * kv_cols), F32),
            jax.ShapeDtypeStruct((1, wide), F32),
        ],
        input_output_aliases={13 + len(grads): 3} if aliased else {},
        compiler_params=pltpu.CompilerParams(vmem_limit_bytes=ATTEND_VMEM),
        cost_estimate=cost(S_attend_back,
            2 * tok * wide * (2 * cols + 2 * kv_cols) + 10 * tok * tok * cols,
            sum(w.size * 2 for w in weights) + tok * wide * 24,
            tok * tok * cols // HEAD_DIM,
        ),
        name="attend_back",
    )(slot, first_len, live_rows, *grads, middle, cotangent, gain, kept, *tables, *weights, *aliased)


def blocks_kernel(core_ref, first_ref, second_ref, own_ref, other_ref):
    rows = [
        ref[...].astype(F32) * core_ref[3 + k].astype(F32) for k, ref in enumerate((first_ref, second_ref))
    ]
    rows = jnp.concatenate(rows, axis=0)
    core = core_ref[0]
    for k in range(rows.shape[1] // 128):
        turned = jnp.transpose(rows[:, k * 128 : (k + 1) * 128])
        low, high = turned[:64], turned[64:]
        own_ref[k * 64 : (k + 1) * 64, :] = jnp.where(core == 0, low, high).astype(BF16)
        other_ref[k * 64 : (k + 1) * 64, :] = jnp.where(core == 0, high, low)


def by_block(choice, first, second):
    tok = 192
    chips = 8
    return pl.pallas_call(
        blocks_kernel,
        grid_spec=pltpu.PrefetchScalarGridSpec(
            num_scalar_prefetch=1,
            grid=(16 // chips,),
            in_specs=[
                pl.BlockSpec((tok, 128 * chips), lambda j, o: (o[1], j)),
                pl.BlockSpec((tok, 128 * chips), lambda j, o: (o[2], j)),
            ],
            out_specs=[pl.BlockSpec((64 * chips, 2 * tok), lambda j, o: (j, 0))] * 2,
        ),
        out_shape=[
            jax.ShapeDtypeStruct((1024, 2 * tok), BF16),
            jax.ShapeDtypeStruct((1024, 2 * tok), F32),
        ],
        compiler_params=pltpu.CompilerParams(vmem_limit_bytes=SMALL_VMEM),
        cost_estimate=cost(S_by_block, 0, 2048 * tok * 10),
        name="by_block",
    )(choice, first, second)


def live_flag(slot_ref, live_ref):
    return jnp.where(slot_ref[0] < live_ref[0], 1.0, 0.0)


def mlp_kernel(
    slot_ref, live_ref, middle_ref, cot_ref, gain_ref, wg_ref, wu_ref, wd_ref, *refs
):
    out_ref, grad_ref, act_ref, normed_ref, dy = refs[-5:]
    step = pl.program_id(0)

    @pl.when(step == 0)
    def _():
        middle = middle_ref[...]
        inverse = lax.rsqrt(jnp.mean(middle * middle, axis=-1, keepdims=True) + EPS)
        normed_ref[...] = (middle * inverse * gain_ref[...].astype(F32)).astype(BF16)
        dy[...] = (cot_ref[...].astype(F32) * live_flag(slot_ref, live_ref)).astype(BF16)

    n = normed_ref[...]
    w_gate = wg_ref[...]
    w_up = wu_ref[...]
    w_down = wd_ref[...]
    gate = jnp.dot(n, w_gate, preferred_element_type=F32)
    up = jnp.dot(n, w_up, preferred_element_type=F32)
    grad_hidden = times_transpose(dy[...], w_down)
    sig = 1.0 / (1.0 + jnp.exp(-gate))
    silu = gate * sig
    hidden = (silu * up).astype(BF16)
    d_gate = (grad_hidden * up * sig * (1.0 + gate * (1.0 - sig))).astype(BF16)
    d_up = (grad_hidden * silu).astype(BF16)
    act_ref[0] = hidden.astype(F32)
    act_ref[1] = d_gate.astype(F32)
    act_ref[2] = d_up.astype(F32)
    out_part = jnp.dot(hidden, w_down, preferred_element_type=F32)
    grad_part = times_transpose(d_gate, w_gate) + times_transpose(d_up, w_up)

    @pl.when(step == 0)
    def _():
        if len(refs) > 5:
            out_ref[...] = refs[0][...] + out_part
            grad_ref[...] = refs[1][...] + grad_part
        else:
            out_ref[...] = out_part
            grad_ref[...] = grad_part

    @pl.when(step > 0)
    def _():
        out_ref[...] += out_part
        grad_ref[...] += grad_part


def mlp(slot, live_rows, middle, cotangent, gain, w_gate, w_up, w_down, start, units, sums=()):
    tok, wide = middle.shape
    tile = 512
    offset = start // tile
    whole = pl.BlockSpec((tok, wide), lambda t, s: (0, 0))
    return pl.pallas_call(
        mlp_kernel,
        grid_spec=pltpu.PrefetchScalarGridSpec(
            num_scalar_prefetch=1,
            grid=(units // tile,),
            in_specs=[
                pl.BlockSpec(memory_space=pltpu.SMEM),
                whole,
                pl.BlockSpec((tok, wide), lambda t, s: (s[0], 0)),
                pl.BlockSpec((1, wide), lambda t, s: (0, 0)),
                pl.BlockSpec((wide, tile), lambda t, s: (0, t + offset)),
                pl.BlockSpec((wide, tile), lambda t, s: (0, t + offset)),
                pl.BlockSpec((tile, wide), lambda t, s: (t + offset, 0)),
            ]
            + [whole] * len(sums),
            out_specs=[whole, whole, pl.BlockSpec((3, tok, tile), lambda t, s: (0, 0, t)), whole],
            scratch_shapes=[pltpu.VMEM((tok, wide), BF16)],
        ),
        out_shape=[
            jax.ShapeDtypeStruct((tok, wide), F32),
            jax.ShapeDtypeStruct((tok, wide), F32),
            jax.ShapeDtypeStruct((3, tok, units), F32),
            jax.ShapeDtypeStruct((tok, wide), BF16),
        ],
        compiler_params=pltpu.CompilerParams(vmem_limit_bytes=MLP_VMEM),
        cost_estimate=cost(S_mlp, 12 * tok * wide * units, 3 * wide * units * 2 + 5 * tok * wide * 4, tok * units),
        name="mlp",
    )(slot, live_rows, middle, cotangent, gain, w_gate, w_up, w_down, *sums)


def mlp_weight_kernel(dy_own, dy_other, two_own, two_other, *refs):
    rhs_refs, out_ref, lhs = refs[:4], refs[-2], refs[-1]
    tok = dy_own.shape[-1]
    step = pl.program_id(0)
    for k, (own, other) in enumerate(((dy_own, dy_other), (two_own, two_other))):

        @pl.when(step == k)
        def _(own=own, other=other):
            lhs[:, :tok] = own[...]
            lhs[:, tok:] = other[...].astype(BF16)

    rhs = jnp.concatenate([ref[0].astype(BF16) for ref in rhs_refs], axis=0)
    out_ref[...] = jnp.dot(lhs[...], rhs, preferred_element_type=F32)


def mlp_weight_grad(half, dy_own, dy_other, two_own, two_other, acts, starts, grads):
    kinds, tok, _ = acts[0].shape
    tile = 1024
    whole = pl.BlockSpec(dy_own.shape, lambda j: (0, 0))
    aliased = () if grads is None else (grads,)
    return pl.pallas_call(
        mlp_weight_kernel,
        grid=(kinds,),
        in_specs=[whole] * 4
        + [pl.BlockSpec((1, tok, tile), lambda j, at=start // tile: (j, 0, at)) for start in starts]
        + [pl.BlockSpec(memory_space=pl.ANY)] * len(aliased),
        out_specs=pl.BlockSpec((1024, tile), lambda j: (0, 2 * j + half)),
        scratch_shapes=[pltpu.VMEM((1024, 4 * tok), BF16)],
        out_shape=jax.ShapeDtypeStruct((1024, kinds * 2 * tile), F32),
        input_output_aliases={8: 0} if aliased else {},
        compiler_params=pltpu.CompilerParams(vmem_limit_bytes=WEIGHT_VMEM),
        cost_estimate=cost(S_mlp_weight_grad, 2 * 1024 * 4 * tok * kinds * 1024, (1024 + 4 * tok) * kinds * 1024 * 4),
        name="mlp_weight_grad",
    )(dy_own, dy_other, two_own, two_other, *acts, *aliased)


def tokens_kernel(slot_ref, grad_ref, mid_ref, x_ref, gain_ref, *refs):
    out_ref, gain_out_ref = refs[-2:]
    grad = grad_ref[...]
    x = x_ref[...].astype(F32)
    inverse = lax.rsqrt(jnp.mean(x * x, axis=-1, keepdims=True) + EPS)
    unit = x * inverse
    scaled = grad * gain_ref[...].astype(F32)
    out_ref[...] = mid_ref[...] + inverse * (scaled - unit * jnp.mean(scaled * unit, axis=-1, keepdims=True))
    gain_part = jnp.sum(grad * unit, axis=0, keepdims=True)

    @pl.when(pl.program_id(0) == 0)
    def _():
        gain_out_ref[...] = gain_part

    @pl.when(pl.program_id(0) > 0)
    def _():
        gain_out_ref[...] += gain_part


def tokens_slot(slot, grad, grad_mid, tokens, gain, whole):
    tok, wide = grad.shape
    parts = 2
    tile = tok // parts
    aliased = () if whole is None else (whole,)
    rows = pl.BlockSpec((tile, wide), lambda j, s: (j, 0))
    in_whole = pl.BlockSpec((tile, wide), lambda j, s: (s[0] * parts + j, 0))
    line = pl.BlockSpec((1, wide), lambda j, s: (0, 0))
    return pl.pallas_call(
        tokens_kernel,
        grid_spec=pltpu.PrefetchScalarGridSpec(
            num_scalar_prefetch=1,
            grid=(parts,),
            in_specs=[rows, rows, in_whole, line] + [pl.BlockSpec(memory_space=pl.ANY)] * len(aliased),
            out_specs=[in_whole, line],
        ),
        out_shape=[jax.ShapeDtypeStruct((2 * tok, wide), F32), jax.ShapeDtypeStruct((1, wide), F32)],
        input_output_aliases={5: 0} if aliased else {},
        compiler_params=pltpu.CompilerParams(vmem_limit_bytes=SMALL_VMEM),
        cost_estimate=cost(S_grad_tokens, 10 * tok * wide, 14 * tok * wide),
        name="grad_tokens",
    )(slot, grad, grad_mid, tokens, gain, *aliased)


def layer_kernel(slot_ref, live_ref, middle_ref, sum_ref, *refs):
    refs[-1][...] = (live_flag(slot_ref, live_ref) * (middle_ref[...] + sum_ref[...])).astype(BF16)


def layer_slot(slot, live_rows, middle, added, whole):
    tok, wide = middle.shape
    parts = 2
    tile = tok // parts
    aliased = () if whole is None else (whole,)
    rows = pl.BlockSpec((tile, wide), lambda j, s: (j, 0))
    return pl.pallas_call(
        layer_kernel,
        grid_spec=pltpu.PrefetchScalarGridSpec(
            num_scalar_prefetch=1,
            grid=(parts,),
            in_specs=[pl.BlockSpec(memory_space=pltpu.SMEM), rows, rows]
            + [pl.BlockSpec(memory_space=pl.ANY)] * len(aliased),
            out_specs=pl.BlockSpec((tile, wide), lambda j, s: (s[0] * parts + j, 0)),
        ),
        out_shape=jax.ShapeDtypeStruct((2 * tok, wide), BF16),
        input_output_aliases={4: 0} if aliased else {},
        compiler_params=pltpu.CompilerParams(vmem_limit_bytes=SMALL_VMEM),
        cost_estimate=cost(S_layer_out, 2 * tok * wide, 10 * tok * wide),
        name="layer_out",
    )(slot, live_rows, middle, added, *aliased)


def weight_kernel(order_ref, own_ref, other_ref, k_ref, n_ref, k_other_ref, n_other_ref, *refs):
    send_ref, keep_ref, lhs = refs[-3:]
    tok = own_ref.shape[-1]
    cols = k_ref.shape[-1]
    for place in range(16):
        chip = pl.multiple_of(order_ref[place] * 64, 64)
        lhs[pl.ds(place * 64, 64), :tok] = own_ref[pl.ds(chip, 64), :]
        lhs[pl.ds(place * 64, 64), tok:] = other_ref[pl.ds(chip, 64), :].astype(BF16)
        if len(refs) > 3:
            half = (send_ref, keep_ref)[place // 8]
            half[pl.ds(place % 8 * 64, 64), cols:] = refs[0][pl.ds(chip, 64), :]
    rhs = jnp.concatenate([ref[0].astype(BF16) for ref in (k_ref, n_ref, k_other_ref, n_other_ref)], axis=0)
    send_ref[:, :cols] = jnp.dot(lhs[:512], rhs, preferred_element_type=F32)
    keep_ref[:, :cols] = jnp.dot(lhs[512:], rhs, preferred_element_type=F32)


def weight_grad(order, own, other, here, there, extra=()):
    _, tok, cols = here.shape
    wide = cols + sum(e.shape[1] for e in extra)

    def whole(array):
        return pl.BlockSpec(array.shape, lambda j, o: (0, 0))

    first = pl.BlockSpec((1, tok, cols), lambda j, o: (0, 0, 0))
    second = pl.BlockSpec((1, tok, cols), lambda j, o: (1, 0, 0))
    return pl.pallas_call(
        weight_kernel,
        grid_spec=pltpu.PrefetchScalarGridSpec(
            num_scalar_prefetch=1,
            grid=(1,),
            in_specs=[whole(own), whole(other), first, second, first, second] + [whole(e) for e in extra],
            out_specs=[pl.BlockSpec((512, wide), lambda j, o: (0, 0))] * 2,
            scratch_shapes=[pltpu.VMEM((1024, 4 * tok), BF16)],
        ),
        out_shape=[jax.ShapeDtypeStruct((512, wide), F32)] * 2,
        compiler_params=pltpu.CompilerParams(vmem_limit_bytes=WEIGHT_VMEM),
        cost_estimate=cost(S_weight_grad, 2 * 1024 * 4 * tok * cols, (1024 + 4 * tok) * wide * 4 + 1024 * tok * 12),
        name="weight_grad",
    )(order, own, other, here, here, there, there, *extra)


PLANES = [[chip * 2 + core for chip in range(16)] for core in range(2)]


def plane_sum(array):
    return lax.psum_scatter(array, "dp", scatter_dimension=0, axis_index_groups=PLANES, tiled=True)


class Piece:
    def __init__(self, stream, send, keep):
        self.perms, self.send, self.keep, self.step = STREAMS[stream], send, keep, 0

    def exchange(self, *after):
        if after:
            self.send = tie(self.send, *after)[0]
        got = swap(self.send, self.perms[self.step])
        self.step += 1
        rows = self.keep.shape[0] // 2
        if self.step == 4:
            self.keep = self.keep + got
        else:
            self.send, self.keep = self.keep[:rows] + got[:rows], self.keep[rows:] + got[rows:]
        return got


def after(value, *others):
    return tie(value, *others)[0]


def ring_sum(parts, at, perms):
    total = lax.dynamic_index_in_dim(parts, at, keepdims=False)
    for k, perm in enumerate(perms):
        total = total + swap(lax.dynamic_index_in_dim(parts, (at + k + 1) % 4, keepdims=False), perm)
    return total


def tie(*arrays):
    return lax.optimization_barrier(arrays)


def on_device(
    tokens,
    norm1_gain,
    w_query,
    w_key,
    w_value,
    w_output,
    norm2_gain,
    w_gate,
    w_up,
    w_down,
    cotangent,
    first_len,
    live_rows,
):
    dp = lax.axis_index("dp")
    y = lax.axis_index("tensor")
    z, x, c = dp // 8, (dp // 2) % 4, dp % 2
    slot = jnp.where(c == 0, low_bit(y), high_bit(y))
    orders = [block_order(s, z, x, c).astype(jnp.int32) for s in range(2)]
    tok, wide = tokens.shape
    gain_one = norm1_gain[None]
    gain_two = norm2_gain[None]
    tables = turn_tables(tok // 2)
    slot_k = jnp.reshape(slot, (1,)).astype(jnp.int32)
    slot_n = 1 - slot_k
    core = jnp.reshape(c, (1,)).astype(jnp.int32)
    plain = jnp.concatenate([core, jnp.array([0, 0, 1, 1], jnp.int32)])
    live = [(s < live_rows).astype(jnp.int32) for s in (slot_k, slot_n)]
    masked = jnp.concatenate([core, slot_k, slot_n, *live])

    weights = (w_query, w_key, w_value, w_output)
    part_n, one_n, attended, kept_n = attend(1, slot_n, first_len, tokens, gain_one, tables, None, *weights)
    got = swap(part_n, ALONG_Y[0])
    part_k, one_k, attended, kept_k = attend(0, slot_k, first_len, tokens, gain_one, tables, attended, *weights)
    half = part_k + got
    x_k = lax.dynamic_slice_in_dim(tokens, slot * (tok // 2), tok // 2, 0).astype(F32)
    middle_k = x_k + half + swap(half, ALONG_Y[1])
    masked, plain, part_k = tie(masked, plain, part_k)
    dy_own, dy_other = by_block(masked, cotangent, cotangent)
    dy_other = swap(dy_other, OTHER_CORE)
    one_own, one_other = by_block(plain, one_k, one_n)
    one_other = swap(one_other, OTHER_CORE)

    attended_other = swap(attended, OTHER_CORE)
    feed = (w_gate, w_up, w_down)
    middle_n = swap(middle_k, ALONG_Y[0])
    out_k, back_k, act_k, two_k = mlp(
        after(slot_k, dy_other, one_other, attended_other) if T7 else slot_k, live_rows, middle_k, cotangent, gain_two, *feed, 0, 2048
    )
    got = swap(back_k, ALONG_Y[0])
    act_k_other = swap(act_k, OTHER_CORE)
    slot_n, out_k = tie(slot_n, out_k)
    out_n, back_n, act_n1, two_n = mlp(slot_n, live_rows, middle_n, cotangent, gain_two, *feed, 0, 1024)
    act_n1_other = swap(act_n1, OTHER_CORE)
    two_own, two_other = by_block(plain, two_k, two_n)
    two_other = swap(two_other, OTHER_CORE)
    live_rows = after(live_rows, two_own)
    if T8:
        live_rows = after(live_rows, act_k_other)
    out_n, back_n, act_n2, _ = mlp(
        slot_n, live_rows, middle_n, cotangent, gain_two, *feed, 1024, 1024, (out_n, back_n)
    )
    act_n2_other = swap(act_n2, OTHER_CORE)

    half = back_n + got
    got = swap(half, ALONG_Y[1])
    grad_2n = half + got
    lefts = (dy_own, dy_other, after(two_own, half) if W1 else two_own, two_other)
    grads = mlp_weight_grad(0, *lefts, (act_k, act_n1, act_k_other, act_n1_other), (0, 0, 0, 0), None)
    grads = mlp_weight_grad(1, *lefts, (act_k, act_n2, act_k_other, act_n2_other), (1024, 0, 1024, 0), grads)
    slot_back, grads = tie(slot_n, grads)
    if not T1:
        slot_back = slot_n
    grads = plane_sum(grads)

    grad_2k = swap(grad_2n, ALONG_Y[0])
    back_n, grad_mid_n, dm_n, lin, gain_2 = attend_back(
        1, slot_back, first_len, live_rows, (half, got), middle_n, cotangent, gain_two, kept_n, tables, None, *weights
    )
    got = swap(back_n, ALONG_Y[0])
    out_got = swap(after(out_n, back_n) if U2 else out_n, ALONG_Y[0])
    back_k, grad_mid_k, dm_k, lin, _ = attend_back(
        0, slot_k, first_len, live_rows, (grad_2k,), middle_k, cotangent, gain_two, kept_k, tables, lin, *weights
    )
    lin_other = swap(lin, OTHER_CORE)
    dm_own, dm_other = by_block(after(plain, back_k), dm_k, dm_n)
    dm_other = swap(dm_other, OTHER_CORE)
    lin_grad = weight_grad(orders[0], one_own, one_other, lin, lin_other)
    out_grad = weight_grad(orders[1], dm_own, dm_other, attended, attended_other)
    lin_piece, out_piece = Piece(0, *lin_grad), Piece(1, *out_grad)
    three = [lin_piece, out_piece]
    if U3:
        back_k = after(back_k, lin_grad[1], out_grad[1])
    half = back_k + got
    if W4:
        lin_piece.send, out_piece.send = after(lin_piece.send, half), after(out_piece.send, half)
    grad_1k = half + swap(half, ALONG_Y[1])
    out_half = out_k + out_got
    out_sum = out_half + swap(after(out_half, half) if U4 else out_half, ALONG_Y[1])
    out_other = swap(out_sum, ALONG_Y[0])
    three_1 = [p.exchange() for p in three]

    grad_1n = swap(grad_1k, ALONG_Y[0])
    grad_tokens, gain_1 = tokens_slot(slot_k, grad_1k, grad_mid_k, tokens, gain_one, None)

    gains = jnp.concatenate([gain_1, gain_2], axis=0)
    gains = gains + swap(gains, ALONG_Y[0])
    gains = jnp.transpose(gains.reshape(2, 16, 2, 64), (2, 1, 0, 3)).reshape(2, 4, 4, 128)
    mine = lax.dynamic_index_in_dim(gains, c, keepdims=False)
    theirs = lax.dynamic_index_in_dim(gains, 1 - c, keepdims=False)
    mine = mine + swap(theirs, OTHER_CORE)
    mine = ring_sum(jnp.transpose(mine, (1, 0, 2)), x, RING_X)
    mine = ring_sum(mine.reshape(4, 1, 128), z, RING_Z)
    three_2 = [p.exchange(*([grad_1k] if W5 else [])) for p in three]
    three_3 = [p.exchange(*([out_sum] if W2 else [])) for p in three]
    three_4 = [p.exchange(*([grad_1n] if W6 else []), *([out_other] if W7 else [])) for p in three]
    query_key_value, output = lin_piece.keep, out_piece.keep
    layer_out = layer_slot(slot_k, live_rows, middle_k, out_sum, None)
    layer_out = layer_slot(slot_n, live_rows, middle_n, out_other, layer_out)
    grad_tokens, _ = tokens_slot(slot_n, grad_1n, grad_mid_n, tokens, gain_one, grad_tokens)

    return (
        layer_out,
        grad_tokens,
        mine[0, :64],
        query_key_value[:, :512],
        query_key_value[:, 512:640],
        query_key_value[:, 640:],
        jnp.transpose(output),
        mine[0, 64:],
        grads[:, 2048:4096],
        grads[:, 4096:],
        jnp.transpose(grads[:, :2048]),
    )


def solution(mesh):
    placed = (
        P("dp", None),
        P(),
        P(None, "tensor"),
        P(None, "tensor"),
        P(None, "tensor"),
        P("tensor", None),
        P(),
        P(None, "tensor"),
        P(None, "tensor"),
        P("tensor", None),
        P("dp", None),
        P("dp"),
        P("dp"),
    )
    return jax.shard_map(
        on_device,
        mesh=mesh,
        in_specs=placed,
        out_specs=(
            P("dp", None),
            P("dp", None),
            P("dp"),
            P("dp", "tensor"),
            P("dp", "tensor"),
            P("dp", "tensor"),
            P("tensor", "dp"),
            P("dp"),
            P("dp", "tensor"),
            P("dp", "tensor"),
            P("tensor", "dp"),
        ),
        check_vma=False,
    )
```

```python
import functools
import math

import jax
import jax.numpy as jnp
import numpy as np
from jax import lax
from jax.experimental import pallas as pl
from jax.experimental.pallas import tpu as pltpu
from jax.sharding import PartitionSpec as P

HEAD_DIM = 64
B2 = True
B4 = True
B5 = True
B7 = False
D1 = False
D8 = True
H1 = False
H2 = True
H3 = True
G1 = False
G2 = False
G3 = True
G4 = False
G5 = True
E3 = False
B1 = True
S_attend = 0.5
S_attend_back = 10.0
S_mlp = 2.5
S_mlp_weight_grad = 1.0
S_weight_grad = 2.5
S_by_block = 2.5
S_tk = 2.5
S_tn = 0.2
S_lk = 10.0
S_ln = 5.0
THETA = 500000.0
EPS = 1e-05
NEGATIVE = -1e30
F32 = jnp.float32
BF16 = jnp.bfloat16
ATTEND_VMEM = 58 * 1024 * 1024
MLP_VMEM = 58 * 1024 * 1024
WEIGHT_VMEM = 58 * 1024 * 1024
SMALL_VMEM = 58 * 1024 * 1024
AXES = ("dp", "tensor")


def pair_low(i):
    return i ^ 1


def pair_high(i):
    return 3 - i


def low_bit(v):
    return (v ^ (v >> 1)) & 1


def high_bit(v):
    return v >> 1


def from_bits(low, high):
    return jnp.where(high == 0, low, 3 - low)


def device_perm(move):
    pairs = []
    for dp in range(32):
        for y in range(4):
            z2, x2, c2, y2 = move(dp // 8, (dp // 2) % 4, dp % 2, y)
            pairs.append((dp * 4 + y, ((z2 * 4 + x2) * 2 + c2) * 4 + y2))
    return pairs


def first_pair(c, i):
    return pair_low(i) if c == 0 else pair_high(i)


def second_pair(c, i):
    return pair_high(i) if c == 0 else pair_low(i)


ALONG_Y = (
    device_perm(lambda z, x, c, y: (z, x, c, first_pair(c, y))),
    device_perm(lambda z, x, c, y: (z, x, c, second_pair(c, y))),
)
ALONG_X = (
    device_perm(lambda z, x, c, y: (z, first_pair(c, x), c, y)),
    device_perm(lambda z, x, c, y: (z, second_pair(c, x), c, y)),
)
ALONG_Z = (
    device_perm(lambda z, x, c, y: (first_pair(c, z), x, c, y)),
    device_perm(lambda z, x, c, y: (second_pair(c, z), x, c, y)),
)
OTHER_CORE = device_perm(lambda z, x, c, y: (z, x, 1 - c, y))
STREAMS = (ALONG_X + ALONG_Z, ALONG_Z + ALONG_X)


def swap(array, perm):
    return lax.ppermute(array, AXES, perm)


def block_order(stream, z, x, c):
    place = jnp.arange(16, dtype=jnp.int32)
    keep = [(place >> (3 - k)) & 1 for k in range(4)]

    def target(v, first, second):
        low = low_bit(v) ^ (1 - jnp.where(c == 0, first, second))
        high = high_bit(v) ^ (1 - jnp.where(c == 0, second, first))
        return from_bits(low, high)

    if stream == 0:
        return target(z, keep[2], keep[3]) * 4 + target(x, keep[0], keep[1])
    return target(z, keep[0], keep[1]) * 4 + target(x, keep[2], keep[3])


def turn_tables(tok):
    half = HEAD_DIM // 2
    freq = np.exp(np.arange(half) * (-2.0 * math.log(THETA) / HEAD_DIM))
    turned = np.arange(tok)[:, None] * freq[None, :]
    cosine, sine = np.cos(turned), np.sin(turned)
    return (
        jnp.asarray(np.tile(cosine, (1, 4)), F32),
        jnp.asarray(np.concatenate([-sine, sine, -sine, sine], axis=1), F32),
    )


def cost(scale, flops, moved, transcendentals=0):
    return pl.CostEstimate(flops=int(flops * scale), bytes_accessed=int(moved * scale), transcendentals=int(transcendentals * scale))


def times_transpose(left, right):
    return lax.dot_general(left, right, (((1,), (1,)), ((), ())), preferred_element_type=F32)


def contract_rows(left, right):
    return lax.dot_general(left, right, (((0,), (0,)), ((), ())), preferred_element_type=F32)


def turn(vectors, cosine, sine):
    lane = lax.broadcasted_iota(jnp.int32, vectors.shape, 1)
    ahead = pltpu.roll(vectors, 96, 1)
    behind = pltpu.roll(vectors, 32, 1)
    return vectors * cosine + jnp.where(lane % 64 < 32, ahead, behind) * sine


def row_turns(first, cos_ref, sin_ref):
    place = lax.broadcasted_iota(jnp.int32, cos_ref.shape, 0)
    return [jnp.where(place >= first, pltpu.roll(ref[...], first, 0), ref[...]) for ref in (cos_ref, sin_ref)]


def allowed_pairs(first, tok, group):
    query = lax.broadcasted_iota(jnp.int32, (group * tok, tok), 0) % tok
    key = lax.broadcasted_iota(jnp.int32, (group * tok, tok), 1)
    same = jnp.logical_not(jnp.logical_xor(query >= first, key >= first))
    return jnp.logical_and(same, key <= query)


def softmax_rows(queries, keys, allowed):
    raw = times_transpose(queries, keys) * HEAD_DIM**-0.5
    scores = jnp.where(allowed, raw, NEGATIVE)
    terms = jnp.exp(scores - jnp.max(scores, axis=-1, keepdims=True))
    return terms / jnp.sum(terms, axis=-1, keepdims=True)


def head_rows(array, head, count):
    return jnp.concatenate(
        [array[:, (head + k) * HEAD_DIM : (head + k + 1) * HEAD_DIM] for k in range(count)], axis=0
    )


def attend_kernel(
    slot_ref, first_ref, x_ref, gain_ref, cos_ref, sin_ref, wq_hbm, wk_hbm, wv_hbm, wo_hbm, *refs
):
    part_ref, normed_ref, attended_ref, kept_ref, wq, wk, wv, wo, sems = refs[-9:]
    copies = [
        pltpu.make_async_copy(src, dst, sems.at[k])
        for k, (src, dst) in enumerate(((wq_hbm, wq), (wk_hbm, wk), (wv_hbm, wv), (wo_hbm, wo)))
    ]
    for copy in copies:
        copy.start()
    x = x_ref[...].astype(F32)
    inverse = lax.rsqrt(jnp.mean(x * x, axis=-1, keepdims=True) + EPS)
    normed = (x * inverse * gain_ref[...].astype(F32)).astype(BF16)
    normed_ref[...] = normed
    first = first_ref[slot_ref[0]]
    cosine, sine = row_turns(first, cos_ref, sin_ref)
    tok = x.shape[0]
    heads = wq.shape[1] // HEAD_DIM
    kv = wk.shape[1] // HEAD_DIM
    group = heads // kv
    copies[0].wait()
    lin = jnp.dot(normed, wq[...], preferred_element_type=F32)
    queries = jnp.concatenate(
        [turn(lin[:, k * 128 : (k + 1) * 128], cosine, sine).astype(BF16) for k in range(heads // 2)], axis=1
    )
    copies[1].wait()
    lin = jnp.dot(normed, wk[...], preferred_element_type=F32)
    keys = jnp.concatenate(
        [turn(lin[:, k * 128 : (k + 1) * 128], cosine, sine).astype(BF16) for k in range(kv // 2)], axis=1
    )
    copies[2].wait()
    values = jnp.dot(normed, wv[...], preferred_element_type=F32).astype(BF16)
    kept_ref[:, : heads * HEAD_DIM] = queries
    kept_ref[:, heads * HEAD_DIM : (heads + kv) * HEAD_DIM] = keys
    kept_ref[:, (heads + kv) * HEAD_DIM :] = values
    allowed = allowed_pairs(first, tok, group)
    mixed = []
    for k in range(kv):
        lanes = slice(k * HEAD_DIM, (k + 1) * HEAD_DIM)
        prob = softmax_rows(head_rows(queries, k * group, group), keys[:, lanes], allowed).astype(BF16)
        out = jnp.dot(prob, values[:, lanes], preferred_element_type=F32)
        mixed += [out[g * tok : (g + 1) * tok] for g in range(group)]
    attended = jnp.concatenate(mixed, axis=1).astype(BF16)
    attended_ref[0] = attended.astype(F32)
    copies[3].wait()
    part_ref[...] = jnp.dot(attended, wo[...], preferred_element_type=F32)


def attend(entry, slot, first_len, tokens, gain, tables, attended, w_query, w_key, w_value, w_output):
    tok, wide = tokens.shape[0] // 2, tokens.shape[1]
    cols = w_query.shape[1]
    kv_cols = w_key.shape[1]
    weights = (w_query, w_key, w_value, w_output)
    aliased = () if attended is None else (attended,)

    def whole(array):
        return pl.BlockSpec(array.shape, lambda j, s: (0,) * array.ndim)

    return pl.pallas_call(
        attend_kernel,
        grid_spec=pltpu.PrefetchScalarGridSpec(
            num_scalar_prefetch=1,
            grid=(1,),
            in_specs=[
                pl.BlockSpec(memory_space=pltpu.SMEM),
                pl.BlockSpec((tok, wide), lambda j, s: (s[0], 0)),
                whole(gain),
                whole(tables[0]),
                whole(tables[1]),
            ]
            + [pl.BlockSpec(memory_space=pl.ANY)] * (4 + len(aliased)),
            out_specs=[
                pl.BlockSpec((tok, wide), lambda j, s: (0, 0)),
                pl.BlockSpec((tok, wide), lambda j, s: (0, 0)),
                pl.BlockSpec((1, tok, cols), lambda j, s: (entry, 0, 0)),
                pl.BlockSpec((tok, cols + 2 * kv_cols), lambda j, s: (0, 0)),
            ],
            scratch_shapes=[pltpu.VMEM(w.shape, w.dtype) for w in weights] + [pltpu.SemaphoreType.DMA((4,))],
        ),
        out_shape=[
            jax.ShapeDtypeStruct((tok, wide), F32),
            jax.ShapeDtypeStruct((tok, wide), BF16),
            jax.ShapeDtypeStruct((2, tok, cols), F32),
            jax.ShapeDtypeStruct((tok, cols + 2 * kv_cols), BF16),
        ],
        input_output_aliases={10: 2} if aliased else {},
        compiler_params=pltpu.CompilerParams(vmem_limit_bytes=ATTEND_VMEM),
        cost_estimate=cost(S_attend,
            2 * tok * wide * (2 * cols + 2 * kv_cols) + 4 * tok * tok * cols,
            sum(w.size * 2 for w in weights) + tok * wide * 8,
            tok * tok * cols // HEAD_DIM,
        ),
        name="attend",
    )(slot, first_len, tokens, gain, *tables, *weights, *aliased)


def attend_back_kernel(
    slot_ref, first_ref, live_ref, grad_ref, more_ref, middle_ref, cot_ref, gain_ref, kept_ref, cos_ref, sin_ref,
    wq_hbm, wk_hbm, wv_hbm, wo_hbm, *refs
):
    part_ref, grad_mid_ref, dm_ref, lin_ref, gain_out_ref, wq, wk, wv, wo, sems = refs[-10:]
    copies = [
        pltpu.make_async_copy(src, dst, sems.at[k])
        for k, (src, dst) in enumerate(((wq_hbm, wq), (wk_hbm, wk), (wv_hbm, wv), (wo_hbm, wo)))
    ]
    for k in (3, 0, 1, 2):
        copies[k].start()
    grad = grad_ref[...]
    if more_ref is not None:
        grad = grad + more_ref[...]
    middle = middle_ref[...]
    inverse = lax.rsqrt(jnp.mean(middle * middle, axis=-1, keepdims=True) + EPS)
    unit = middle * inverse
    gain_out_ref[...] = jnp.sum(grad * unit, axis=0, keepdims=True)
    scaled = grad * gain_ref[...].astype(F32)
    grad_mid = cot_ref[...].astype(F32) * live_flag(slot_ref, live_ref) + inverse * (
        scaled - unit * jnp.mean(scaled * unit, axis=-1, keepdims=True)
    )
    grad_mid_ref[...] = grad_mid
    dm = grad_mid.astype(BF16)
    dm_ref[...] = dm
    tok = dm.shape[0]
    heads = wq.shape[1] // HEAD_DIM
    kv = wk.shape[1] // HEAD_DIM
    group = heads // kv
    first = first_ref[slot_ref[0]]
    cosine, sine = row_turns(first, cos_ref, sin_ref)
    sine = -sine
    allowed = allowed_pairs(first, tok, group)
    copies[3].wait()
    grad_att = times_transpose(dm, wo[...]).astype(BF16)
    grad_q, grad_k, grad_v = [], [], []
    scale = HEAD_DIM**-0.5
    for k in range(kv):
        q_rows = head_rows(kept_ref, k * group, group)
        keys = kept_ref[:, (heads + k) * HEAD_DIM : (heads + k + 1) * HEAD_DIM]
        values = kept_ref[:, (heads + kv + k) * HEAD_DIM : (heads + kv + k + 1) * HEAD_DIM]
        prob = softmax_rows(q_rows, keys, allowed)
        d_rows = head_rows(grad_att, k * group, group)
        grad_v.append(contract_rows(prob.astype(BF16), d_rows))
        grad_prob = times_transpose(d_rows, values)
        delta = jnp.sum(prob * grad_prob, axis=-1, keepdims=True)
        grad_score = (prob * (grad_prob - delta)).astype(BF16)
        rows = jnp.dot(grad_score, keys, preferred_element_type=F32) * scale
        grad_q += [rows[g * tok : (g + 1) * tok] for g in range(group)]
        grad_k.append(contract_rows(grad_score, q_rows) * scale)

    def turned_back(parts):
        pairs = [jnp.concatenate(parts[k : k + 2], axis=1) for k in range(0, len(parts), 2)]
        return jnp.concatenate([turn(p, cosine, sine).astype(BF16) for p in pairs], axis=1)

    lin_q = turned_back(grad_q)
    lin_k = turned_back(grad_k)
    lin_v = jnp.concatenate(grad_v, axis=1).astype(BF16)
    cols, kv_cols = heads * HEAD_DIM, kv * HEAD_DIM
    lin_ref[0, :, :cols] = lin_q.astype(F32)
    lin_ref[0, :, cols : cols + kv_cols] = lin_k.astype(F32)
    lin_ref[0, :, cols + kv_cols :] = lin_v.astype(F32)
    for k in range(3):
        copies[k].wait()
    part_ref[...] = (
        times_transpose(lin_q, wq[...]) + times_transpose(lin_k, wk[...]) + times_transpose(lin_v, wv[...])
    )


def attend_back(
    entry, slot, first_len, live_rows, grads, middle, cotangent, gain, kept, tables, lin, w_query, w_key, w_value, w_output
):
    tok, wide = middle.shape
    cols = w_query.shape[1]
    kv_cols = w_key.shape[1]
    weights = (w_query, w_key, w_value, w_output)
    aliased = () if lin is None else (lin,)
    rows = pl.BlockSpec((tok, wide), lambda j, s: (0, 0))

    def whole(array):
        return pl.BlockSpec(array.shape, lambda j, s: (0,) * array.ndim)

    def kernel(slot_ref, first_ref, live_ref, grad_ref, *refs):
        if len(grads) == 1:
            refs = (None, *refs)
        attend_back_kernel(slot_ref, first_ref, live_ref, grad_ref, *refs)

    return pl.pallas_call(
        kernel,
        grid_spec=pltpu.PrefetchScalarGridSpec(
            num_scalar_prefetch=1,
            grid=(1,),
            in_specs=[
                pl.BlockSpec(memory_space=pltpu.SMEM),
                pl.BlockSpec(memory_space=pltpu.SMEM),
                *[rows] * (len(grads) + 1),
                pl.BlockSpec((tok, wide), lambda j, s: (s[0], 0)),
                whole(gain),
                whole(kept),
                whole(tables[0]),
                whole(tables[1]),
            ]
            + [pl.BlockSpec(memory_space=pl.ANY)] * (4 + len(aliased)),
            out_specs=[
                rows,
                rows,
                rows,
                pl.BlockSpec((1, tok, cols + 2 * kv_cols), lambda j, s: (entry, 0, 0)),
                pl.BlockSpec((1, wide), lambda j, s: (0, 0)),
            ],
            scratch_shapes=[pltpu.VMEM(w.shape, w.dtype) for w in weights] + [pltpu.SemaphoreType.DMA((4,))],
        ),
        out_shape=[
            jax.ShapeDtypeStruct((tok, wide), F32),
            jax.ShapeDtypeStruct((tok, wide), F32),
            jax.ShapeDtypeStruct((tok, wide), BF16),
            jax.ShapeDtypeStruct((2, tok, cols + 2 * kv_cols), F32),
            jax.ShapeDtypeStruct((1, wide), F32),
        ],
        input_output_aliases={13 + len(grads): 3} if aliased else {},
        compiler_params=pltpu.CompilerParams(vmem_limit_bytes=ATTEND_VMEM),
        cost_estimate=cost(S_attend_back,
            2 * tok * wide * (2 * cols + 2 * kv_cols) + 10 * tok * tok * cols,
            sum(w.size * 2 for w in weights) + tok * wide * 24,
            tok * tok * cols // HEAD_DIM,
        ),
        name="attend_back",
    )(slot, first_len, live_rows, *grads, middle, cotangent, gain, kept, *tables, *weights, *aliased)


def blocks_kernel(core_ref, first_ref, second_ref, own_ref, other_ref):
    rows = [
        ref[...].astype(F32) * core_ref[3 + k].astype(F32) for k, ref in enumerate((first_ref, second_ref))
    ]
    rows = jnp.concatenate(rows, axis=0)
    core = core_ref[0]
    for k in range(rows.shape[1] // 128):
        turned = jnp.transpose(rows[:, k * 128 : (k + 1) * 128])
        low, high = turned[:64], turned[64:]
        own_ref[k * 64 : (k + 1) * 64, :] = jnp.where(core == 0, low, high).astype(BF16)
        other_ref[k * 64 : (k + 1) * 64, :] = jnp.where(core == 0, high, low)


def by_block(choice, first, second):
    tok = 192
    chips = 8
    return pl.pallas_call(
        blocks_kernel,
        grid_spec=pltpu.PrefetchScalarGridSpec(
            num_scalar_prefetch=1,
            grid=(16 // chips,),
            in_specs=[
                pl.BlockSpec((tok, 128 * chips), lambda j, o: (o[1], j)),
                pl.BlockSpec((tok, 128 * chips), lambda j, o: (o[2], j)),
            ],
            out_specs=[pl.BlockSpec((64 * chips, 2 * tok), lambda j, o: (j, 0))] * 2,
        ),
        out_shape=[
            jax.ShapeDtypeStruct((1024, 2 * tok), BF16),
            jax.ShapeDtypeStruct((1024, 2 * tok), F32),
        ],
        compiler_params=pltpu.CompilerParams(vmem_limit_bytes=SMALL_VMEM),
        cost_estimate=cost(S_by_block, 0, 2048 * tok * 10),
        name="by_block",
    )(choice, first, second)


def live_flag(slot_ref, live_ref):
    return jnp.where(slot_ref[0] < live_ref[0], 1.0, 0.0)


def mlp_kernel(
    slot_ref, live_ref, middle_ref, cot_ref, gain_ref, wg_ref, wu_ref, wd_ref, *refs
):
    out_ref, grad_ref, hidden_ref, act_ref, normed_ref, dy = refs[-6:]
    step = pl.program_id(0)

    @pl.when(step == 0)
    def _():
        middle = middle_ref[...]
        inverse = lax.rsqrt(jnp.mean(middle * middle, axis=-1, keepdims=True) + EPS)
        normed_ref[...] = (middle * inverse * gain_ref[...].astype(F32)).astype(BF16)
        dy[...] = (cot_ref[...].astype(F32) * live_flag(slot_ref, live_ref)).astype(BF16)

    n = normed_ref[...]
    w_gate = wg_ref[...]
    w_up = wu_ref[...]
    w_down = wd_ref[...]
    gate = jnp.dot(n, w_gate, preferred_element_type=F32)
    up = jnp.dot(n, w_up, preferred_element_type=F32)
    grad_hidden = times_transpose(dy[...], w_down)
    sig = 1.0 / (1.0 + jnp.exp(-gate))
    silu = gate * sig
    hidden = (silu * up).astype(BF16)
    d_gate = (grad_hidden * up * sig * (1.0 + gate * (1.0 - sig))).astype(BF16)
    d_up = (grad_hidden * silu).astype(BF16)
    hidden_ref[...] = hidden.astype(F32)
    act_ref[0] = d_gate.astype(F32)
    act_ref[1] = d_up.astype(F32)
    out_part = jnp.dot(hidden, w_down, preferred_element_type=F32)
    grad_part = times_transpose(d_gate, w_gate) + times_transpose(d_up, w_up)

    @pl.when(step == 0)
    def _():
        out_ref[...] = out_part
        grad_ref[...] = grad_part

    @pl.when(step > 0)
    def _():
        out_ref[...] += out_part
        grad_ref[...] += grad_part


def mlp(slot, live_rows, middle, cotangent, gain, w_gate, w_up, w_down):
    tok, wide = middle.shape
    units = w_gate.shape[1]
    tile = 512
    whole = pl.BlockSpec((tok, wide), lambda t, s: (0, 0))
    return pl.pallas_call(
        mlp_kernel,
        grid_spec=pltpu.PrefetchScalarGridSpec(
            num_scalar_prefetch=1,
            grid=(units // tile,),
            in_specs=[
                pl.BlockSpec(memory_space=pltpu.SMEM),
                whole,
                pl.BlockSpec((tok, wide), lambda t, s: (s[0], 0)),
                pl.BlockSpec((1, wide), lambda t, s: (0, 0)),
                pl.BlockSpec((wide, tile), lambda t, s: (0, t)),
                pl.BlockSpec((wide, tile), lambda t, s: (0, t)),
                pl.BlockSpec((tile, wide), lambda t, s: (t, 0)),
            ],
            out_specs=[
                whole,
                whole,
                pl.BlockSpec((tok, tile), lambda t, s: (0, t)),
                pl.BlockSpec((2, tok, tile), lambda t, s: (0, 0, t)),
                whole,
            ],
            scratch_shapes=[pltpu.VMEM((tok, wide), BF16)],
        ),
        out_shape=[
            jax.ShapeDtypeStruct((tok, wide), F32),
            jax.ShapeDtypeStruct((tok, wide), F32),
            jax.ShapeDtypeStruct((tok, units), F32),
            jax.ShapeDtypeStruct((2, tok, units), F32),
            jax.ShapeDtypeStruct((tok, wide), BF16),
        ],
        compiler_params=pltpu.CompilerParams(vmem_limit_bytes=MLP_VMEM),
        cost_estimate=cost(S_mlp, 12 * tok * wide * units, 3 * wide * units * 2 + 5 * tok * wide * 4, tok * units),
        name="mlp",
    )(slot, live_rows, middle, cotangent, gain, w_gate, w_up, w_down)


def mlp_weight_kernel(own_ref, other_ref, *refs):
    rhs_refs, out_ref, lhs = refs[:4], refs[-2], refs[-1]
    tok = own_ref.shape[-1]

    @pl.when(pl.program_id(0) == 0)
    def _():
        lhs[:, :tok] = own_ref[...]
        lhs[:, tok:] = other_ref[...].astype(BF16)

    rhs = jnp.concatenate([ref[...].reshape(ref.shape[-2:]).astype(BF16) for ref in rhs_refs], axis=0)
    out_ref[...] = jnp.dot(lhs[...], rhs, preferred_element_type=F32)


def mlp_weight_grad(kind, own, other, acts, grads):
    tok, cols = acts[0].shape[-2:]
    tile = 1024
    per = cols // tile
    whole = pl.BlockSpec(own.shape, lambda j: (0, 0))
    if acts[0].ndim == 2:
        columns = pl.BlockSpec((tok, tile), lambda j: (0, j))
    else:
        columns = pl.BlockSpec((1, tok, tile), lambda j: (kind - 1, 0, j))
    aliased = () if grads is None else (grads,)
    return pl.pallas_call(
        mlp_weight_kernel,
        grid=(per,),
        in_specs=[whole] * 2 + [columns] * 4 + [pl.BlockSpec(memory_space=pl.ANY)] * len(aliased),
        out_specs=pl.BlockSpec((1024, tile), lambda j: (0, kind * per + j)),
        scratch_shapes=[pltpu.VMEM((1024, 4 * tok), BF16)],
        out_shape=jax.ShapeDtypeStruct((1024, 3 * cols), F32),
        compiler_params=pltpu.CompilerParams(vmem_limit_bytes=WEIGHT_VMEM),
        cost_estimate=cost(S_mlp_weight_grad, 2 * 1024 * 4 * tok * cols, (1024 + 4 * tok) * cols * 4),
        input_output_aliases={6: 0} if aliased else {},
        name="mlp_weight_grad",
    )(own, other, *acts, *aliased)


def tokens_kernel(slot_ref, grad_ref, mid_ref, x_ref, gain_ref, *refs):
    out_ref, gain_out_ref = refs[-2:]
    grad = grad_ref[...]
    x = x_ref[...].astype(F32)
    inverse = lax.rsqrt(jnp.mean(x * x, axis=-1, keepdims=True) + EPS)
    unit = x * inverse
    scaled = grad * gain_ref[...].astype(F32)
    out_ref[...] = mid_ref[...] + inverse * (scaled - unit * jnp.mean(scaled * unit, axis=-1, keepdims=True))
    gain_part = jnp.sum(grad * unit, axis=0, keepdims=True)

    @pl.when(pl.program_id(0) == 0)
    def _():
        gain_out_ref[...] = gain_part

    @pl.when(pl.program_id(0) > 0)
    def _():
        gain_out_ref[...] += gain_part


def tokens_slot(slot, grad, grad_mid, tokens, gain, whole):
    tok, wide = grad.shape
    parts = 2
    tile = tok // parts
    aliased = () if whole is None else (whole,)
    rows = pl.BlockSpec((tile, wide), lambda j, s: (j, 0))
    in_whole = pl.BlockSpec((tile, wide), lambda j, s: (s[0] * parts + j, 0))
    line = pl.BlockSpec((1, wide), lambda j, s: (0, 0))
    return pl.pallas_call(
        tokens_kernel,
        grid_spec=pltpu.PrefetchScalarGridSpec(
            num_scalar_prefetch=1,
            grid=(parts,),
            in_specs=[rows, rows, in_whole, line] + [pl.BlockSpec(memory_space=pl.ANY)] * len(aliased),
            out_specs=[in_whole, line],
        ),
        out_shape=[jax.ShapeDtypeStruct((2 * tok, wide), F32), jax.ShapeDtypeStruct((1, wide), F32)],
        input_output_aliases={5: 0} if aliased else {},
        compiler_params=pltpu.CompilerParams(vmem_limit_bytes=SMALL_VMEM),
        cost_estimate=cost(S_tk if whole is None else S_tn, 10 * tok * wide, 14 * tok * wide),
        name="grad_tokens",
    )(slot, grad, grad_mid, tokens, gain, *aliased)


def layer_kernel(slot_ref, live_ref, middle_ref, sum_ref, *refs):
    refs[-1][...] = (live_flag(slot_ref, live_ref) * (middle_ref[...] + sum_ref[...])).astype(BF16)


def layer_slot(slot, live_rows, middle, added, whole):
    tok, wide = middle.shape
    parts = 2
    tile = tok // parts
    aliased = () if whole is None else (whole,)
    rows = pl.BlockSpec((tile, wide), lambda j, s: (j, 0))
    return pl.pallas_call(
        layer_kernel,
        grid_spec=pltpu.PrefetchScalarGridSpec(
            num_scalar_prefetch=1,
            grid=(parts,),
            in_specs=[pl.BlockSpec(memory_space=pltpu.SMEM), rows, rows]
            + [pl.BlockSpec(memory_space=pl.ANY)] * len(aliased),
            out_specs=pl.BlockSpec((tile, wide), lambda j, s: (s[0] * parts + j, 0)),
        ),
        out_shape=jax.ShapeDtypeStruct((2 * tok, wide), BF16),
        input_output_aliases={4: 0} if aliased else {},
        compiler_params=pltpu.CompilerParams(vmem_limit_bytes=SMALL_VMEM),
        cost_estimate=cost(S_lk if whole is None else S_ln, 2 * tok * wide, 10 * tok * wide),
        name="layer_out",
    )(slot, live_rows, middle, added, *aliased)


def weight_kernel(order_ref, own_ref, other_ref, k_ref, n_ref, k_other_ref, n_other_ref, *refs):
    send_ref, keep_ref, lhs = refs[-3:]
    tok = own_ref.shape[-1]
    cols = k_ref.shape[-1]
    for place in range(16):
        chip = pl.multiple_of(order_ref[place] * 64, 64)
        lhs[pl.ds(place * 64, 64), :tok] = own_ref[pl.ds(chip, 64), :]
        lhs[pl.ds(place * 64, 64), tok:] = other_ref[pl.ds(chip, 64), :].astype(BF16)
        if len(refs) > 3:
            half = (send_ref, keep_ref)[place // 8]
            half[pl.ds(place % 8 * 64, 64), cols:] = refs[0][pl.ds(chip, 64), :]
    rhs = jnp.concatenate([ref[0].astype(BF16) for ref in (k_ref, n_ref, k_other_ref, n_other_ref)], axis=0)
    send_ref[:, :cols] = jnp.dot(lhs[:512], rhs, preferred_element_type=F32)
    keep_ref[:, :cols] = jnp.dot(lhs[512:], rhs, preferred_element_type=F32)


def weight_grad(order, own, other, here, there, extra=()):
    _, tok, cols = here.shape
    wide = cols + sum(e.shape[1] for e in extra)

    def whole(array):
        return pl.BlockSpec(array.shape, lambda j, o: (0, 0))

    first = pl.BlockSpec((1, tok, cols), lambda j, o: (0, 0, 0))
    second = pl.BlockSpec((1, tok, cols), lambda j, o: (1, 0, 0))
    return pl.pallas_call(
        weight_kernel,
        grid_spec=pltpu.PrefetchScalarGridSpec(
            num_scalar_prefetch=1,
            grid=(1,),
            in_specs=[whole(own), whole(other), first, second, first, second] + [whole(e) for e in extra],
            out_specs=[pl.BlockSpec((512, wide), lambda j, o: (0, 0))] * 2,
            scratch_shapes=[pltpu.VMEM((1024, 4 * tok), BF16)],
        ),
        out_shape=[jax.ShapeDtypeStruct((512, wide), F32)] * 2,
        compiler_params=pltpu.CompilerParams(vmem_limit_bytes=WEIGHT_VMEM),
        cost_estimate=cost(S_weight_grad, 2 * 1024 * 4 * tok * cols, (1024 + 4 * tok) * wide * 4 + 1024 * tok * 12),
        name="weight_grad",
    )(order, own, other, here, here, there, there, *extra)


PLANES = [[chip * 2 + core for chip in range(16)] for core in range(2)]


def plane_sum(array):
    return lax.psum_scatter(array, "dp", scatter_dimension=0, axis_index_groups=PLANES, tiled=True)


class Piece:
    def __init__(self, stream, send, keep):
        self.perms, self.send, self.keep, self.step = STREAMS[stream], send, keep, 0

    def exchange(self):
        got = swap(self.send, self.perms[self.step])
        self.step += 1
        rows = self.keep.shape[0] // 2
        if self.step == 4:
            self.keep = self.keep + got
        else:
            self.send, self.keep = self.keep[:rows] + got[:rows], self.keep[rows:] + got[rows:]
        return got


def hold(value, pieces, when=True):
    if not when:
        return value
    value, *sends = tie(value, *[p.send for p in pieces])
    for p, send in zip(pieces, sends):
        p.send = send
    return value


def tie(*arrays):
    return lax.optimization_barrier(arrays)


def on_device(
    tokens,
    norm1_gain,
    w_query,
    w_key,
    w_value,
    w_output,
    norm2_gain,
    w_gate,
    w_up,
    w_down,
    cotangent,
    first_len,
    live_rows,
):
    dp = lax.axis_index("dp")
    y = lax.axis_index("tensor")
    z, x, c = dp // 8, (dp // 2) % 4, dp % 2
    slot = jnp.where(c == 0, low_bit(y), high_bit(y))
    orders = [block_order(s, z, x, c).astype(jnp.int32) for s in range(2)]
    tok, wide = tokens.shape
    gain_one = norm1_gain[None]
    gain_two = norm2_gain[None]
    tables = turn_tables(tok // 2)
    slot_k = jnp.reshape(slot, (1,)).astype(jnp.int32)
    slot_n = 1 - slot_k
    core = jnp.reshape(c, (1,)).astype(jnp.int32)
    plain = jnp.concatenate([core, jnp.array([0, 0, 1, 1], jnp.int32)])
    live = [(s < live_rows).astype(jnp.int32) for s in (slot_k, slot_n)]
    masked = jnp.concatenate([core, slot_k, slot_n, *live])

    weights = (w_query, w_key, w_value, w_output)
    part_n, one_n, attended, kept_n = attend(1, slot_n, first_len, tokens, gain_one, tables, None, *weights)
    got = swap(part_n, ALONG_Y[0])
    part_k, one_k, attended, kept_k = attend(0, slot_k, first_len, tokens, gain_one, tables, attended, *weights)
    if B1:
        masked, plain, part_k = tie(masked, plain, part_k)
    half = part_k + got
    x_k = lax.dynamic_slice_in_dim(tokens, slot * (tok // 2), tok // 2, 0).astype(F32)
    middle_k = x_k + half + swap(half, ALONG_Y[1])
    dy_own, dy_other = by_block(masked, cotangent, cotangent)
    dy_other = swap(dy_other, OTHER_CORE)
    one_own, one_other = by_block(plain, one_k, one_n)
    one_other = swap(one_other, OTHER_CORE)
    attended_other = swap(attended, OTHER_CORE)
    if B2:
        middle_k, dy_other, one_other, attended_other = tie(middle_k, dy_other, one_other, attended_other)

    feed = (w_gate, w_up, w_down)
    middle_n = swap(middle_k, ALONG_Y[0])
    out_k, back_k, hidden_k, act_k, two_k = mlp(slot_k, live_rows, middle_k, cotangent, gain_two, *feed)
    got = swap(back_k, ALONG_Y[0])
    hidden_k_other = swap(hidden_k, OTHER_CORE)
    act_k_other = swap(act_k, OTHER_CORE)
    slot_n, out_k = tie(slot_n, out_k)
    out_n, back_n, hidden_n, act_n, two_n = mlp(slot_n, live_rows, middle_n, cotangent, gain_two, *feed)
    hidden_n_other = swap(hidden_n, OTHER_CORE)
    act_n_other = swap(act_n, OTHER_CORE)
    two_own, two_other = by_block(plain, two_k, two_n)
    two_other = swap(two_other, OTHER_CORE)

    half = back_n + got
    if B4:
        half, dy_own = tie(half, dy_own)
    got = swap(half, ALONG_Y[1])

    grads = mlp_weight_grad(0, dy_own, dy_other, (hidden_k, hidden_n, hidden_k_other, hidden_n_other), None)
    acts = (act_k, act_n, act_k_other, act_n_other)
    grads = mlp_weight_grad(1, two_own, two_other, acts, grads)
    if H2:
        grads, got = tie(grads, got)
    grads = mlp_weight_grad(2, two_own, two_other, acts, grads)
    slot_b = slot_n
    if B5:
        slot_b, grads = tie(slot_b, grads)
    grad_2n = half + got
    if H1:
        grad_2n, grads = tie(grad_2n, grads)
    grads = plane_sum(grads)

    grad_2k = swap(grad_2n, ALONG_Y[0])
    back_n, grad_mid_n, dm_n, lin, gain_2 = attend_back(
        1, slot_b, first_len, live_rows, (half, got), middle_n, cotangent, gain_two, kept_n, tables, None, *weights
    )
    if D1:
        out_n, back_n = tie(out_n, back_n)
    got = swap(back_n, ALONG_Y[0])
    slot_b = slot_k
    back_k, grad_mid_k, dm_k, lin, _ = attend_back(
        0, slot_b, first_len, live_rows, (grad_2k,), middle_k, cotangent, gain_two, kept_k, tables, lin, *weights
    )
    if E3:
        out_n, back_k = tie(out_n, back_k)
    out_got = swap(out_n, ALONG_Y[0])
    lin_other = swap(lin, OTHER_CORE)
    dm_own, dm_other = by_block(plain, dm_k, dm_n)
    order_0 = orders[0]
    if G1:
        order_0, got = tie(order_0, got)
    dm_other = swap(dm_other, OTHER_CORE)
    lin_grad = weight_grad(order_0, one_own, one_other, lin, lin_other)
    out_grad = weight_grad(orders[1], dm_own, dm_other, attended, attended_other)
    three = [Piece(0, *lin_grad), Piece(1, *out_grad)]
    back_k = hold(back_k, three, B7)
    half = back_k + got
    grad_1k = half + swap(half, ALONG_Y[1])
    out_half = out_k + out_got
    for p in three:
        p.exchange()
    if G2:
        grad_1k = hold(grad_1k, three)
    if G4:
        out_half = hold(out_half, three)
    out_sum = out_half + swap(out_half, ALONG_Y[1])
    out_other = swap(out_sum, ALONG_Y[0])
    out_kept = out_sum
    for p in three:
        p.exchange()

    grad_1n = swap(grad_1k, ALONG_Y[0])
    if G3:
        grad_1n = hold(grad_1n, three)
    if G5:
        out_kept = hold(out_sum, three)
    slot_t = slot_k
    grad_tokens, gain_1 = tokens_slot(slot_t, grad_1k, grad_mid_k, tokens, gain_one, None)

    gains = jnp.concatenate([gain_1, gain_2], axis=0)
    gains = gains + swap(gains, ALONG_Y[0])
    gains = jnp.transpose(gains.reshape(2, 16, 2, 64), (2, 1, 0, 3)).reshape(2, 16, 128)
    mine = lax.dynamic_index_in_dim(gains, c, keepdims=False)
    theirs = lax.dynamic_index_in_dim(gains, 1 - c, keepdims=False)
    mine = mine + swap(theirs, OTHER_CORE)
    picks = orders[0][:, None] == jnp.arange(16, dtype=jnp.int32)[None, :]
    mine = jnp.sum(jnp.where(picks[:, :, None], mine[None], 0.0), axis=1)
    for perm in STREAMS[0][:2]:
        rows = mine.shape[0] // 2
        mine = mine[rows:] + swap(mine[:rows], perm)
    mine = hold(mine, three, D8)
    for perm in STREAMS[0][2:]:
        rows = mine.shape[0] // 2
        mine = mine[rows:] + swap(mine[:rows], perm)
    for p in three:
        p.exchange()
    if H3:
        out_other = hold(out_other, three)
    for p in three:
        if p.step < 4:
            p.exchange()
    query_key_value, output = [p.keep for p in three]

    layer_out = layer_slot(slot_k, live_rows, middle_k, out_kept, None)
    layer_out = layer_slot(slot_n, live_rows, middle_n, out_other, layer_out)
    grad_tokens, _ = tokens_slot(slot_n, grad_1n, grad_mid_n, tokens, gain_one, grad_tokens)

    return (
        layer_out,
        grad_tokens,
        mine[0, :64],
        query_key_value[:, :512],
        query_key_value[:, 512:640],
        query_key_value[:, 640:],
        jnp.transpose(output),
        mine[0, 64:],
        grads[:, 2048:4096],
        grads[:, 4096:],
        jnp.transpose(grads[:, :2048]),
    )


def solution(mesh):
    placed = (
        P("dp", None),
        P(),
        P(None, "tensor"),
        P(None, "tensor"),
        P(None, "tensor"),
        P("tensor", None),
        P(),
        P(None, "tensor"),
        P(None, "tensor"),
        P("tensor", None),
        P("dp", None),
        P("dp"),
        P("dp"),
    )
    return jax.shard_map(
        on_device,
        mesh=mesh,
        in_specs=placed,
        out_specs=(
            P("dp", None),
            P("dp", None),
            P("dp"),
            P("dp", "tensor"),
            P("dp", "tensor"),
            P("dp", "tensor"),
            P("tensor", "dp"),
            P("dp"),
            P("dp", "tensor"),
            P("dp", "tensor"),
            P("tensor", "dp"),
        ),
        check_vma=False,
    )
```

```python
import functools
import math

import jax
import jax.numpy as jnp
import numpy as np
from jax import lax
from jax.experimental import pallas as pl
from jax.experimental.pallas import tpu as pltpu
from jax.sharding import PartitionSpec as P

HEAD_DIM = 64
B2 = True
B4 = False
B5 = False
B7 = False
D1 = False
D8 = True
H3 = True
G1 = False
G2 = False
G3 = True
G4 = False
G5 = True
E3 = False
B1 = True
S_attend = 0.5
S_attend_back = 10.0
S_mlp = 2.5
S_mlp_weight_grad = 1.0
S_weight_grad = 2.5
S_by_block = 2.5
S_tk = 2.5
S_tn = 0.2
S_lk = 10.0
S_ln = 5.0
THETA = 500000.0
EPS = 1e-05
NEGATIVE = -1e30
F32 = jnp.float32
BF16 = jnp.bfloat16
ATTEND_VMEM = 58 * 1024 * 1024
MLP_VMEM = 58 * 1024 * 1024
WEIGHT_VMEM = 58 * 1024 * 1024
SMALL_VMEM = 58 * 1024 * 1024
AXES = ("dp", "tensor")


def pair_low(i):
    return i ^ 1


def pair_high(i):
    return 3 - i


def low_bit(v):
    return (v ^ (v >> 1)) & 1


def high_bit(v):
    return v >> 1


def from_bits(low, high):
    return jnp.where(high == 0, low, 3 - low)


def device_perm(move):
    pairs = []
    for dp in range(32):
        for y in range(4):
            z2, x2, c2, y2 = move(dp // 8, (dp // 2) % 4, dp % 2, y)
            pairs.append((dp * 4 + y, ((z2 * 4 + x2) * 2 + c2) * 4 + y2))
    return pairs


def first_pair(c, i):
    return pair_low(i) if c == 0 else pair_high(i)


def second_pair(c, i):
    return pair_high(i) if c == 0 else pair_low(i)


ALONG_Y = (
    device_perm(lambda z, x, c, y: (z, x, c, first_pair(c, y))),
    device_perm(lambda z, x, c, y: (z, x, c, second_pair(c, y))),
)
ALONG_X = (
    device_perm(lambda z, x, c, y: (z, first_pair(c, x), c, y)),
    device_perm(lambda z, x, c, y: (z, second_pair(c, x), c, y)),
)
ALONG_Z = (
    device_perm(lambda z, x, c, y: (first_pair(c, z), x, c, y)),
    device_perm(lambda z, x, c, y: (second_pair(c, z), x, c, y)),
)
OTHER_CORE = device_perm(lambda z, x, c, y: (z, x, 1 - c, y))
STREAMS = (ALONG_X + ALONG_Z, ALONG_Z + ALONG_X)


def swap(array, perm):
    return lax.ppermute(array, AXES, perm)


def block_order(stream, z, x, c):
    place = jnp.arange(16, dtype=jnp.int32)
    keep = [(place >> (3 - k)) & 1 for k in range(4)]

    def target(v, first, second):
        low = low_bit(v) ^ (1 - jnp.where(c == 0, first, second))
        high = high_bit(v) ^ (1 - jnp.where(c == 0, second, first))
        return from_bits(low, high)

    if stream == 0:
        return target(z, keep[2], keep[3]) * 4 + target(x, keep[0], keep[1])
    return target(z, keep[0], keep[1]) * 4 + target(x, keep[2], keep[3])


def turn_tables(tok):
    half = HEAD_DIM // 2
    freq = np.exp(np.arange(half) * (-2.0 * math.log(THETA) / HEAD_DIM))
    turned = np.arange(tok)[:, None] * freq[None, :]
    cosine, sine = np.cos(turned), np.sin(turned)
    return (
        jnp.asarray(np.tile(cosine, (1, 4)), F32),
        jnp.asarray(np.concatenate([-sine, sine, -sine, sine], axis=1), F32),
    )


def cost(scale, flops, moved, transcendentals=0):
    return pl.CostEstimate(flops=int(flops * scale), bytes_accessed=int(moved * scale), transcendentals=int(transcendentals * scale))


def times_transpose(left, right):
    return lax.dot_general(left, right, (((1,), (1,)), ((), ())), preferred_element_type=F32)


def contract_rows(left, right):
    return lax.dot_general(left, right, (((0,), (0,)), ((), ())), preferred_element_type=F32)


def turn(vectors, cosine, sine):
    lane = lax.broadcasted_iota(jnp.int32, vectors.shape, 1)
    ahead = pltpu.roll(vectors, 96, 1)
    behind = pltpu.roll(vectors, 32, 1)
    return vectors * cosine + jnp.where(lane % 64 < 32, ahead, behind) * sine


def row_turns(first, cos_ref, sin_ref):
    place = lax.broadcasted_iota(jnp.int32, cos_ref.shape, 0)
    return [jnp.where(place >= first, pltpu.roll(ref[...], first, 0), ref[...]) for ref in (cos_ref, sin_ref)]


def allowed_pairs(first, tok, group):
    query = lax.broadcasted_iota(jnp.int32, (group * tok, tok), 0) % tok
    key = lax.broadcasted_iota(jnp.int32, (group * tok, tok), 1)
    same = jnp.logical_not(jnp.logical_xor(query >= first, key >= first))
    return jnp.logical_and(same, key <= query)


def softmax_rows(queries, keys, allowed):
    raw = times_transpose(queries, keys) * HEAD_DIM**-0.5
    scores = jnp.where(allowed, raw, NEGATIVE)
    terms = jnp.exp(scores - jnp.max(scores, axis=-1, keepdims=True))
    return terms / jnp.sum(terms, axis=-1, keepdims=True)


def head_rows(array, head, count):
    return jnp.concatenate(
        [array[:, (head + k) * HEAD_DIM : (head + k + 1) * HEAD_DIM] for k in range(count)], axis=0
    )


def attend_kernel(
    slot_ref, first_ref, x_ref, gain_ref, cos_ref, sin_ref, wq_hbm, wk_hbm, wv_hbm, wo_hbm, *refs
):
    part_ref, normed_ref, attended_ref, kept_ref, wq, wk, wv, wo, sems = refs[-9:]
    copies = [
        pltpu.make_async_copy(src, dst, sems.at[k])
        for k, (src, dst) in enumerate(((wq_hbm, wq), (wk_hbm, wk), (wv_hbm, wv), (wo_hbm, wo)))
    ]
    for copy in copies:
        copy.start()
    x = x_ref[...].astype(F32)
    inverse = lax.rsqrt(jnp.mean(x * x, axis=-1, keepdims=True) + EPS)
    normed = (x * inverse * gain_ref[...].astype(F32)).astype(BF16)
    normed_ref[...] = normed
    first = first_ref[slot_ref[0]]
    cosine, sine = row_turns(first, cos_ref, sin_ref)
    tok = x.shape[0]
    heads = wq.shape[1] // HEAD_DIM
    kv = wk.shape[1] // HEAD_DIM
    group = heads // kv
    copies[0].wait()
    lin = jnp.dot(normed, wq[...], preferred_element_type=F32)
    queries = jnp.concatenate(
        [turn(lin[:, k * 128 : (k + 1) * 128], cosine, sine).astype(BF16) for k in range(heads // 2)], axis=1
    )
    copies[1].wait()
    lin = jnp.dot(normed, wk[...], preferred_element_type=F32)
    keys = jnp.concatenate(
        [turn(lin[:, k * 128 : (k + 1) * 128], cosine, sine).astype(BF16) for k in range(kv // 2)], axis=1
    )
    copies[2].wait()
    values = jnp.dot(normed, wv[...], preferred_element_type=F32).astype(BF16)
    kept_ref[:, : heads * HEAD_DIM] = queries
    kept_ref[:, heads * HEAD_DIM : (heads + kv) * HEAD_DIM] = keys
    kept_ref[:, (heads + kv) * HEAD_DIM :] = values
    allowed = allowed_pairs(first, tok, group)
    mixed = []
    for k in range(kv):
        lanes = slice(k * HEAD_DIM, (k + 1) * HEAD_DIM)
        prob = softmax_rows(head_rows(queries, k * group, group), keys[:, lanes], allowed).astype(BF16)
        out = jnp.dot(prob, values[:, lanes], preferred_element_type=F32)
        mixed += [out[g * tok : (g + 1) * tok] for g in range(group)]
    attended = jnp.concatenate(mixed, axis=1).astype(BF16)
    attended_ref[0] = attended.astype(F32)
    copies[3].wait()
    part_ref[...] = jnp.dot(attended, wo[...], preferred_element_type=F32)


def attend(entry, slot, first_len, tokens, gain, tables, attended, w_query, w_key, w_value, w_output):
    tok, wide = tokens.shape[0] // 2, tokens.shape[1]
    cols = w_query.shape[1]
    kv_cols = w_key.shape[1]
    weights = (w_query, w_key, w_value, w_output)
    aliased = () if attended is None else (attended,)

    def whole(array):
        return pl.BlockSpec(array.shape, lambda j, s: (0,) * array.ndim)

    return pl.pallas_call(
        attend_kernel,
        grid_spec=pltpu.PrefetchScalarGridSpec(
            num_scalar_prefetch=1,
            grid=(1,),
            in_specs=[
                pl.BlockSpec(memory_space=pltpu.SMEM),
                pl.BlockSpec((tok, wide), lambda j, s: (s[0], 0)),
                whole(gain),
                whole(tables[0]),
                whole(tables[1]),
            ]
            + [pl.BlockSpec(memory_space=pl.ANY)] * (4 + len(aliased)),
            out_specs=[
                pl.BlockSpec((tok, wide), lambda j, s: (0, 0)),
                pl.BlockSpec((tok, wide), lambda j, s: (0, 0)),
                pl.BlockSpec((1, tok, cols), lambda j, s: (entry, 0, 0)),
                pl.BlockSpec((tok, cols + 2 * kv_cols), lambda j, s: (0, 0)),
            ],
            scratch_shapes=[pltpu.VMEM(w.shape, w.dtype) for w in weights] + [pltpu.SemaphoreType.DMA((4,))],
        ),
        out_shape=[
            jax.ShapeDtypeStruct((tok, wide), F32),
            jax.ShapeDtypeStruct((tok, wide), BF16),
            jax.ShapeDtypeStruct((2, tok, cols), F32),
            jax.ShapeDtypeStruct((tok, cols + 2 * kv_cols), BF16),
        ],
        input_output_aliases={10: 2} if aliased else {},
        compiler_params=pltpu.CompilerParams(vmem_limit_bytes=ATTEND_VMEM),
        cost_estimate=cost(S_attend,
            2 * tok * wide * (2 * cols + 2 * kv_cols) + 4 * tok * tok * cols,
            sum(w.size * 2 for w in weights) + tok * wide * 8,
            tok * tok * cols // HEAD_DIM,
        ),
        name="attend",
    )(slot, first_len, tokens, gain, *tables, *weights, *aliased)


def attend_back_kernel(
    slot_ref, first_ref, live_ref, grad_ref, more_ref, middle_ref, cot_ref, gain_ref, kept_ref, cos_ref, sin_ref,
    wq_hbm, wk_hbm, wv_hbm, wo_hbm, *refs
):
    part_ref, grad_mid_ref, dm_ref, lin_ref, gain_out_ref, wq, wk, wv, wo, sems = refs[-10:]
    copies = [
        pltpu.make_async_copy(src, dst, sems.at[k])
        for k, (src, dst) in enumerate(((wq_hbm, wq), (wk_hbm, wk), (wv_hbm, wv), (wo_hbm, wo)))
    ]
    for k in (3, 0, 1, 2):
        copies[k].start()
    grad = grad_ref[...]
    if more_ref is not None:
        grad = grad + more_ref[...]
    middle = middle_ref[...]
    inverse = lax.rsqrt(jnp.mean(middle * middle, axis=-1, keepdims=True) + EPS)
    unit = middle * inverse
    gain_out_ref[...] = jnp.sum(grad * unit, axis=0, keepdims=True)
    scaled = grad * gain_ref[...].astype(F32)
    grad_mid = cot_ref[...].astype(F32) * live_flag(slot_ref, live_ref) + inverse * (
        scaled - unit * jnp.mean(scaled * unit, axis=-1, keepdims=True)
    )
    grad_mid_ref[...] = grad_mid
    dm = grad_mid.astype(BF16)
    dm_ref[...] = dm
    tok = dm.shape[0]
    heads = wq.shape[1] // HEAD_DIM
    kv = wk.shape[1] // HEAD_DIM
    group = heads // kv
    first = first_ref[slot_ref[0]]
    cosine, sine = row_turns(first, cos_ref, sin_ref)
    sine = -sine
    allowed = allowed_pairs(first, tok, group)
    copies[3].wait()
    grad_att = times_transpose(dm, wo[...]).astype(BF16)
    grad_q, grad_k, grad_v = [], [], []
    scale = HEAD_DIM**-0.5
    for k in range(kv):
        q_rows = head_rows(kept_ref, k * group, group)
        keys = kept_ref[:, (heads + k) * HEAD_DIM : (heads + k + 1) * HEAD_DIM]
        values = kept_ref[:, (heads + kv + k) * HEAD_DIM : (heads + kv + k + 1) * HEAD_DIM]
        prob = softmax_rows(q_rows, keys, allowed)
        d_rows = head_rows(grad_att, k * group, group)
        grad_v.append(contract_rows(prob.astype(BF16), d_rows))
        grad_prob = times_transpose(d_rows, values)
        delta = jnp.sum(prob * grad_prob, axis=-1, keepdims=True)
        grad_score = (prob * (grad_prob - delta)).astype(BF16)
        rows = jnp.dot(grad_score, keys, preferred_element_type=F32) * scale
        grad_q += [rows[g * tok : (g + 1) * tok] for g in range(group)]
        grad_k.append(contract_rows(grad_score, q_rows) * scale)

    def turned_back(parts):
        pairs = [jnp.concatenate(parts[k : k + 2], axis=1) for k in range(0, len(parts), 2)]
        return jnp.concatenate([turn(p, cosine, sine).astype(BF16) for p in pairs], axis=1)

    lin_q = turned_back(grad_q)
    lin_k = turned_back(grad_k)
    lin_v = jnp.concatenate(grad_v, axis=1).astype(BF16)
    cols, kv_cols = heads * HEAD_DIM, kv * HEAD_DIM
    lin_ref[0, :, :cols] = lin_q.astype(F32)
    lin_ref[0, :, cols : cols + kv_cols] = lin_k.astype(F32)
    lin_ref[0, :, cols + kv_cols :] = lin_v.astype(F32)
    for k in range(3):
        copies[k].wait()
    part_ref[...] = (
        times_transpose(lin_q, wq[...]) + times_transpose(lin_k, wk[...]) + times_transpose(lin_v, wv[...])
    )


def attend_back(
    entry, slot, first_len, live_rows, grads, middle, cotangent, gain, kept, tables, lin, w_query, w_key, w_value, w_output
):
    tok, wide = middle.shape
    cols = w_query.shape[1]
    kv_cols = w_key.shape[1]
    weights = (w_query, w_key, w_value, w_output)
    aliased = () if lin is None else (lin,)
    rows = pl.BlockSpec((tok, wide), lambda j, s: (0, 0))

    def whole(array):
        return pl.BlockSpec(array.shape, lambda j, s: (0,) * array.ndim)

    def kernel(slot_ref, first_ref, live_ref, grad_ref, *refs):
        if len(grads) == 1:
            refs = (None, *refs)
        attend_back_kernel(slot_ref, first_ref, live_ref, grad_ref, *refs)

    return pl.pallas_call(
        kernel,
        grid_spec=pltpu.PrefetchScalarGridSpec(
            num_scalar_prefetch=1,
            grid=(1,),
            in_specs=[
                pl.BlockSpec(memory_space=pltpu.SMEM),
                pl.BlockSpec(memory_space=pltpu.SMEM),
                *[rows] * (len(grads) + 1),
                pl.BlockSpec((tok, wide), lambda j, s: (s[0], 0)),
                whole(gain),
                whole(kept),
                whole(tables[0]),
                whole(tables[1]),
            ]
            + [pl.BlockSpec(memory_space=pl.ANY)] * (4 + len(aliased)),
            out_specs=[
                rows,
                rows,
                rows,
                pl.BlockSpec((1, tok, cols + 2 * kv_cols), lambda j, s: (entry, 0, 0)),
                pl.BlockSpec((1, wide), lambda j, s: (0, 0)),
            ],
            scratch_shapes=[pltpu.VMEM(w.shape, w.dtype) for w in weights] + [pltpu.SemaphoreType.DMA((4,))],
        ),
        out_shape=[
            jax.ShapeDtypeStruct((tok, wide), F32),
            jax.ShapeDtypeStruct((tok, wide), F32),
            jax.ShapeDtypeStruct((tok, wide), BF16),
            jax.ShapeDtypeStruct((2, tok, cols + 2 * kv_cols), F32),
            jax.ShapeDtypeStruct((1, wide), F32),
        ],
        input_output_aliases={13 + len(grads): 3} if aliased else {},
        compiler_params=pltpu.CompilerParams(vmem_limit_bytes=ATTEND_VMEM),
        cost_estimate=cost(S_attend_back,
            2 * tok * wide * (2 * cols + 2 * kv_cols) + 10 * tok * tok * cols,
            sum(w.size * 2 for w in weights) + tok * wide * 24,
            tok * tok * cols // HEAD_DIM,
        ),
        name="attend_back",
    )(slot, first_len, live_rows, *grads, middle, cotangent, gain, kept, *tables, *weights, *aliased)


def blocks_kernel(core_ref, first_ref, second_ref, own_ref, other_ref):
    rows = [
        ref[...].astype(F32) * core_ref[3 + k].astype(F32) for k, ref in enumerate((first_ref, second_ref))
    ]
    rows = jnp.concatenate(rows, axis=0)
    core = core_ref[0]
    for k in range(rows.shape[1] // 128):
        turned = jnp.transpose(rows[:, k * 128 : (k + 1) * 128])
        low, high = turned[:64], turned[64:]
        own_ref[k * 64 : (k + 1) * 64, :] = jnp.where(core == 0, low, high).astype(BF16)
        other_ref[k * 64 : (k + 1) * 64, :] = jnp.where(core == 0, high, low)


def by_block(choice, first, second):
    tok = 192
    chips = 8
    return pl.pallas_call(
        blocks_kernel,
        grid_spec=pltpu.PrefetchScalarGridSpec(
            num_scalar_prefetch=1,
            grid=(16 // chips,),
            in_specs=[
                pl.BlockSpec((tok, 128 * chips), lambda j, o: (o[1], j)),
                pl.BlockSpec((tok, 128 * chips), lambda j, o: (o[2], j)),
            ],
            out_specs=[pl.BlockSpec((64 * chips, 2 * tok), lambda j, o: (j, 0))] * 2,
        ),
        out_shape=[
            jax.ShapeDtypeStruct((1024, 2 * tok), BF16),
            jax.ShapeDtypeStruct((1024, 2 * tok), F32),
        ],
        compiler_params=pltpu.CompilerParams(vmem_limit_bytes=SMALL_VMEM),
        cost_estimate=cost(S_by_block, 0, 2048 * tok * 10),
        name="by_block",
    )(choice, first, second)


def live_flag(slot_ref, live_ref):
    return jnp.where(slot_ref[0] < live_ref[0], 1.0, 0.0)


def mlp_kernel(
    slot_ref, live_ref, middle_ref, cot_ref, gain_ref, wg_ref, wu_ref, wd_ref, *refs
):
    hidden_ref, act_ref, normed_ref, dy = refs[-4:]
    step = pl.program_id(0)

    @pl.when(step == 0)
    def _():
        middle = middle_ref[...]
        inverse = lax.rsqrt(jnp.mean(middle * middle, axis=-1, keepdims=True) + EPS)
        normed_ref[...] = (middle * inverse * gain_ref[...].astype(F32)).astype(BF16)
        dy[...] = (cot_ref[...].astype(F32) * live_flag(slot_ref, live_ref)).astype(BF16)

    n = normed_ref[...]
    w_gate = wg_ref[...]
    w_up = wu_ref[...]
    w_down = wd_ref[...]
    gate = jnp.dot(n, w_gate, preferred_element_type=F32)
    up = jnp.dot(n, w_up, preferred_element_type=F32)
    grad_hidden = times_transpose(dy[...], w_down)
    sig = 1.0 / (1.0 + jnp.exp(-gate))
    silu = gate * sig
    hidden = (silu * up).astype(BF16)
    d_gate = (grad_hidden * up * sig * (1.0 + gate * (1.0 - sig))).astype(BF16)
    d_up = (grad_hidden * silu).astype(BF16)
    hidden_ref[...] = hidden.astype(F32)
    act_ref[0] = d_gate.astype(F32)
    act_ref[1] = d_up.astype(F32)
    if len(refs) == 4:
        return
    out_ref, grad_ref = refs[:2]
    out_part = jnp.dot(hidden, w_down, preferred_element_type=F32)
    grad_part = times_transpose(d_gate, w_gate) + times_transpose(d_up, w_up)

    @pl.when(step == 0)
    def _():
        out_ref[...] = out_part
        grad_ref[...] = grad_part

    @pl.when(step > 0)
    def _():
        out_ref[...] += out_part
        grad_ref[...] += grad_part


def mlp(slot, live_rows, middle, cotangent, gain, w_gate, w_up, w_down, sums):
    tok, wide = middle.shape
    units = w_gate.shape[1]
    tile = 512
    whole = pl.BlockSpec((tok, wide), lambda t, s: (0, 0))
    return pl.pallas_call(
        mlp_kernel,
        grid_spec=pltpu.PrefetchScalarGridSpec(
            num_scalar_prefetch=1,
            grid=(units // tile,),
            in_specs=[
                pl.BlockSpec(memory_space=pltpu.SMEM),
                whole,
                pl.BlockSpec((tok, wide), lambda t, s: (s[0], 0)),
                pl.BlockSpec((1, wide), lambda t, s: (0, 0)),
                pl.BlockSpec((wide, tile), lambda t, s: (0, t)),
                pl.BlockSpec((wide, tile), lambda t, s: (0, t)),
                pl.BlockSpec((tile, wide), lambda t, s: (t, 0)),
            ],
            out_specs=[whole] * (2 * sums)
            + [
                pl.BlockSpec((tok, tile), lambda t, s: (0, t)),
                pl.BlockSpec((2, tok, tile), lambda t, s: (0, 0, t)),
                whole,
            ],
            scratch_shapes=[pltpu.VMEM((tok, wide), BF16)],
        ),
        out_shape=[jax.ShapeDtypeStruct((tok, wide), F32)] * (2 * sums)
        + [
            jax.ShapeDtypeStruct((tok, units), F32),
            jax.ShapeDtypeStruct((2, tok, units), F32),
            jax.ShapeDtypeStruct((tok, wide), BF16),
        ],
        compiler_params=pltpu.CompilerParams(vmem_limit_bytes=MLP_VMEM),
        cost_estimate=cost(S_mlp, 12 * tok * wide * units, 3 * wide * units * 2 + 5 * tok * wide * 4, tok * units),
        name="mlp",
    )(slot, live_rows, middle, cotangent, gain, w_gate, w_up, w_down)


def normed_grad_kernel(gate_ref, up_ref, wg_ref, wu_ref, out_ref):
    part = times_transpose(gate_ref[0].astype(BF16), wg_ref[...])
    part += times_transpose(up_ref[0].astype(BF16), wu_ref[...])

    @pl.when(pl.program_id(0) == 0)
    def _():
        out_ref[...] = part

    @pl.when(pl.program_id(0) > 0)
    def _():
        out_ref[...] += part


def normed_grad(act, w_gate, w_up):
    _, tok, units = act.shape
    wide = w_gate.shape[0]
    tile = 512
    return pl.pallas_call(
        normed_grad_kernel,
        grid=(units // tile,),
        in_specs=[
            pl.BlockSpec((1, tok, tile), lambda t: (0, 0, t)),
            pl.BlockSpec((1, tok, tile), lambda t: (1, 0, t)),
            pl.BlockSpec((wide, tile), lambda t: (0, t)),
            pl.BlockSpec((wide, tile), lambda t: (0, t)),
        ],
        out_specs=pl.BlockSpec((tok, wide), lambda t: (0, 0)),
        out_shape=jax.ShapeDtypeStruct((tok, wide), F32),
        compiler_params=pltpu.CompilerParams(vmem_limit_bytes=MLP_VMEM),
        cost_estimate=cost(S_mlp, 4 * tok * wide * units, 2 * wide * units * 2 + 3 * tok * wide * 4),
        name="normed_grad",
    )(act, act, w_gate, w_up)


def layer_part_kernel(hidden_ref, wd_ref, out_ref):
    out_ref[...] = jnp.dot(hidden_ref[...].astype(BF16), wd_ref[...], preferred_element_type=F32)


def layer_part(hidden, w_down):
    tok, units = hidden.shape
    wide = w_down.shape[1]
    tile = 512
    return pl.pallas_call(
        layer_part_kernel,
        grid=(wide // tile,),
        in_specs=[
            pl.BlockSpec((tok, units), lambda t: (0, 0)),
            pl.BlockSpec((units, tile), lambda t: (0, t)),
        ],
        out_specs=pl.BlockSpec((tok, tile), lambda t: (0, t)),
        out_shape=jax.ShapeDtypeStruct((tok, wide), F32),
        compiler_params=pltpu.CompilerParams(vmem_limit_bytes=MLP_VMEM),
        cost_estimate=cost(S_mlp, 2 * tok * wide * units, wide * units * 2 + 2 * tok * wide * 4),
        name="layer_part",
    )(hidden, w_down)


def mlp_weight_kernel(dy_own, dy_other, two_own, two_other, *refs):
    hidden_refs, act_refs, out_ref, lhs = refs[:4], refs[4:8], refs[8], refs[9]
    tok = dy_own.shape[-1]
    step = pl.program_id(0)

    def product(own, other, rhs_refs, first):
        @pl.when(first)
        def _():
            lhs[:, :tok] = own[...]
            lhs[:, tok:] = other[...].astype(BF16)

        rhs = jnp.concatenate([ref[...].reshape(ref.shape[-2:]).astype(BF16) for ref in rhs_refs], axis=0)
        out_ref[...] = jnp.dot(lhs[...], rhs, preferred_element_type=F32)

    @pl.when(step < 2)
    def _():
        product(dy_own, dy_other, hidden_refs, step == 0)

    @pl.when(step >= 2)
    def _():
        product(two_own, two_other, act_refs, step == 2)


def mlp_weight_grad(dy_own, dy_other, two_own, two_other, hidden, acts):
    kinds, tok, cols = acts[0].shape
    tile = cols // 2
    whole = pl.BlockSpec(dy_own.shape, lambda j: (0, 0))

    def act_at(j):
        k = jnp.maximum(j - 2, 0)
        return (k // 2, 0, k % 2)

    return pl.pallas_call(
        mlp_weight_kernel,
        grid=(2 + 2 * kinds,),
        in_specs=[whole] * 4
        + [pl.BlockSpec((tok, tile), lambda j: (0, jnp.minimum(j, 1)))] * 4
        + [pl.BlockSpec((1, tok, tile), act_at)] * 4,
        out_specs=pl.BlockSpec((1024, tile), lambda j: (0, j)),
        scratch_shapes=[pltpu.VMEM((1024, 4 * tok), BF16)],
        out_shape=jax.ShapeDtypeStruct((1024, (2 + 2 * kinds) * tile), F32),
        compiler_params=pltpu.CompilerParams(vmem_limit_bytes=WEIGHT_VMEM),
        cost_estimate=cost(S_mlp_weight_grad, 2 * 1024 * 4 * tok * 6 * tile, (1024 + 4 * tok) * 6 * tile * 4),
        name="mlp_weight_grad",
    )(dy_own, dy_other, two_own, two_other, *hidden, *acts)


def tokens_kernel(slot_ref, grad_ref, mid_ref, x_ref, gain_ref, *refs):
    out_ref, gain_out_ref = refs[-2:]
    grad = grad_ref[...]
    x = x_ref[...].astype(F32)
    inverse = lax.rsqrt(jnp.mean(x * x, axis=-1, keepdims=True) + EPS)
    unit = x * inverse
    scaled = grad * gain_ref[...].astype(F32)
    out_ref[...] = mid_ref[...] + inverse * (scaled - unit * jnp.mean(scaled * unit, axis=-1, keepdims=True))
    gain_part = jnp.sum(grad * unit, axis=0, keepdims=True)

    @pl.when(pl.program_id(0) == 0)
    def _():
        gain_out_ref[...] = gain_part

    @pl.when(pl.program_id(0) > 0)
    def _():
        gain_out_ref[...] += gain_part


def tokens_slot(slot, grad, grad_mid, tokens, gain, whole):
    tok, wide = grad.shape
    parts = 2
    tile = tok // parts
    aliased = () if whole is None else (whole,)
    rows = pl.BlockSpec((tile, wide), lambda j, s: (j, 0))
    in_whole = pl.BlockSpec((tile, wide), lambda j, s: (s[0] * parts + j, 0))
    line = pl.BlockSpec((1, wide), lambda j, s: (0, 0))
    return pl.pallas_call(
        tokens_kernel,
        grid_spec=pltpu.PrefetchScalarGridSpec(
            num_scalar_prefetch=1,
            grid=(parts,),
            in_specs=[rows, rows, in_whole, line] + [pl.BlockSpec(memory_space=pl.ANY)] * len(aliased),
            out_specs=[in_whole, line],
        ),
        out_shape=[jax.ShapeDtypeStruct((2 * tok, wide), F32), jax.ShapeDtypeStruct((1, wide), F32)],
        input_output_aliases={5: 0} if aliased else {},
        compiler_params=pltpu.CompilerParams(vmem_limit_bytes=SMALL_VMEM),
        cost_estimate=cost(S_tk if whole is None else S_tn, 10 * tok * wide, 14 * tok * wide),
        name="grad_tokens",
    )(slot, grad, grad_mid, tokens, gain, *aliased)


def layer_kernel(slot_ref, live_ref, middle_ref, sum_ref, *refs):
    refs[-1][...] = (live_flag(slot_ref, live_ref) * (middle_ref[...] + sum_ref[...])).astype(BF16)


def layer_slot(slot, live_rows, middle, added, whole):
    tok, wide = middle.shape
    parts = 2
    tile = tok // parts
    aliased = () if whole is None else (whole,)
    rows = pl.BlockSpec((tile, wide), lambda j, s: (j, 0))
    return pl.pallas_call(
        layer_kernel,
        grid_spec=pltpu.PrefetchScalarGridSpec(
            num_scalar_prefetch=1,
            grid=(parts,),
            in_specs=[pl.BlockSpec(memory_space=pltpu.SMEM), rows, rows]
            + [pl.BlockSpec(memory_space=pl.ANY)] * len(aliased),
            out_specs=pl.BlockSpec((tile, wide), lambda j, s: (s[0] * parts + j, 0)),
        ),
        out_shape=jax.ShapeDtypeStruct((2 * tok, wide), BF16),
        input_output_aliases={4: 0} if aliased else {},
        compiler_params=pltpu.CompilerParams(vmem_limit_bytes=SMALL_VMEM),
        cost_estimate=cost(S_lk if whole is None else S_ln, 2 * tok * wide, 10 * tok * wide),
        name="layer_out",
    )(slot, live_rows, middle, added, *aliased)


def weight_kernel(order_ref, own_ref, other_ref, k_ref, n_ref, k_other_ref, n_other_ref, *refs):
    send_ref, keep_ref, lhs = refs[-3:]
    tok = own_ref.shape[-1]
    cols = k_ref.shape[-1]
    for place in range(16):
        chip = pl.multiple_of(order_ref[place] * 64, 64)
        lhs[pl.ds(place * 64, 64), :tok] = own_ref[pl.ds(chip, 64), :]
        lhs[pl.ds(place * 64, 64), tok:] = other_ref[pl.ds(chip, 64), :].astype(BF16)
        if len(refs) > 3:
            half = (send_ref, keep_ref)[place // 8]
            half[pl.ds(place % 8 * 64, 64), cols:] = refs[0][pl.ds(chip, 64), :]
    rhs = jnp.concatenate([ref[0].astype(BF16) for ref in (k_ref, n_ref, k_other_ref, n_other_ref)], axis=0)
    send_ref[:, :cols] = jnp.dot(lhs[:512], rhs, preferred_element_type=F32)
    keep_ref[:, :cols] = jnp.dot(lhs[512:], rhs, preferred_element_type=F32)


def weight_grad(order, own, other, here, there, extra=()):
    _, tok, cols = here.shape
    wide = cols + sum(e.shape[1] for e in extra)

    def whole(array):
        return pl.BlockSpec(array.shape, lambda j, o: (0, 0))

    first = pl.BlockSpec((1, tok, cols), lambda j, o: (0, 0, 0))
    second = pl.BlockSpec((1, tok, cols), lambda j, o: (1, 0, 0))
    return pl.pallas_call(
        weight_kernel,
        grid_spec=pltpu.PrefetchScalarGridSpec(
            num_scalar_prefetch=1,
            grid=(1,),
            in_specs=[whole(own), whole(other), first, second, first, second] + [whole(e) for e in extra],
            out_specs=[pl.BlockSpec((512, wide), lambda j, o: (0, 0))] * 2,
            scratch_shapes=[pltpu.VMEM((1024, 4 * tok), BF16)],
        ),
        out_shape=[jax.ShapeDtypeStruct((512, wide), F32)] * 2,
        compiler_params=pltpu.CompilerParams(vmem_limit_bytes=WEIGHT_VMEM),
        cost_estimate=cost(S_weight_grad, 2 * 1024 * 4 * tok * cols, (1024 + 4 * tok) * wide * 4 + 1024 * tok * 12),
        name="weight_grad",
    )(order, own, other, here, here, there, there, *extra)


PLANES = [[chip * 2 + core for chip in range(16)] for core in range(2)]


def plane_sum(array):
    return lax.psum_scatter(array, "dp", scatter_dimension=0, axis_index_groups=PLANES, tiled=True)


class Piece:
    def __init__(self, stream, send, keep):
        self.perms, self.send, self.keep, self.step = STREAMS[stream], send, keep, 0

    def exchange(self):
        got = swap(self.send, self.perms[self.step])
        self.step += 1
        rows = self.keep.shape[0] // 2
        if self.step == 4:
            self.keep = self.keep + got
        else:
            self.send, self.keep = self.keep[:rows] + got[:rows], self.keep[rows:] + got[rows:]
        return got


def hold(value, pieces, when=True):
    if not when:
        return value
    value, *sends = tie(value, *[p.send for p in pieces])
    for p, send in zip(pieces, sends):
        p.send = send
    return value


def tie(*arrays):
    return lax.optimization_barrier(arrays)


def on_device(
    tokens,
    norm1_gain,
    w_query,
    w_key,
    w_value,
    w_output,
    norm2_gain,
    w_gate,
    w_up,
    w_down,
    cotangent,
    first_len,
    live_rows,
):
    dp = lax.axis_index("dp")
    y = lax.axis_index("tensor")
    z, x, c = dp // 8, (dp // 2) % 4, dp % 2
    slot = jnp.where(c == 0, low_bit(y), high_bit(y))
    orders = [block_order(s, z, x, c).astype(jnp.int32) for s in range(2)]
    tok, wide = tokens.shape
    gain_one = norm1_gain[None]
    gain_two = norm2_gain[None]
    tables = turn_tables(tok // 2)
    slot_k = jnp.reshape(slot, (1,)).astype(jnp.int32)
    slot_n = 1 - slot_k
    core = jnp.reshape(c, (1,)).astype(jnp.int32)
    plain = jnp.concatenate([core, jnp.array([0, 0, 1, 1], jnp.int32)])
    live = [(s < live_rows).astype(jnp.int32) for s in (slot_k, slot_n)]
    masked = jnp.concatenate([core, slot_k, slot_n, *live])

    weights = (w_query, w_key, w_value, w_output)
    part_n, one_n, attended, kept_n = attend(1, slot_n, first_len, tokens, gain_one, tables, None, *weights)
    got = swap(part_n, ALONG_Y[0])
    part_k, one_k, attended, kept_k = attend(0, slot_k, first_len, tokens, gain_one, tables, attended, *weights)
    if B1:
        masked, plain, part_k = tie(masked, plain, part_k)
    half = part_k + got
    x_k = lax.dynamic_slice_in_dim(tokens, slot * (tok // 2), tok // 2, 0).astype(F32)
    middle_k = x_k + half + swap(half, ALONG_Y[1])
    dy_own, dy_other = by_block(masked, cotangent, cotangent)
    dy_other = swap(dy_other, OTHER_CORE)
    one_own, one_other = by_block(plain, one_k, one_n)
    one_other = swap(one_other, OTHER_CORE)
    attended_other = swap(attended, OTHER_CORE)
    if B2:
        middle_k, dy_other, one_other, attended_other = tie(middle_k, dy_other, one_other, attended_other)

    feed = (w_gate, w_up, w_down)
    middle_n = swap(middle_k, ALONG_Y[0])
    out_k, back_k, hidden_k, act_k, two_k = mlp(slot_k, live_rows, middle_k, cotangent, gain_two, *feed, True)
    got = swap(back_k, ALONG_Y[0])
    hidden_k_other = swap(hidden_k, OTHER_CORE)
    act_k_other = swap(act_k, OTHER_CORE)
    slot_n, out_k = tie(slot_n, out_k)
    hidden_n, act_n, two_n = mlp(slot_n, live_rows, middle_n, cotangent, gain_two, *feed, False)
    hidden_n_other = swap(hidden_n, OTHER_CORE)
    act_n_other = swap(act_n, OTHER_CORE)
    two_own, two_other = by_block(plain, two_k, two_n)
    two_other = swap(two_other, OTHER_CORE)

    dy_own, got = tie(dy_own, got)
    hidden = (hidden_k, hidden_n, hidden_k_other, hidden_n_other)
    grads = mlp_weight_grad(dy_own, dy_other, two_own, two_other, hidden, (act_k, act_n, act_k_other, act_n_other))
    back_n = normed_grad(act_n, w_gate, w_up)
    if B4:
        back_n, grads = tie(back_n, grads)
    grads = plane_sum(grads)
    half = back_n + got
    got = swap(half, ALONG_Y[1])
    grad_2n = half + got
    slot_b = slot_n
    if B5:
        slot_b, grad_2n = tie(slot_b, grad_2n)

    grad_2k = swap(grad_2n, ALONG_Y[0])
    back_n, grad_mid_n, dm_n, lin, gain_2 = attend_back(
        1, slot_b, first_len, live_rows, (half, got), middle_n, cotangent, gain_two, kept_n, tables, None, *weights
    )
    if D1:
        hidden_n, back_n = tie(hidden_n, back_n)
    out_n = layer_part(hidden_n, w_down)
    got = swap(back_n, ALONG_Y[0])
    slot_b = slot_k
    back_k, grad_mid_k, dm_k, lin, _ = attend_back(
        0, slot_b, first_len, live_rows, (grad_2k,), middle_k, cotangent, gain_two, kept_k, tables, lin, *weights
    )
    if E3:
        out_n, back_k = tie(out_n, back_k)
    out_got = swap(out_n, ALONG_Y[0])
    lin_other = swap(lin, OTHER_CORE)
    dm_own, dm_other = by_block(plain, dm_k, dm_n)
    order_0 = orders[0]
    if G1:
        order_0, got = tie(order_0, got)
    dm_other = swap(dm_other, OTHER_CORE)
    lin_grad = weight_grad(order_0, one_own, one_other, lin, lin_other)
    out_grad = weight_grad(orders[1], dm_own, dm_other, attended, attended_other)
    three = [Piece(0, *lin_grad), Piece(1, *out_grad)]
    back_k = hold(back_k, three, B7)
    half = back_k + got
    grad_1k = half + swap(half, ALONG_Y[1])
    out_half = out_k + out_got
    for p in three:
        p.exchange()
    if G2:
        grad_1k = hold(grad_1k, three)
    if G4:
        out_half = hold(out_half, three)
    out_sum = out_half + swap(out_half, ALONG_Y[1])
    out_other = swap(out_sum, ALONG_Y[0])
    out_kept = out_sum
    for p in three:
        p.exchange()

    grad_1n = swap(grad_1k, ALONG_Y[0])
    if G3:
        grad_1n = hold(grad_1n, three)
    if G5:
        out_kept = hold(out_sum, three)
    slot_t = slot_k
    grad_tokens, gain_1 = tokens_slot(slot_t, grad_1k, grad_mid_k, tokens, gain_one, None)

    gains = jnp.concatenate([gain_1, gain_2], axis=0)
    gains = gains + swap(gains, ALONG_Y[0])
    gains = jnp.transpose(gains.reshape(2, 16, 2, 64), (2, 1, 0, 3)).reshape(2, 16, 128)
    mine = lax.dynamic_index_in_dim(gains, c, keepdims=False)
    theirs = lax.dynamic_index_in_dim(gains, 1 - c, keepdims=False)
    mine = mine + swap(theirs, OTHER_CORE)
    picks = orders[0][:, None] == jnp.arange(16, dtype=jnp.int32)[None, :]
    mine = jnp.sum(jnp.where(picks[:, :, None], mine[None], 0.0), axis=1)
    for perm in STREAMS[0][:2]:
        rows = mine.shape[0] // 2
        mine = mine[rows:] + swap(mine[:rows], perm)
    mine = hold(mine, three, D8)
    for perm in STREAMS[0][2:]:
        rows = mine.shape[0] // 2
        mine = mine[rows:] + swap(mine[:rows], perm)
    for p in three:
        p.exchange()
    if H3:
        out_other = hold(out_other, three)
    for p in three:
        if p.step < 4:
            p.exchange()
    query_key_value, output = [p.keep for p in three]

    layer_out = layer_slot(slot_k, live_rows, middle_k, out_kept, None)
    layer_out = layer_slot(slot_n, live_rows, middle_n, out_other, layer_out)
    grad_tokens, _ = tokens_slot(slot_n, grad_1n, grad_mid_n, tokens, gain_one, grad_tokens)

    return (
        layer_out,
        grad_tokens,
        mine[0, :64],
        query_key_value[:, :512],
        query_key_value[:, 512:640],
        query_key_value[:, 640:],
        jnp.transpose(output),
        mine[0, 64:],
        grads[:, 2048:4096],
        grads[:, 4096:],
        jnp.transpose(grads[:, :2048]),
    )


def solution(mesh):
    placed = (
        P("dp", None),
        P(),
        P(None, "tensor"),
        P(None, "tensor"),
        P(None, "tensor"),
        P("tensor", None),
        P(),
        P(None, "tensor"),
        P(None, "tensor"),
        P("tensor", None),
        P("dp", None),
        P("dp"),
        P("dp"),
    )
    return jax.shard_map(
        on_device,
        mesh=mesh,
        in_specs=placed,
        out_specs=(
            P("dp", None),
            P("dp", None),
            P("dp"),
            P("dp", "tensor"),
            P("dp", "tensor"),
            P("dp", "tensor"),
            P("tensor", "dp"),
            P("dp"),
            P("dp", "tensor"),
            P("dp", "tensor"),
            P("tensor", "dp"),
        ),
        check_vma=False,
    )
```

```python
import functools
import math

import jax
import jax.numpy as jnp
import numpy as np
from jax import lax
from jax.experimental import pallas as pl
from jax.experimental.pallas import tpu as pltpu
from jax.sharding import PartitionSpec as P

HEAD_DIM = 64
B2 = True
B4 = False
I1 = False
I2 = True
I3 = False
B7 = False
D1 = False
D8 = True
H3 = True
G1 = False
G2 = False
G3 = True
G4 = False
G5 = True
E3 = False
B1 = True
S_attend = 0.5
S_attend_back = 10.0
S_mlp = 2.5
S_mlp_weight_grad = 1.0
S_weight_grad = 2.5
S_by_block = 2.5
S_tk = 2.5
S_tn = 0.2
S_lk = 10.0
S_ln = 5.0
THETA = 500000.0
EPS = 1e-05
NEGATIVE = -1e30
F32 = jnp.float32
BF16 = jnp.bfloat16
ATTEND_VMEM = 58 * 1024 * 1024
MLP_VMEM = 58 * 1024 * 1024
WEIGHT_VMEM = 58 * 1024 * 1024
SMALL_VMEM = 58 * 1024 * 1024
AXES = ("dp", "tensor")


def pair_low(i):
    return i ^ 1


def pair_high(i):
    return 3 - i


def low_bit(v):
    return (v ^ (v >> 1)) & 1


def high_bit(v):
    return v >> 1


def from_bits(low, high):
    return jnp.where(high == 0, low, 3 - low)


def device_perm(move):
    pairs = []
    for dp in range(32):
        for y in range(4):
            z2, x2, c2, y2 = move(dp // 8, (dp // 2) % 4, dp % 2, y)
            pairs.append((dp * 4 + y, ((z2 * 4 + x2) * 2 + c2) * 4 + y2))
    return pairs


def first_pair(c, i):
    return pair_low(i) if c == 0 else pair_high(i)


def second_pair(c, i):
    return pair_high(i) if c == 0 else pair_low(i)


ALONG_Y = (
    device_perm(lambda z, x, c, y: (z, x, c, first_pair(c, y))),
    device_perm(lambda z, x, c, y: (z, x, c, second_pair(c, y))),
)
ALONG_X = (
    device_perm(lambda z, x, c, y: (z, first_pair(c, x), c, y)),
    device_perm(lambda z, x, c, y: (z, second_pair(c, x), c, y)),
)
ALONG_Z = (
    device_perm(lambda z, x, c, y: (first_pair(c, z), x, c, y)),
    device_perm(lambda z, x, c, y: (second_pair(c, z), x, c, y)),
)
OTHER_CORE = device_perm(lambda z, x, c, y: (z, x, 1 - c, y))
STREAMS = (ALONG_X + ALONG_Z, ALONG_Z + ALONG_X)


def swap(array, perm):
    return lax.ppermute(array, AXES, perm)


def block_order(stream, z, x, c):
    place = jnp.arange(16, dtype=jnp.int32)
    keep = [(place >> (3 - k)) & 1 for k in range(4)]

    def target(v, first, second):
        low = low_bit(v) ^ (1 - jnp.where(c == 0, first, second))
        high = high_bit(v) ^ (1 - jnp.where(c == 0, second, first))
        return from_bits(low, high)

    if stream == 0:
        return target(z, keep[2], keep[3]) * 4 + target(x, keep[0], keep[1])
    return target(z, keep[0], keep[1]) * 4 + target(x, keep[2], keep[3])


def turn_tables(tok):
    half = HEAD_DIM // 2
    freq = np.exp(np.arange(half) * (-2.0 * math.log(THETA) / HEAD_DIM))
    turned = np.arange(tok)[:, None] * freq[None, :]
    cosine, sine = np.cos(turned), np.sin(turned)
    return (
        jnp.asarray(np.tile(cosine, (1, 4)), F32),
        jnp.asarray(np.concatenate([-sine, sine, -sine, sine], axis=1), F32),
    )


def cost(scale, flops, moved, transcendentals=0):
    return pl.CostEstimate(flops=int(flops * scale), bytes_accessed=int(moved * scale), transcendentals=int(transcendentals * scale))


def times_transpose(left, right):
    return lax.dot_general(left, right, (((1,), (1,)), ((), ())), preferred_element_type=F32)


def contract_rows(left, right):
    return lax.dot_general(left, right, (((0,), (0,)), ((), ())), preferred_element_type=F32)


def turn(vectors, cosine, sine):
    lane = lax.broadcasted_iota(jnp.int32, vectors.shape, 1)
    ahead = pltpu.roll(vectors, 96, 1)
    behind = pltpu.roll(vectors, 32, 1)
    return vectors * cosine + jnp.where(lane % 64 < 32, ahead, behind) * sine


def row_turns(first, cos_ref, sin_ref):
    place = lax.broadcasted_iota(jnp.int32, cos_ref.shape, 0)
    return [jnp.where(place >= first, pltpu.roll(ref[...], first, 0), ref[...]) for ref in (cos_ref, sin_ref)]


def allowed_pairs(first, tok, group):
    query = lax.broadcasted_iota(jnp.int32, (group * tok, tok), 0) % tok
    key = lax.broadcasted_iota(jnp.int32, (group * tok, tok), 1)
    same = jnp.logical_not(jnp.logical_xor(query >= first, key >= first))
    return jnp.logical_and(same, key <= query)


def softmax_rows(queries, keys, allowed):
    raw = times_transpose(queries, keys) * HEAD_DIM**-0.5
    scores = jnp.where(allowed, raw, NEGATIVE)
    terms = jnp.exp(scores - jnp.max(scores, axis=-1, keepdims=True))
    return terms / jnp.sum(terms, axis=-1, keepdims=True)


def head_rows(array, head, count):
    return jnp.concatenate(
        [array[:, (head + k) * HEAD_DIM : (head + k + 1) * HEAD_DIM] for k in range(count)], axis=0
    )


def attend_kernel(
    slot_ref, first_ref, x_ref, gain_ref, cos_ref, sin_ref, wq_hbm, wk_hbm, wv_hbm, wo_hbm, *refs
):
    part_ref, normed_ref, attended_ref, kept_ref, wq, wk, wv, wo, sems = refs[-9:]
    copies = [
        pltpu.make_async_copy(src, dst, sems.at[k])
        for k, (src, dst) in enumerate(((wq_hbm, wq), (wk_hbm, wk), (wv_hbm, wv), (wo_hbm, wo)))
    ]
    for copy in copies:
        copy.start()
    x = x_ref[...].astype(F32)
    inverse = lax.rsqrt(jnp.mean(x * x, axis=-1, keepdims=True) + EPS)
    normed = (x * inverse * gain_ref[...].astype(F32)).astype(BF16)
    normed_ref[...] = normed
    first = first_ref[slot_ref[0]]
    cosine, sine = row_turns(first, cos_ref, sin_ref)
    tok = x.shape[0]
    heads = wq.shape[1] // HEAD_DIM
    kv = wk.shape[1] // HEAD_DIM
    group = heads // kv
    copies[0].wait()
    lin = jnp.dot(normed, wq[...], preferred_element_type=F32)
    queries = jnp.concatenate(
        [turn(lin[:, k * 128 : (k + 1) * 128], cosine, sine).astype(BF16) for k in range(heads // 2)], axis=1
    )
    copies[1].wait()
    lin = jnp.dot(normed, wk[...], preferred_element_type=F32)
    keys = jnp.concatenate(
        [turn(lin[:, k * 128 : (k + 1) * 128], cosine, sine).astype(BF16) for k in range(kv // 2)], axis=1
    )
    copies[2].wait()
    values = jnp.dot(normed, wv[...], preferred_element_type=F32).astype(BF16)
    kept_ref[:, : heads * HEAD_DIM] = queries
    kept_ref[:, heads * HEAD_DIM : (heads + kv) * HEAD_DIM] = keys
    kept_ref[:, (heads + kv) * HEAD_DIM :] = values
    allowed = allowed_pairs(first, tok, group)
    mixed = []
    for k in range(kv):
        lanes = slice(k * HEAD_DIM, (k + 1) * HEAD_DIM)
        prob = softmax_rows(head_rows(queries, k * group, group), keys[:, lanes], allowed).astype(BF16)
        out = jnp.dot(prob, values[:, lanes], preferred_element_type=F32)
        mixed += [out[g * tok : (g + 1) * tok] for g in range(group)]
    attended = jnp.concatenate(mixed, axis=1).astype(BF16)
    attended_ref[0] = attended.astype(F32)
    copies[3].wait()
    part_ref[...] = jnp.dot(attended, wo[...], preferred_element_type=F32)


def attend(entry, slot, first_len, tokens, gain, tables, attended, w_query, w_key, w_value, w_output):
    tok, wide = tokens.shape[0] // 2, tokens.shape[1]
    cols = w_query.shape[1]
    kv_cols = w_key.shape[1]
    weights = (w_query, w_key, w_value, w_output)
    aliased = () if attended is None else (attended,)

    def whole(array):
        return pl.BlockSpec(array.shape, lambda j, s: (0,) * array.ndim)

    return pl.pallas_call(
        attend_kernel,
        grid_spec=pltpu.PrefetchScalarGridSpec(
            num_scalar_prefetch=1,
            grid=(1,),
            in_specs=[
                pl.BlockSpec(memory_space=pltpu.SMEM),
                pl.BlockSpec((tok, wide), lambda j, s: (s[0], 0)),
                whole(gain),
                whole(tables[0]),
                whole(tables[1]),
            ]
            + [pl.BlockSpec(memory_space=pl.ANY)] * (4 + len(aliased)),
            out_specs=[
                pl.BlockSpec((tok, wide), lambda j, s: (0, 0)),
                pl.BlockSpec((tok, wide), lambda j, s: (0, 0)),
                pl.BlockSpec((1, tok, cols), lambda j, s: (entry, 0, 0)),
                pl.BlockSpec((tok, cols + 2 * kv_cols), lambda j, s: (0, 0)),
            ],
            scratch_shapes=[pltpu.VMEM(w.shape, w.dtype) for w in weights] + [pltpu.SemaphoreType.DMA((4,))],
        ),
        out_shape=[
            jax.ShapeDtypeStruct((tok, wide), F32),
            jax.ShapeDtypeStruct((tok, wide), BF16),
            jax.ShapeDtypeStruct((2, tok, cols), F32),
            jax.ShapeDtypeStruct((tok, cols + 2 * kv_cols), BF16),
        ],
        input_output_aliases={10: 2} if aliased else {},
        compiler_params=pltpu.CompilerParams(vmem_limit_bytes=ATTEND_VMEM),
        cost_estimate=cost(S_attend,
            2 * tok * wide * (2 * cols + 2 * kv_cols) + 4 * tok * tok * cols,
            sum(w.size * 2 for w in weights) + tok * wide * 8,
            tok * tok * cols // HEAD_DIM,
        ),
        name="attend",
    )(slot, first_len, tokens, gain, *tables, *weights, *aliased)


def attend_back_kernel(
    slot_ref, first_ref, live_ref, grad_ref, more_ref, middle_ref, cot_ref, gain_ref, kept_ref, cos_ref, sin_ref,
    wq_hbm, wk_hbm, wv_hbm, wo_hbm, *refs
):
    part_ref, grad_mid_ref, dm_ref, lin_ref, gain_out_ref, wq, wk, wv, wo, sems = refs[-10:]
    copies = [
        pltpu.make_async_copy(src, dst, sems.at[k])
        for k, (src, dst) in enumerate(((wq_hbm, wq), (wk_hbm, wk), (wv_hbm, wv), (wo_hbm, wo)))
    ]
    for k in (3, 0, 1, 2):
        copies[k].start()
    grad = grad_ref[...]
    if more_ref is not None:
        grad = grad + more_ref[...]
    middle = middle_ref[...]
    inverse = lax.rsqrt(jnp.mean(middle * middle, axis=-1, keepdims=True) + EPS)
    unit = middle * inverse
    gain_out_ref[...] = jnp.sum(grad * unit, axis=0, keepdims=True)
    scaled = grad * gain_ref[...].astype(F32)
    grad_mid = cot_ref[...].astype(F32) * live_flag(slot_ref, live_ref) + inverse * (
        scaled - unit * jnp.mean(scaled * unit, axis=-1, keepdims=True)
    )
    grad_mid_ref[...] = grad_mid
    dm = grad_mid.astype(BF16)
    dm_ref[...] = dm
    tok = dm.shape[0]
    heads = wq.shape[1] // HEAD_DIM
    kv = wk.shape[1] // HEAD_DIM
    group = heads // kv
    first = first_ref[slot_ref[0]]
    cosine, sine = row_turns(first, cos_ref, sin_ref)
    sine = -sine
    allowed = allowed_pairs(first, tok, group)
    copies[3].wait()
    grad_att = times_transpose(dm, wo[...]).astype(BF16)
    grad_q, grad_k, grad_v = [], [], []
    scale = HEAD_DIM**-0.5
    for k in range(kv):
        q_rows = head_rows(kept_ref, k * group, group)
        keys = kept_ref[:, (heads + k) * HEAD_DIM : (heads + k + 1) * HEAD_DIM]
        values = kept_ref[:, (heads + kv + k) * HEAD_DIM : (heads + kv + k + 1) * HEAD_DIM]
        prob = softmax_rows(q_rows, keys, allowed)
        d_rows = head_rows(grad_att, k * group, group)
        grad_v.append(contract_rows(prob.astype(BF16), d_rows))
        grad_prob = times_transpose(d_rows, values)
        delta = jnp.sum(prob * grad_prob, axis=-1, keepdims=True)
        grad_score = (prob * (grad_prob - delta)).astype(BF16)
        rows = jnp.dot(grad_score, keys, preferred_element_type=F32) * scale
        grad_q += [rows[g * tok : (g + 1) * tok] for g in range(group)]
        grad_k.append(contract_rows(grad_score, q_rows) * scale)

    def turned_back(parts):
        pairs = [jnp.concatenate(parts[k : k + 2], axis=1) for k in range(0, len(parts), 2)]
        return jnp.concatenate([turn(p, cosine, sine).astype(BF16) for p in pairs], axis=1)

    lin_q = turned_back(grad_q)
    lin_k = turned_back(grad_k)
    lin_v = jnp.concatenate(grad_v, axis=1).astype(BF16)
    cols, kv_cols = heads * HEAD_DIM, kv * HEAD_DIM
    lin_ref[0, :, :cols] = lin_q.astype(F32)
    lin_ref[0, :, cols : cols + kv_cols] = lin_k.astype(F32)
    lin_ref[0, :, cols + kv_cols :] = lin_v.astype(F32)
    for k in range(3):
        copies[k].wait()
    part_ref[...] = (
        times_transpose(lin_q, wq[...]) + times_transpose(lin_k, wk[...]) + times_transpose(lin_v, wv[...])
    )


def attend_back(
    entry, slot, first_len, live_rows, grads, middle, cotangent, gain, kept, tables, lin, w_query, w_key, w_value, w_output
):
    tok, wide = middle.shape
    cols = w_query.shape[1]
    kv_cols = w_key.shape[1]
    weights = (w_query, w_key, w_value, w_output)
    aliased = () if lin is None else (lin,)
    rows = pl.BlockSpec((tok, wide), lambda j, s: (0, 0))

    def whole(array):
        return pl.BlockSpec(array.shape, lambda j, s: (0,) * array.ndim)

    def kernel(slot_ref, first_ref, live_ref, grad_ref, *refs):
        if len(grads) == 1:
            refs = (None, *refs)
        attend_back_kernel(slot_ref, first_ref, live_ref, grad_ref, *refs)

    return pl.pallas_call(
        kernel,
        grid_spec=pltpu.PrefetchScalarGridSpec(
            num_scalar_prefetch=1,
            grid=(1,),
            in_specs=[
                pl.BlockSpec(memory_space=pltpu.SMEM),
                pl.BlockSpec(memory_space=pltpu.SMEM),
                *[rows] * (len(grads) + 1),
                pl.BlockSpec((tok, wide), lambda j, s: (s[0], 0)),
                whole(gain),
                whole(kept),
                whole(tables[0]),
                whole(tables[1]),
            ]
            + [pl.BlockSpec(memory_space=pl.ANY)] * (4 + len(aliased)),
            out_specs=[
                rows,
                rows,
                rows,
                pl.BlockSpec((1, tok, cols + 2 * kv_cols), lambda j, s: (entry, 0, 0)),
                pl.BlockSpec((1, wide), lambda j, s: (0, 0)),
            ],
            scratch_shapes=[pltpu.VMEM(w.shape, w.dtype) for w in weights] + [pltpu.SemaphoreType.DMA((4,))],
        ),
        out_shape=[
            jax.ShapeDtypeStruct((tok, wide), F32),
            jax.ShapeDtypeStruct((tok, wide), F32),
            jax.ShapeDtypeStruct((tok, wide), BF16),
            jax.ShapeDtypeStruct((2, tok, cols + 2 * kv_cols), F32),
            jax.ShapeDtypeStruct((1, wide), F32),
        ],
        input_output_aliases={13 + len(grads): 3} if aliased else {},
        compiler_params=pltpu.CompilerParams(vmem_limit_bytes=ATTEND_VMEM),
        cost_estimate=cost(S_attend_back,
            2 * tok * wide * (2 * cols + 2 * kv_cols) + 10 * tok * tok * cols,
            sum(w.size * 2 for w in weights) + tok * wide * 24,
            tok * tok * cols // HEAD_DIM,
        ),
        name="attend_back",
    )(slot, first_len, live_rows, *grads, middle, cotangent, gain, kept, *tables, *weights, *aliased)


def blocks_kernel(core_ref, first_ref, second_ref, own_ref, other_ref):
    rows = [
        ref[...].astype(F32) * core_ref[3 + k].astype(F32) for k, ref in enumerate((first_ref, second_ref))
    ]
    rows = jnp.concatenate(rows, axis=0)
    core = core_ref[0]
    for k in range(rows.shape[1] // 128):
        turned = jnp.transpose(rows[:, k * 128 : (k + 1) * 128])
        low, high = turned[:64], turned[64:]
        own_ref[k * 64 : (k + 1) * 64, :] = jnp.where(core == 0, low, high).astype(BF16)
        other_ref[k * 64 : (k + 1) * 64, :] = jnp.where(core == 0, high, low)


def by_block(choice, first, second):
    tok = 192
    chips = 8
    return pl.pallas_call(
        blocks_kernel,
        grid_spec=pltpu.PrefetchScalarGridSpec(
            num_scalar_prefetch=1,
            grid=(16 // chips,),
            in_specs=[
                pl.BlockSpec((tok, 128 * chips), lambda j, o: (o[1], j)),
                pl.BlockSpec((tok, 128 * chips), lambda j, o: (o[2], j)),
            ],
            out_specs=[pl.BlockSpec((64 * chips, 2 * tok), lambda j, o: (j, 0))] * 2,
        ),
        out_shape=[
            jax.ShapeDtypeStruct((1024, 2 * tok), BF16),
            jax.ShapeDtypeStruct((1024, 2 * tok), F32),
        ],
        compiler_params=pltpu.CompilerParams(vmem_limit_bytes=SMALL_VMEM),
        cost_estimate=cost(S_by_block, 0, 2048 * tok * 10),
        name="by_block",
    )(choice, first, second)


def live_flag(slot_ref, live_ref):
    return jnp.where(slot_ref[0] < live_ref[0], 1.0, 0.0)


def mlp_kernel(
    slot_ref, live_ref, middle_ref, cot_ref, gain_ref, wg_ref, wu_ref, wd_ref, *refs
):
    hidden_ref, act_ref, normed_ref, dy = refs[-4:]
    step = pl.program_id(0)

    @pl.when(step == 0)
    def _():
        middle = middle_ref[...]
        inverse = lax.rsqrt(jnp.mean(middle * middle, axis=-1, keepdims=True) + EPS)
        normed_ref[...] = (middle * inverse * gain_ref[...].astype(F32)).astype(BF16)
        dy[...] = (cot_ref[...].astype(F32) * live_flag(slot_ref, live_ref)).astype(BF16)

    n = normed_ref[...]
    w_gate = wg_ref[...]
    w_up = wu_ref[...]
    w_down = wd_ref[...]
    gate = jnp.dot(n, w_gate, preferred_element_type=F32)
    up = jnp.dot(n, w_up, preferred_element_type=F32)
    grad_hidden = times_transpose(dy[...], w_down)
    sig = 1.0 / (1.0 + jnp.exp(-gate))
    silu = gate * sig
    hidden = (silu * up).astype(BF16)
    d_gate = (grad_hidden * up * sig * (1.0 + gate * (1.0 - sig))).astype(BF16)
    d_up = (grad_hidden * silu).astype(BF16)
    hidden_ref[...] = hidden.astype(F32)
    act_ref[0] = d_gate.astype(F32)
    act_ref[1] = d_up.astype(F32)
    if len(refs) == 4:
        return
    grad_ref = refs[0]
    grad_part = times_transpose(d_gate, w_gate) + times_transpose(d_up, w_up)

    @pl.when(step == 0)
    def _():
        grad_ref[...] = grad_part

    @pl.when(step > 0)
    def _():
        grad_ref[...] += grad_part


def mlp(slot, live_rows, middle, cotangent, gain, w_gate, w_up, w_down, sums):
    tok, wide = middle.shape
    units = w_gate.shape[1]
    tile = 512
    whole = pl.BlockSpec((tok, wide), lambda t, s: (0, 0))
    return pl.pallas_call(
        mlp_kernel,
        grid_spec=pltpu.PrefetchScalarGridSpec(
            num_scalar_prefetch=1,
            grid=(units // tile,),
            in_specs=[
                pl.BlockSpec(memory_space=pltpu.SMEM),
                whole,
                pl.BlockSpec((tok, wide), lambda t, s: (s[0], 0)),
                pl.BlockSpec((1, wide), lambda t, s: (0, 0)),
                pl.BlockSpec((wide, tile), lambda t, s: (0, t)),
                pl.BlockSpec((wide, tile), lambda t, s: (0, t)),
                pl.BlockSpec((tile, wide), lambda t, s: (t, 0)),
            ],
            out_specs=[whole] * sums
            + [
                pl.BlockSpec((tok, tile), lambda t, s: (0, t)),
                pl.BlockSpec((2, tok, tile), lambda t, s: (0, 0, t)),
                whole,
            ],
            scratch_shapes=[pltpu.VMEM((tok, wide), BF16)],
        ),
        out_shape=[jax.ShapeDtypeStruct((tok, wide), F32)] * sums
        + [
            jax.ShapeDtypeStruct((tok, units), F32),
            jax.ShapeDtypeStruct((2, tok, units), F32),
            jax.ShapeDtypeStruct((tok, wide), BF16),
        ],
        compiler_params=pltpu.CompilerParams(vmem_limit_bytes=MLP_VMEM),
        cost_estimate=cost(S_mlp, 12 * tok * wide * units, 3 * wide * units * 2 + 5 * tok * wide * 4, tok * units),
        name="mlp",
    )(slot, live_rows, middle, cotangent, gain, w_gate, w_up, w_down)


def normed_grad_kernel(gate_ref, up_ref, wg_ref, wu_ref, out_ref):
    part = times_transpose(gate_ref[0].astype(BF16), wg_ref[...])
    part += times_transpose(up_ref[0].astype(BF16), wu_ref[...])

    @pl.when(pl.program_id(0) == 0)
    def _():
        out_ref[...] = part

    @pl.when(pl.program_id(0) > 0)
    def _():
        out_ref[...] += part


def normed_grad(act, w_gate, w_up):
    _, tok, units = act.shape
    wide = w_gate.shape[0]
    tile = 512
    return pl.pallas_call(
        normed_grad_kernel,
        grid=(units // tile,),
        in_specs=[
            pl.BlockSpec((1, tok, tile), lambda t: (0, 0, t)),
            pl.BlockSpec((1, tok, tile), lambda t: (1, 0, t)),
            pl.BlockSpec((wide, tile), lambda t: (0, t)),
            pl.BlockSpec((wide, tile), lambda t: (0, t)),
        ],
        out_specs=pl.BlockSpec((tok, wide), lambda t: (0, 0)),
        out_shape=jax.ShapeDtypeStruct((tok, wide), F32),
        compiler_params=pltpu.CompilerParams(vmem_limit_bytes=MLP_VMEM),
        cost_estimate=cost(S_mlp, 4 * tok * wide * units, 2 * wide * units * 2 + 3 * tok * wide * 4),
        name="normed_grad",
    )(act, act, w_gate, w_up)


def layer_part_kernel(k_ref, n_ref, wd_ref, out_k_ref, out_n_ref):
    rows = jnp.concatenate([k_ref[...], n_ref[...]], axis=0).astype(BF16)
    product = jnp.dot(rows, wd_ref[...], preferred_element_type=F32)
    tok = k_ref.shape[0]
    out_k_ref[...] = product[:tok]
    out_n_ref[...] = product[tok:]


def layer_part(hidden_k, hidden_n, w_down):
    tok, units = hidden_k.shape
    wide = w_down.shape[1]
    tile = 512
    return pl.pallas_call(
        layer_part_kernel,
        grid=(wide // tile,),
        in_specs=[
            pl.BlockSpec((tok, units), lambda t: (0, 0)),
            pl.BlockSpec((tok, units), lambda t: (0, 0)),
            pl.BlockSpec((units, tile), lambda t: (0, t)),
        ],
        out_specs=[pl.BlockSpec((tok, tile), lambda t: (0, t))] * 2,
        out_shape=[jax.ShapeDtypeStruct((tok, wide), F32)] * 2,
        compiler_params=pltpu.CompilerParams(vmem_limit_bytes=MLP_VMEM),
        cost_estimate=cost(S_mlp, 4 * tok * wide * units, wide * units * 2 + 4 * tok * wide * 4),
        name="layer_part",
    )(hidden_k, hidden_n, w_down)


def mlp_weight_kernel(dy_own, dy_other, two_own, two_other, *refs):
    hidden_refs, act_refs, out_ref, lhs = refs[:4], refs[4:8], refs[8], refs[9]
    tok = dy_own.shape[-1]
    step = pl.program_id(0)

    def product(own, other, rhs_refs, first):
        @pl.when(first)
        def _():
            lhs[:, :tok] = own[...]
            lhs[:, tok:] = other[...].astype(BF16)

        rhs = jnp.concatenate([ref[...].reshape(ref.shape[-2:]).astype(BF16) for ref in rhs_refs], axis=0)
        out_ref[...] = jnp.dot(lhs[...], rhs, preferred_element_type=F32)

    @pl.when(step < 2)
    def _():
        product(dy_own, dy_other, hidden_refs, step == 0)

    @pl.when(step >= 2)
    def _():
        product(two_own, two_other, act_refs, step == 2)


def mlp_weight_grad(dy_own, dy_other, two_own, two_other, hidden, acts):
    kinds, tok, cols = acts[0].shape
    tile = cols // 2
    whole = pl.BlockSpec(dy_own.shape, lambda j: (0, 0))

    def act_at(j):
        k = jnp.maximum(j - 2, 0)
        return (k // 2, 0, k % 2)

    return pl.pallas_call(
        mlp_weight_kernel,
        grid=(2 + 2 * kinds,),
        in_specs=[whole] * 4
        + [pl.BlockSpec((tok, tile), lambda j: (0, jnp.minimum(j, 1)))] * 4
        + [pl.BlockSpec((1, tok, tile), act_at)] * 4,
        out_specs=pl.BlockSpec((1024, tile), lambda j: (0, j)),
        scratch_shapes=[pltpu.VMEM((1024, 4 * tok), BF16)],
        out_shape=jax.ShapeDtypeStruct((1024, (2 + 2 * kinds) * tile), F32),
        compiler_params=pltpu.CompilerParams(vmem_limit_bytes=WEIGHT_VMEM),
        cost_estimate=cost(S_mlp_weight_grad, 2 * 1024 * 4 * tok * 6 * tile, (1024 + 4 * tok) * 6 * tile * 4),
        name="mlp_weight_grad",
    )(dy_own, dy_other, two_own, two_other, *hidden, *acts)


def tokens_kernel(slot_ref, grad_ref, mid_ref, x_ref, gain_ref, *refs):
    out_ref, gain_out_ref = refs[-2:]
    grad = grad_ref[...]
    x = x_ref[...].astype(F32)
    inverse = lax.rsqrt(jnp.mean(x * x, axis=-1, keepdims=True) + EPS)
    unit = x * inverse
    scaled = grad * gain_ref[...].astype(F32)
    out_ref[...] = mid_ref[...] + inverse * (scaled - unit * jnp.mean(scaled * unit, axis=-1, keepdims=True))
    gain_part = jnp.sum(grad * unit, axis=0, keepdims=True)

    @pl.when(pl.program_id(0) == 0)
    def _():
        gain_out_ref[...] = gain_part

    @pl.when(pl.program_id(0) > 0)
    def _():
        gain_out_ref[...] += gain_part


def tokens_slot(slot, grad, grad_mid, tokens, gain, whole):
    tok, wide = grad.shape
    parts = 2
    tile = tok // parts
    aliased = () if whole is None else (whole,)
    rows = pl.BlockSpec((tile, wide), lambda j, s: (j, 0))
    in_whole = pl.BlockSpec((tile, wide), lambda j, s: (s[0] * parts + j, 0))
    line = pl.BlockSpec((1, wide), lambda j, s: (0, 0))
    return pl.pallas_call(
        tokens_kernel,
        grid_spec=pltpu.PrefetchScalarGridSpec(
            num_scalar_prefetch=1,
            grid=(parts,),
            in_specs=[rows, rows, in_whole, line] + [pl.BlockSpec(memory_space=pl.ANY)] * len(aliased),
            out_specs=[in_whole, line],
        ),
        out_shape=[jax.ShapeDtypeStruct((2 * tok, wide), F32), jax.ShapeDtypeStruct((1, wide), F32)],
        input_output_aliases={5: 0} if aliased else {},
        compiler_params=pltpu.CompilerParams(vmem_limit_bytes=SMALL_VMEM),
        cost_estimate=cost(S_tk if whole is None else S_tn, 10 * tok * wide, 14 * tok * wide),
        name="grad_tokens",
    )(slot, grad, grad_mid, tokens, gain, *aliased)


def layer_kernel(slot_ref, live_ref, middle_ref, sum_ref, *refs):
    refs[-1][...] = (live_flag(slot_ref, live_ref) * (middle_ref[...] + sum_ref[...])).astype(BF16)


def layer_slot(slot, live_rows, middle, added, whole):
    tok, wide = middle.shape
    parts = 2
    tile = tok // parts
    aliased = () if whole is None else (whole,)
    rows = pl.BlockSpec((tile, wide), lambda j, s: (j, 0))
    return pl.pallas_call(
        layer_kernel,
        grid_spec=pltpu.PrefetchScalarGridSpec(
            num_scalar_prefetch=1,
            grid=(parts,),
            in_specs=[pl.BlockSpec(memory_space=pltpu.SMEM), rows, rows]
            + [pl.BlockSpec(memory_space=pl.ANY)] * len(aliased),
            out_specs=pl.BlockSpec((tile, wide), lambda j, s: (s[0] * parts + j, 0)),
        ),
        out_shape=jax.ShapeDtypeStruct((2 * tok, wide), BF16),
        input_output_aliases={4: 0} if aliased else {},
        compiler_params=pltpu.CompilerParams(vmem_limit_bytes=SMALL_VMEM),
        cost_estimate=cost(S_lk if whole is None else S_ln, 2 * tok * wide, 10 * tok * wide),
        name="layer_out",
    )(slot, live_rows, middle, added, *aliased)


def weight_kernel(order_ref, own_ref, other_ref, k_ref, n_ref, k_other_ref, n_other_ref, *refs):
    send_ref, keep_ref, lhs = refs[-3:]
    tok = own_ref.shape[-1]
    cols = k_ref.shape[-1]
    for place in range(16):
        chip = pl.multiple_of(order_ref[place] * 64, 64)
        lhs[pl.ds(place * 64, 64), :tok] = own_ref[pl.ds(chip, 64), :]
        lhs[pl.ds(place * 64, 64), tok:] = other_ref[pl.ds(chip, 64), :].astype(BF16)
        if len(refs) > 3:
            half = (send_ref, keep_ref)[place // 8]
            half[pl.ds(place % 8 * 64, 64), cols:] = refs[0][pl.ds(chip, 64), :]
    rhs = jnp.concatenate([ref[0].astype(BF16) for ref in (k_ref, n_ref, k_other_ref, n_other_ref)], axis=0)
    send_ref[:, :cols] = jnp.dot(lhs[:512], rhs, preferred_element_type=F32)
    keep_ref[:, :cols] = jnp.dot(lhs[512:], rhs, preferred_element_type=F32)


def weight_grad(order, own, other, here, there, extra=()):
    _, tok, cols = here.shape
    wide = cols + sum(e.shape[1] for e in extra)

    def whole(array):
        return pl.BlockSpec(array.shape, lambda j, o: (0, 0))

    first = pl.BlockSpec((1, tok, cols), lambda j, o: (0, 0, 0))
    second = pl.BlockSpec((1, tok, cols), lambda j, o: (1, 0, 0))
    return pl.pallas_call(
        weight_kernel,
        grid_spec=pltpu.PrefetchScalarGridSpec(
            num_scalar_prefetch=1,
            grid=(1,),
            in_specs=[whole(own), whole(other), first, second, first, second] + [whole(e) for e in extra],
            out_specs=[pl.BlockSpec((512, wide), lambda j, o: (0, 0))] * 2,
            scratch_shapes=[pltpu.VMEM((1024, 4 * tok), BF16)],
        ),
        out_shape=[jax.ShapeDtypeStruct((512, wide), F32)] * 2,
        compiler_params=pltpu.CompilerParams(vmem_limit_bytes=WEIGHT_VMEM),
        cost_estimate=cost(S_weight_grad, 2 * 1024 * 4 * tok * cols, (1024 + 4 * tok) * wide * 4 + 1024 * tok * 12),
        name="weight_grad",
    )(order, own, other, here, here, there, there, *extra)


PLANES = [[chip * 2 + core for chip in range(16)] for core in range(2)]


def plane_sum(array):
    return lax.psum_scatter(array, "dp", scatter_dimension=0, axis_index_groups=PLANES, tiled=True)


class Piece:
    def __init__(self, stream, send, keep):
        self.perms, self.send, self.keep, self.step = STREAMS[stream], send, keep, 0

    def exchange(self):
        got = swap(self.send, self.perms[self.step])
        self.step += 1
        rows = self.keep.shape[0] // 2
        if self.step == 4:
            self.keep = self.keep + got
        else:
            self.send, self.keep = self.keep[:rows] + got[:rows], self.keep[rows:] + got[rows:]
        return got


def hold(value, pieces, when=True):
    if not when:
        return value
    value, *sends = tie(value, *[p.send for p in pieces])
    for p, send in zip(pieces, sends):
        p.send = send
    return value


def tie(*arrays):
    return lax.optimization_barrier(arrays)


def on_device(
    tokens,
    norm1_gain,
    w_query,
    w_key,
    w_value,
    w_output,
    norm2_gain,
    w_gate,
    w_up,
    w_down,
    cotangent,
    first_len,
    live_rows,
):
    dp = lax.axis_index("dp")
    y = lax.axis_index("tensor")
    z, x, c = dp // 8, (dp // 2) % 4, dp % 2
    slot = jnp.where(c == 0, low_bit(y), high_bit(y))
    orders = [block_order(s, z, x, c).astype(jnp.int32) for s in range(2)]
    tok, wide = tokens.shape
    gain_one = norm1_gain[None]
    gain_two = norm2_gain[None]
    tables = turn_tables(tok // 2)
    slot_k = jnp.reshape(slot, (1,)).astype(jnp.int32)
    slot_n = 1 - slot_k
    core = jnp.reshape(c, (1,)).astype(jnp.int32)
    plain = jnp.concatenate([core, jnp.array([0, 0, 1, 1], jnp.int32)])
    live = [(s < live_rows).astype(jnp.int32) for s in (slot_k, slot_n)]
    masked = jnp.concatenate([core, slot_k, slot_n, *live])

    weights = (w_query, w_key, w_value, w_output)
    part_n, one_n, attended, kept_n = attend(1, slot_n, first_len, tokens, gain_one, tables, None, *weights)
    got = swap(part_n, ALONG_Y[0])
    part_k, one_k, attended, kept_k = attend(0, slot_k, first_len, tokens, gain_one, tables, attended, *weights)
    if B1:
        masked, plain, part_k = tie(masked, plain, part_k)
    half = part_k + got
    x_k = lax.dynamic_slice_in_dim(tokens, slot * (tok // 2), tok // 2, 0).astype(F32)
    middle_k = x_k + half + swap(half, ALONG_Y[1])
    dy_own, dy_other = by_block(masked, cotangent, cotangent)
    dy_other = swap(dy_other, OTHER_CORE)
    one_own, one_other = by_block(plain, one_k, one_n)
    one_other = swap(one_other, OTHER_CORE)
    attended_other = swap(attended, OTHER_CORE)
    if B2:
        middle_k, dy_other, one_other, attended_other = tie(middle_k, dy_other, one_other, attended_other)

    feed = (w_gate, w_up, w_down)
    middle_n = swap(middle_k, ALONG_Y[0])
    back_k, hidden_k, act_k, two_k = mlp(slot_k, live_rows, middle_k, cotangent, gain_two, *feed, True)
    got = swap(back_k, ALONG_Y[0])
    hidden_k_other = swap(hidden_k, OTHER_CORE)
    act_k_other = swap(act_k, OTHER_CORE)
    slot_n, two_k = tie(slot_n, two_k)
    hidden_n, act_n, two_n = mlp(slot_n, live_rows, middle_n, cotangent, gain_two, *feed, False)
    hidden_n_other = swap(hidden_n, OTHER_CORE)
    act_n_other = swap(act_n, OTHER_CORE)
    two_own, two_other = by_block(plain, two_k, two_n)
    two_other = swap(two_other, OTHER_CORE)

    back_n = normed_grad(act_n, w_gate, w_up)
    half = back_n + got
    dy_own, half = tie(dy_own, half)
    got = swap(half, ALONG_Y[1])
    hidden = (hidden_k, hidden_n, hidden_k_other, hidden_n_other)
    grads = mlp_weight_grad(dy_own, dy_other, two_own, two_other, hidden, (act_k, act_n, act_k_other, act_n_other))
    if B4:
        got, grads = tie(got, grads)
    grad_2n = half + got
    slot_b = slot_n
    if I2:
        hidden_n, grads = tie(hidden_n, grads)
        out_k, out_n = layer_part(hidden_k, hidden_n, w_down)
        slot_b, out_k = tie(slot_b, out_k)

    grads = plane_sum(grads)
    grad_2k = swap(grad_2n, ALONG_Y[0])
    back_n, grad_mid_n, dm_n, lin, gain_2 = attend_back(
        1, slot_b, first_len, live_rows, (half, got), middle_n, cotangent, gain_two, kept_n, tables, None, *weights
    )
    if not I2:
        if D1:
            hidden_n, back_n = tie(hidden_n, back_n)
        out_k, out_n = layer_part(hidden_k, hidden_n, w_down)
    if I3:
        out_n, back_n = tie(out_n, back_n)
    got = swap(back_n, ALONG_Y[0])
    slot_b = slot_k
    if I1:
        slot_b, out_k = tie(slot_b, out_k)
    back_k, grad_mid_k, dm_k, lin, _ = attend_back(
        0, slot_b, first_len, live_rows, (grad_2k,), middle_k, cotangent, gain_two, kept_k, tables, lin, *weights
    )
    if E3:
        out_n, back_k = tie(out_n, back_k)
    out_got = swap(out_n, ALONG_Y[0])
    lin_other = swap(lin, OTHER_CORE)
    dm_own, dm_other = by_block(plain, dm_k, dm_n)
    order_0 = orders[0]
    if G1:
        order_0, got = tie(order_0, got)
    dm_other = swap(dm_other, OTHER_CORE)
    lin_grad = weight_grad(order_0, one_own, one_other, lin, lin_other)
    out_grad = weight_grad(orders[1], dm_own, dm_other, attended, attended_other)
    three = [Piece(0, *lin_grad), Piece(1, *out_grad)]
    back_k = hold(back_k, three, B7)
    half = back_k + got
    grad_1k = half + swap(half, ALONG_Y[1])
    out_half = out_k + out_got
    for p in three:
        p.exchange()
    if G2:
        grad_1k = hold(grad_1k, three)
    if G4:
        out_half = hold(out_half, three)
    out_sum = out_half + swap(out_half, ALONG_Y[1])
    out_other = swap(out_sum, ALONG_Y[0])
    out_kept = out_sum
    for p in three:
        p.exchange()

    grad_1n = swap(grad_1k, ALONG_Y[0])
    if G3:
        grad_1n = hold(grad_1n, three)
    if G5:
        out_kept = hold(out_sum, three)
    slot_t = slot_k
    grad_tokens, gain_1 = tokens_slot(slot_t, grad_1k, grad_mid_k, tokens, gain_one, None)

    gains = jnp.concatenate([gain_1, gain_2], axis=0)
    gains = gains + swap(gains, ALONG_Y[0])
    gains = jnp.transpose(gains.reshape(2, 16, 2, 64), (2, 1, 0, 3)).reshape(2, 16, 128)
    mine = lax.dynamic_index_in_dim(gains, c, keepdims=False)
    theirs = lax.dynamic_index_in_dim(gains, 1 - c, keepdims=False)
    mine = mine + swap(theirs, OTHER_CORE)
    picks = orders[0][:, None] == jnp.arange(16, dtype=jnp.int32)[None, :]
    mine = jnp.sum(jnp.where(picks[:, :, None], mine[None], 0.0), axis=1)
    for perm in STREAMS[0][:2]:
        rows = mine.shape[0] // 2
        mine = mine[rows:] + swap(mine[:rows], perm)
    mine = hold(mine, three, D8)
    for perm in STREAMS[0][2:]:
        rows = mine.shape[0] // 2
        mine = mine[rows:] + swap(mine[:rows], perm)
    for p in three:
        p.exchange()
    if H3:
        out_other = hold(out_other, three)
    for p in three:
        if p.step < 4:
            p.exchange()
    query_key_value, output = [p.keep for p in three]

    layer_out = layer_slot(slot_k, live_rows, middle_k, out_kept, None)
    layer_out = layer_slot(slot_n, live_rows, middle_n, out_other, layer_out)
    grad_tokens, _ = tokens_slot(slot_n, grad_1n, grad_mid_n, tokens, gain_one, grad_tokens)

    return (
        layer_out,
        grad_tokens,
        mine[0, :64],
        query_key_value[:, :512],
        query_key_value[:, 512:640],
        query_key_value[:, 640:],
        jnp.transpose(output),
        mine[0, 64:],
        grads[:, 2048:4096],
        grads[:, 4096:],
        jnp.transpose(grads[:, :2048]),
    )


def solution(mesh):
    placed = (
        P("dp", None),
        P(),
        P(None, "tensor"),
        P(None, "tensor"),
        P(None, "tensor"),
        P("tensor", None),
        P(),
        P(None, "tensor"),
        P(None, "tensor"),
        P("tensor", None),
        P("dp", None),
        P("dp"),
        P("dp"),
    )
    return jax.shard_map(
        on_device,
        mesh=mesh,
        in_specs=placed,
        out_specs=(
            P("dp", None),
            P("dp", None),
            P("dp"),
            P("dp", "tensor"),
            P("dp", "tensor"),
            P("dp", "tensor"),
            P("tensor", "dp"),
            P("dp"),
            P("dp", "tensor"),
            P("dp", "tensor"),
            P("tensor", "dp"),
        ),
        check_vma=False,
    )
```

```python
import functools
import math

import jax
import jax.numpy as jnp
import numpy as np
from jax import lax
from jax.experimental import pallas as pl
from jax.experimental.pallas import tpu as pltpu
from jax.sharding import PartitionSpec as P

HEAD_DIM = 64
B2 = True
B4 = False
I1 = False
I2 = True
I3 = False
B7 = False
D1 = False
D8 = True
H3 = True
G1 = False
G2 = False
G3 = True
G4 = False
G5 = True
E3 = False
B1 = True
S_attend = 0.5
S_attend_back = 10.0
S_mlp = 2.5
S_mlp_weight_grad = 1.0
S_weight_grad = 2.5
S_by_block = 2.5
S_tk = 2.5
S_tn = 0.2
S_lk = 10.0
S_ln = 5.0
THETA = 500000.0
EPS = 1e-05
NEGATIVE = -1e30
F32 = jnp.float32
BF16 = jnp.bfloat16
ATTEND_VMEM = 58 * 1024 * 1024
MLP_VMEM = 58 * 1024 * 1024
WEIGHT_VMEM = 58 * 1024 * 1024
SMALL_VMEM = 58 * 1024 * 1024
AXES = ("dp", "tensor")


def pair_low(i):
    return i ^ 1


def pair_high(i):
    return 3 - i


def low_bit(v):
    return (v ^ (v >> 1)) & 1


def high_bit(v):
    return v >> 1


def from_bits(low, high):
    return jnp.where(high == 0, low, 3 - low)


def device_perm(move):
    pairs = []
    for dp in range(32):
        for y in range(4):
            z2, x2, c2, y2 = move(dp // 8, (dp // 2) % 4, dp % 2, y)
            pairs.append((dp * 4 + y, ((z2 * 4 + x2) * 2 + c2) * 4 + y2))
    return pairs


def first_pair(c, i):
    return pair_low(i) if c == 0 else pair_high(i)


def second_pair(c, i):
    return pair_high(i) if c == 0 else pair_low(i)


ALONG_Y = (
    device_perm(lambda z, x, c, y: (z, x, c, first_pair(c, y))),
    device_perm(lambda z, x, c, y: (z, x, c, second_pair(c, y))),
)
ALONG_X = (
    device_perm(lambda z, x, c, y: (z, first_pair(c, x), c, y)),
    device_perm(lambda z, x, c, y: (z, second_pair(c, x), c, y)),
)
ALONG_Z = (
    device_perm(lambda z, x, c, y: (first_pair(c, z), x, c, y)),
    device_perm(lambda z, x, c, y: (second_pair(c, z), x, c, y)),
)
OTHER_CORE = device_perm(lambda z, x, c, y: (z, x, 1 - c, y))
STREAMS = (ALONG_X + ALONG_Z, ALONG_Z + ALONG_X)


def swap(array, perm):
    return lax.ppermute(array, AXES, perm)


def block_order(stream, z, x, c):
    place = jnp.arange(16, dtype=jnp.int32)
    keep = [(place >> (3 - k)) & 1 for k in range(4)]

    def target(v, first, second):
        low = low_bit(v) ^ (1 - jnp.where(c == 0, first, second))
        high = high_bit(v) ^ (1 - jnp.where(c == 0, second, first))
        return from_bits(low, high)

    if stream == 0:
        return target(z, keep[2], keep[3]) * 4 + target(x, keep[0], keep[1])
    return target(z, keep[0], keep[1]) * 4 + target(x, keep[2], keep[3])


def turn_tables(tok):
    half = HEAD_DIM // 2
    freq = np.exp(np.arange(half) * (-2.0 * math.log(THETA) / HEAD_DIM))
    turned = np.arange(tok)[:, None] * freq[None, :]
    cosine, sine = np.cos(turned), np.sin(turned)
    return (
        jnp.asarray(np.tile(cosine, (1, 4)), F32),
        jnp.asarray(np.concatenate([-sine, sine, -sine, sine], axis=1), F32),
    )


def cost(scale, flops, moved, transcendentals=0):
    return pl.CostEstimate(flops=int(flops * scale), bytes_accessed=int(moved * scale), transcendentals=int(transcendentals * scale))


def times_transpose(left, right):
    return lax.dot_general(left, right, (((1,), (1,)), ((), ())), preferred_element_type=F32)


def contract_rows(left, right):
    return lax.dot_general(left, right, (((0,), (0,)), ((), ())), preferred_element_type=F32)


def turn(vectors, cosine, sine):
    lane = lax.broadcasted_iota(jnp.int32, vectors.shape, 1)
    ahead = pltpu.roll(vectors, 96, 1)
    behind = pltpu.roll(vectors, 32, 1)
    return vectors * cosine + jnp.where(lane % 64 < 32, ahead, behind) * sine


def row_turns(first, cos_ref, sin_ref):
    place = lax.broadcasted_iota(jnp.int32, cos_ref.shape, 0)
    return [jnp.where(place >= first, pltpu.roll(ref[...], first, 0), ref[...]) for ref in (cos_ref, sin_ref)]


def allowed_pairs(first, tok, group):
    query = lax.broadcasted_iota(jnp.int32, (group * tok, tok), 0) % tok
    key = lax.broadcasted_iota(jnp.int32, (group * tok, tok), 1)
    same = jnp.logical_not(jnp.logical_xor(query >= first, key >= first))
    return jnp.logical_and(same, key <= query)


def softmax_rows(queries, keys, allowed):
    raw = times_transpose(queries, keys) * HEAD_DIM**-0.5
    scores = jnp.where(allowed, raw, NEGATIVE)
    terms = jnp.exp(scores - jnp.max(scores, axis=-1, keepdims=True))
    return terms / jnp.sum(terms, axis=-1, keepdims=True)


def head_rows(array, head, count):
    return jnp.concatenate(
        [array[:, (head + k) * HEAD_DIM : (head + k + 1) * HEAD_DIM] for k in range(count)], axis=0
    )


def attend_kernel(
    slot_ref, first_ref, x_ref, gain_ref, cos_ref, sin_ref, wq_hbm, wk_hbm, wv_hbm, wo_hbm, *refs
):
    part_ref, normed_ref, attended_ref, kept_ref, wq, wk, wv, wo, sems = refs[-9:]
    copies = [
        pltpu.make_async_copy(src, dst, sems.at[k])
        for k, (src, dst) in enumerate(((wq_hbm, wq), (wk_hbm, wk), (wv_hbm, wv), (wo_hbm, wo)))
    ]
    for copy in copies:
        copy.start()
    x = x_ref[...].astype(F32)
    inverse = lax.rsqrt(jnp.mean(x * x, axis=-1, keepdims=True) + EPS)
    normed = (x * inverse * gain_ref[...].astype(F32)).astype(BF16)
    normed_ref[...] = normed
    first = first_ref[slot_ref[0]]
    cosine, sine = row_turns(first, cos_ref, sin_ref)
    tok = x.shape[0]
    heads = wq.shape[1] // HEAD_DIM
    kv = wk.shape[1] // HEAD_DIM
    group = heads // kv
    copies[0].wait()
    lin = jnp.dot(normed, wq[...], preferred_element_type=F32)
    queries = jnp.concatenate(
        [turn(lin[:, k * 128 : (k + 1) * 128], cosine, sine).astype(BF16) for k in range(heads // 2)], axis=1
    )
    copies[1].wait()
    lin = jnp.dot(normed, wk[...], preferred_element_type=F32)
    keys = jnp.concatenate(
        [turn(lin[:, k * 128 : (k + 1) * 128], cosine, sine).astype(BF16) for k in range(kv // 2)], axis=1
    )
    copies[2].wait()
    values = jnp.dot(normed, wv[...], preferred_element_type=F32).astype(BF16)
    kept_ref[:, : heads * HEAD_DIM] = queries
    kept_ref[:, heads * HEAD_DIM : (heads + kv) * HEAD_DIM] = keys
    kept_ref[:, (heads + kv) * HEAD_DIM :] = values
    allowed = allowed_pairs(first, tok, group)
    mixed = []
    for k in range(kv):
        lanes = slice(k * HEAD_DIM, (k + 1) * HEAD_DIM)
        prob = softmax_rows(head_rows(queries, k * group, group), keys[:, lanes], allowed).astype(BF16)
        out = jnp.dot(prob, values[:, lanes], preferred_element_type=F32)
        mixed += [out[g * tok : (g + 1) * tok] for g in range(group)]
    attended = jnp.concatenate(mixed, axis=1).astype(BF16)
    attended_ref[0] = attended.astype(F32)
    copies[3].wait()
    part_ref[...] = jnp.dot(attended, wo[...], preferred_element_type=F32)


def attend(entry, slot, first_len, tokens, gain, tables, attended, w_query, w_key, w_value, w_output):
    tok, wide = tokens.shape[0] // 2, tokens.shape[1]
    cols = w_query.shape[1]
    kv_cols = w_key.shape[1]
    weights = (w_query, w_key, w_value, w_output)
    aliased = () if attended is None else (attended,)

    def whole(array):
        return pl.BlockSpec(array.shape, lambda j, s: (0,) * array.ndim)

    return pl.pallas_call(
        attend_kernel,
        grid_spec=pltpu.PrefetchScalarGridSpec(
            num_scalar_prefetch=1,
            grid=(1,),
            in_specs=[
                pl.BlockSpec(memory_space=pltpu.SMEM),
                pl.BlockSpec((tok, wide), lambda j, s: (s[0], 0)),
                whole(gain),
                whole(tables[0]),
                whole(tables[1]),
            ]
            + [pl.BlockSpec(memory_space=pl.ANY)] * (4 + len(aliased)),
            out_specs=[
                pl.BlockSpec((tok, wide), lambda j, s: (0, 0)),
                pl.BlockSpec((tok, wide), lambda j, s: (0, 0)),
                pl.BlockSpec((1, tok, cols), lambda j, s: (entry, 0, 0)),
                pl.BlockSpec((tok, cols + 2 * kv_cols), lambda j, s: (0, 0)),
            ],
            scratch_shapes=[pltpu.VMEM(w.shape, w.dtype) for w in weights] + [pltpu.SemaphoreType.DMA((4,))],
        ),
        out_shape=[
            jax.ShapeDtypeStruct((tok, wide), F32),
            jax.ShapeDtypeStruct((tok, wide), BF16),
            jax.ShapeDtypeStruct((2, tok, cols), F32),
            jax.ShapeDtypeStruct((tok, cols + 2 * kv_cols), BF16),
        ],
        input_output_aliases={10: 2} if aliased else {},
        compiler_params=pltpu.CompilerParams(vmem_limit_bytes=ATTEND_VMEM),
        cost_estimate=cost(S_attend,
            2 * tok * wide * (2 * cols + 2 * kv_cols) + 4 * tok * tok * cols,
            sum(w.size * 2 for w in weights) + tok * wide * 8,
            tok * tok * cols // HEAD_DIM,
        ),
        name="attend",
    )(slot, first_len, tokens, gain, *tables, *weights, *aliased)


def attend_back_kernel(
    slot_ref, first_ref, live_ref, grad_ref, more_ref, middle_ref, cot_ref, gain_ref, kept_ref, cos_ref, sin_ref,
    wq_hbm, wk_hbm, wv_hbm, wo_hbm, *refs
):
    part_ref, grad_mid_ref, dm_ref, lin_ref, gain_out_ref, wq, wk, wv, wo, sems = refs[-10:]
    copies = [
        pltpu.make_async_copy(src, dst, sems.at[k])
        for k, (src, dst) in enumerate(((wq_hbm, wq), (wk_hbm, wk), (wv_hbm, wv), (wo_hbm, wo)))
    ]
    for k in (3, 0, 1, 2):
        copies[k].start()
    grad = grad_ref[...]
    if more_ref is not None:
        grad = grad + more_ref[...]
    middle = middle_ref[...]
    inverse = lax.rsqrt(jnp.mean(middle * middle, axis=-1, keepdims=True) + EPS)
    unit = middle * inverse
    gain_out_ref[...] = jnp.sum(grad * unit, axis=0, keepdims=True)
    scaled = grad * gain_ref[...].astype(F32)
    grad_mid = cot_ref[...].astype(F32) * live_flag(slot_ref, live_ref) + inverse * (
        scaled - unit * jnp.mean(scaled * unit, axis=-1, keepdims=True)
    )
    grad_mid_ref[...] = grad_mid
    dm = grad_mid.astype(BF16)
    dm_ref[...] = dm
    tok = dm.shape[0]
    heads = wq.shape[1] // HEAD_DIM
    kv = wk.shape[1] // HEAD_DIM
    group = heads // kv
    first = first_ref[slot_ref[0]]
    cosine, sine = row_turns(first, cos_ref, sin_ref)
    sine = -sine
    allowed = allowed_pairs(first, tok, group)
    copies[3].wait()
    grad_att = times_transpose(dm, wo[...]).astype(BF16)
    grad_q, grad_k, grad_v = [], [], []
    scale = HEAD_DIM**-0.5
    for k in range(kv):
        q_rows = head_rows(kept_ref, k * group, group)
        keys = kept_ref[:, (heads + k) * HEAD_DIM : (heads + k + 1) * HEAD_DIM]
        values = kept_ref[:, (heads + kv + k) * HEAD_DIM : (heads + kv + k + 1) * HEAD_DIM]
        prob = softmax_rows(q_rows, keys, allowed)
        d_rows = head_rows(grad_att, k * group, group)
        grad_v.append(contract_rows(prob.astype(BF16), d_rows))
        grad_prob = times_transpose(d_rows, values)
        delta = jnp.sum(prob * grad_prob, axis=-1, keepdims=True)
        grad_score = (prob * (grad_prob - delta)).astype(BF16)
        rows = jnp.dot(grad_score, keys, preferred_element_type=F32) * scale
        grad_q += [rows[g * tok : (g + 1) * tok] for g in range(group)]
        grad_k.append(contract_rows(grad_score, q_rows) * scale)

    def turned_back(parts):
        pairs = [jnp.concatenate(parts[k : k + 2], axis=1) for k in range(0, len(parts), 2)]
        return jnp.concatenate([turn(p, cosine, sine).astype(BF16) for p in pairs], axis=1)

    lin_q = turned_back(grad_q)
    lin_k = turned_back(grad_k)
    lin_v = jnp.concatenate(grad_v, axis=1).astype(BF16)
    cols, kv_cols = heads * HEAD_DIM, kv * HEAD_DIM
    lin_ref[0, :, :cols] = lin_q.astype(F32)
    lin_ref[0, :, cols : cols + kv_cols] = lin_k.astype(F32)
    lin_ref[0, :, cols + kv_cols :] = lin_v.astype(F32)
    for k in range(3):
        copies[k].wait()
    part_ref[...] = (
        times_transpose(lin_q, wq[...]) + times_transpose(lin_k, wk[...]) + times_transpose(lin_v, wv[...])
    )


def attend_back(
    entry, slot, first_len, live_rows, grads, middle, cotangent, gain, kept, tables, lin, w_query, w_key, w_value, w_output
):
    tok, wide = middle.shape
    cols = w_query.shape[1]
    kv_cols = w_key.shape[1]
    weights = (w_query, w_key, w_value, w_output)
    aliased = () if lin is None else (lin,)
    rows = pl.BlockSpec((tok, wide), lambda j, s: (0, 0))

    def whole(array):
        return pl.BlockSpec(array.shape, lambda j, s: (0,) * array.ndim)

    def kernel(slot_ref, first_ref, live_ref, grad_ref, *refs):
        if len(grads) == 1:
            refs = (None, *refs)
        attend_back_kernel(slot_ref, first_ref, live_ref, grad_ref, *refs)

    return pl.pallas_call(
        kernel,
        grid_spec=pltpu.PrefetchScalarGridSpec(
            num_scalar_prefetch=1,
            grid=(1,),
            in_specs=[
                pl.BlockSpec(memory_space=pltpu.SMEM),
                pl.BlockSpec(memory_space=pltpu.SMEM),
                *[rows] * (len(grads) + 1),
                pl.BlockSpec((tok, wide), lambda j, s: (s[0], 0)),
                whole(gain),
                whole(kept),
                whole(tables[0]),
                whole(tables[1]),
            ]
            + [pl.BlockSpec(memory_space=pl.ANY)] * (4 + len(aliased)),
            out_specs=[
                rows,
                rows,
                rows,
                pl.BlockSpec((1, tok, cols + 2 * kv_cols), lambda j, s: (entry, 0, 0)),
                pl.BlockSpec((1, wide), lambda j, s: (0, 0)),
            ],
            scratch_shapes=[pltpu.VMEM(w.shape, w.dtype) for w in weights] + [pltpu.SemaphoreType.DMA((4,))],
        ),
        out_shape=[
            jax.ShapeDtypeStruct((tok, wide), F32),
            jax.ShapeDtypeStruct((tok, wide), F32),
            jax.ShapeDtypeStruct((tok, wide), BF16),
            jax.ShapeDtypeStruct((2, tok, cols + 2 * kv_cols), F32),
            jax.ShapeDtypeStruct((1, wide), F32),
        ],
        input_output_aliases={13 + len(grads): 3} if aliased else {},
        compiler_params=pltpu.CompilerParams(vmem_limit_bytes=ATTEND_VMEM),
        cost_estimate=cost(S_attend_back,
            2 * tok * wide * (2 * cols + 2 * kv_cols) + 10 * tok * tok * cols,
            sum(w.size * 2 for w in weights) + tok * wide * 24,
            tok * tok * cols // HEAD_DIM,
        ),
        name="attend_back",
    )(slot, first_len, live_rows, *grads, middle, cotangent, gain, kept, *tables, *weights, *aliased)


def blocks_kernel(core_ref, first_ref, second_ref, own_ref, other_ref):
    rows = [
        ref[...].astype(F32) * core_ref[3 + k].astype(F32) for k, ref in enumerate((first_ref, second_ref))
    ]
    rows = jnp.concatenate(rows, axis=0)
    core = core_ref[0]
    for k in range(rows.shape[1] // 128):
        turned = jnp.transpose(rows[:, k * 128 : (k + 1) * 128])
        low, high = turned[:64], turned[64:]
        own_ref[k * 64 : (k + 1) * 64, :] = jnp.where(core == 0, low, high).astype(BF16)
        other_ref[k * 64 : (k + 1) * 64, :] = jnp.where(core == 0, high, low)


def by_block(choice, first, second):
    tok = 192
    chips = 8
    return pl.pallas_call(
        blocks_kernel,
        grid_spec=pltpu.PrefetchScalarGridSpec(
            num_scalar_prefetch=1,
            grid=(16 // chips,),
            in_specs=[
                pl.BlockSpec((tok, 128 * chips), lambda j, o: (o[1], j)),
                pl.BlockSpec((tok, 128 * chips), lambda j, o: (o[2], j)),
            ],
            out_specs=[pl.BlockSpec((64 * chips, 2 * tok), lambda j, o: (j, 0))] * 2,
        ),
        out_shape=[
            jax.ShapeDtypeStruct((1024, 2 * tok), BF16),
            jax.ShapeDtypeStruct((1024, 2 * tok), F32),
        ],
        compiler_params=pltpu.CompilerParams(vmem_limit_bytes=SMALL_VMEM),
        cost_estimate=cost(S_by_block, 0, 2048 * tok * 10),
        name="by_block",
    )(choice, first, second)


def live_flag(slot_ref, live_ref):
    return jnp.where(slot_ref[0] < live_ref[0], 1.0, 0.0)


def mlp_kernel(
    slot_ref, live_ref, middle_ref, cot_ref, gain_ref, wg_ref, wu_ref, wd_ref, *refs
):
    hidden_ref, act_ref, normed_ref, dy = refs[-4:]
    step = pl.program_id(0)

    @pl.when(step == 0)
    def _():
        middle = middle_ref[...]
        inverse = lax.rsqrt(jnp.mean(middle * middle, axis=-1, keepdims=True) + EPS)
        normed_ref[...] = (middle * inverse * gain_ref[...].astype(F32)).astype(BF16)
        dy[...] = (cot_ref[...].astype(F32) * live_flag(slot_ref, live_ref)).astype(BF16)

    n = normed_ref[...]
    w_gate = wg_ref[...]
    w_up = wu_ref[...]
    w_down = wd_ref[...]
    gate = jnp.dot(n, w_gate, preferred_element_type=F32)
    up = jnp.dot(n, w_up, preferred_element_type=F32)
    grad_hidden = times_transpose(dy[...], w_down)
    sig = 1.0 / (1.0 + jnp.exp(-gate))
    silu = gate * sig
    hidden = (silu * up).astype(BF16)
    d_gate = (grad_hidden * up * sig * (1.0 + gate * (1.0 - sig))).astype(BF16)
    d_up = (grad_hidden * silu).astype(BF16)
    hidden_ref[...] = hidden.astype(F32)
    act_ref[0] = d_gate.astype(F32)
    act_ref[1] = d_up.astype(F32)
    if len(refs) == 4:
        return
    grad_ref = refs[0]
    grad_part = times_transpose(d_gate, w_gate) + times_transpose(d_up, w_up)

    @pl.when(step == 0)
    def _():
        grad_ref[...] = grad_part

    @pl.when(step > 0)
    def _():
        grad_ref[...] += grad_part


def mlp(slot, live_rows, middle, cotangent, gain, w_gate, w_up, w_down, sums):
    tok, wide = middle.shape
    units = w_gate.shape[1]
    tile = 512
    whole = pl.BlockSpec((tok, wide), lambda t, s: (0, 0))
    return pl.pallas_call(
        mlp_kernel,
        grid_spec=pltpu.PrefetchScalarGridSpec(
            num_scalar_prefetch=1,
            grid=(units // tile,),
            in_specs=[
                pl.BlockSpec(memory_space=pltpu.SMEM),
                whole,
                pl.BlockSpec((tok, wide), lambda t, s: (s[0], 0)),
                pl.BlockSpec((1, wide), lambda t, s: (0, 0)),
                pl.BlockSpec((wide, tile), lambda t, s: (0, t)),
                pl.BlockSpec((wide, tile), lambda t, s: (0, t)),
                pl.BlockSpec((tile, wide), lambda t, s: (t, 0)),
            ],
            out_specs=[whole] * sums
            + [
                pl.BlockSpec((tok, tile), lambda t, s: (0, t)),
                pl.BlockSpec((2, tok, tile), lambda t, s: (0, 0, t)),
                whole,
            ],
            scratch_shapes=[pltpu.VMEM((tok, wide), BF16)],
        ),
        out_shape=[jax.ShapeDtypeStruct((tok, wide), F32)] * sums
        + [
            jax.ShapeDtypeStruct((tok, units), F32),
            jax.ShapeDtypeStruct((2, tok, units), F32),
            jax.ShapeDtypeStruct((tok, wide), BF16),
        ],
        compiler_params=pltpu.CompilerParams(vmem_limit_bytes=MLP_VMEM),
        cost_estimate=cost(S_mlp, 12 * tok * wide * units, 3 * wide * units * 2 + 5 * tok * wide * 4, tok * units),
        name="mlp",
    )(slot, live_rows, middle, cotangent, gain, w_gate, w_up, w_down)


def layer_part_kernel(k_ref, n_ref, wd_ref, out_k_ref, out_n_ref):
    rows = jnp.concatenate([k_ref[...], n_ref[...]], axis=0).astype(BF16)
    product = jnp.dot(rows, wd_ref[...], preferred_element_type=F32)
    tok = k_ref.shape[0]
    out_k_ref[...] = product[:tok]
    out_n_ref[...] = product[tok:]


def layer_part(hidden_k, hidden_n, w_down):
    tok, units = hidden_k.shape
    wide = w_down.shape[1]
    tile = 512
    return pl.pallas_call(
        layer_part_kernel,
        grid=(wide // tile,),
        in_specs=[
            pl.BlockSpec((tok, units), lambda t: (0, 0)),
            pl.BlockSpec((tok, units), lambda t: (0, 0)),
            pl.BlockSpec((units, tile), lambda t: (0, t)),
        ],
        out_specs=[pl.BlockSpec((tok, tile), lambda t: (0, t))] * 2,
        out_shape=[jax.ShapeDtypeStruct((tok, wide), F32)] * 2,
        compiler_params=pltpu.CompilerParams(vmem_limit_bytes=MLP_VMEM),
        cost_estimate=cost(S_mlp, 4 * tok * wide * units, wide * units * 2 + 4 * tok * wide * 4),
        name="layer_part",
    )(hidden_k, hidden_n, w_down)


def mlp_weight_kernel(dy_own, dy_other, two_own, two_other, *refs):
    hidden_refs, act_refs, out_ref, lhs = refs[:4], refs[4:8], refs[8], refs[9]
    tok = dy_own.shape[-1]
    step = pl.program_id(0)

    def product(own, other, rhs_refs, first):
        @pl.when(first)
        def _():
            lhs[:, :tok] = own[...]
            lhs[:, tok:] = other[...].astype(BF16)

        rhs = jnp.concatenate([ref[...].reshape(ref.shape[-2:]).astype(BF16) for ref in rhs_refs], axis=0)
        out_ref[...] = jnp.dot(lhs[...], rhs, preferred_element_type=F32)

    @pl.when(step < 2)
    def _():
        product(dy_own, dy_other, hidden_refs, step == 0)

    @pl.when(step >= 2)
    def _():
        product(two_own, two_other, act_refs, step == 2)


def mlp_weight_grad(dy_own, dy_other, two_own, two_other, hidden, acts):
    kinds, tok, cols = acts[0].shape
    tile = cols // 2
    whole = pl.BlockSpec(dy_own.shape, lambda j: (0, 0))

    def act_at(j):
        k = jnp.maximum(j - 2, 0)
        return (k // 2, 0, k % 2)

    return pl.pallas_call(
        mlp_weight_kernel,
        grid=(2 + 2 * kinds,),
        in_specs=[whole] * 4
        + [pl.BlockSpec((tok, tile), lambda j: (0, jnp.minimum(j, 1)))] * 4
        + [pl.BlockSpec((1, tok, tile), act_at)] * 4,
        out_specs=pl.BlockSpec((1024, tile), lambda j: (0, j)),
        scratch_shapes=[pltpu.VMEM((1024, 4 * tok), BF16)],
        out_shape=jax.ShapeDtypeStruct((1024, (2 + 2 * kinds) * tile), F32),
        compiler_params=pltpu.CompilerParams(vmem_limit_bytes=WEIGHT_VMEM),
        cost_estimate=cost(S_mlp_weight_grad, 2 * 1024 * 4 * tok * 6 * tile, (1024 + 4 * tok) * 6 * tile * 4),
        name="mlp_weight_grad",
    )(dy_own, dy_other, two_own, two_other, *hidden, *acts)


def tokens_kernel(slot_ref, grad_ref, mid_ref, x_ref, gain_ref, *refs):
    out_ref, gain_out_ref = refs[-2:]
    grad = grad_ref[...]
    x = x_ref[...].astype(F32)
    inverse = lax.rsqrt(jnp.mean(x * x, axis=-1, keepdims=True) + EPS)
    unit = x * inverse
    scaled = grad * gain_ref[...].astype(F32)
    out_ref[...] = mid_ref[...] + inverse * (scaled - unit * jnp.mean(scaled * unit, axis=-1, keepdims=True))
    gain_part = jnp.sum(grad * unit, axis=0, keepdims=True)

    @pl.when(pl.program_id(0) == 0)
    def _():
        gain_out_ref[...] = gain_part

    @pl.when(pl.program_id(0) > 0)
    def _():
        gain_out_ref[...] += gain_part


def tokens_slot(slot, grad, grad_mid, tokens, gain, whole):
    tok, wide = grad.shape
    parts = 2
    tile = tok // parts
    aliased = () if whole is None else (whole,)
    rows = pl.BlockSpec((tile, wide), lambda j, s: (j, 0))
    in_whole = pl.BlockSpec((tile, wide), lambda j, s: (s[0] * parts + j, 0))
    line = pl.BlockSpec((1, wide), lambda j, s: (0, 0))
    return pl.pallas_call(
        tokens_kernel,
        grid_spec=pltpu.PrefetchScalarGridSpec(
            num_scalar_prefetch=1,
            grid=(parts,),
            in_specs=[rows, rows, in_whole, line] + [pl.BlockSpec(memory_space=pl.ANY)] * len(aliased),
            out_specs=[in_whole, line],
        ),
        out_shape=[jax.ShapeDtypeStruct((2 * tok, wide), F32), jax.ShapeDtypeStruct((1, wide), F32)],
        input_output_aliases={5: 0} if aliased else {},
        compiler_params=pltpu.CompilerParams(vmem_limit_bytes=SMALL_VMEM),
        cost_estimate=cost(S_tk if whole is None else S_tn, 10 * tok * wide, 14 * tok * wide),
        name="grad_tokens",
    )(slot, grad, grad_mid, tokens, gain, *aliased)


def layer_kernel(slot_ref, live_ref, middle_ref, sum_ref, *refs):
    refs[-1][...] = (live_flag(slot_ref, live_ref) * (middle_ref[...] + sum_ref[...])).astype(BF16)


def layer_slot(slot, live_rows, middle, added, whole):
    tok, wide = middle.shape
    parts = 2
    tile = tok // parts
    aliased = () if whole is None else (whole,)
    rows = pl.BlockSpec((tile, wide), lambda j, s: (j, 0))
    return pl.pallas_call(
        layer_kernel,
        grid_spec=pltpu.PrefetchScalarGridSpec(
            num_scalar_prefetch=1,
            grid=(parts,),
            in_specs=[pl.BlockSpec(memory_space=pltpu.SMEM), rows, rows]
            + [pl.BlockSpec(memory_space=pl.ANY)] * len(aliased),
            out_specs=pl.BlockSpec((tile, wide), lambda j, s: (s[0] * parts + j, 0)),
        ),
        out_shape=jax.ShapeDtypeStruct((2 * tok, wide), BF16),
        input_output_aliases={4: 0} if aliased else {},
        compiler_params=pltpu.CompilerParams(vmem_limit_bytes=SMALL_VMEM),
        cost_estimate=cost(S_lk if whole is None else S_ln, 2 * tok * wide, 10 * tok * wide),
        name="layer_out",
    )(slot, live_rows, middle, added, *aliased)


def weight_kernel(order_ref, own_ref, other_ref, k_ref, n_ref, k_other_ref, n_other_ref, *refs):
    send_ref, keep_ref, lhs = refs[-3:]
    tok = own_ref.shape[-1]
    cols = k_ref.shape[-1]
    for place in range(16):
        chip = pl.multiple_of(order_ref[place] * 64, 64)
        lhs[pl.ds(place * 64, 64), :tok] = own_ref[pl.ds(chip, 64), :]
        lhs[pl.ds(place * 64, 64), tok:] = other_ref[pl.ds(chip, 64), :].astype(BF16)
        if len(refs) > 3:
            half = (send_ref, keep_ref)[place // 8]
            half[pl.ds(place % 8 * 64, 64), cols:] = refs[0][pl.ds(chip, 64), :]
    rhs = jnp.concatenate([ref[0].astype(BF16) for ref in (k_ref, n_ref, k_other_ref, n_other_ref)], axis=0)
    send_ref[:, :cols] = jnp.dot(lhs[:512], rhs, preferred_element_type=F32)
    keep_ref[:, :cols] = jnp.dot(lhs[512:], rhs, preferred_element_type=F32)


def weight_grad(order, own, other, here, there, extra=()):
    _, tok, cols = here.shape
    wide = cols + sum(e.shape[1] for e in extra)

    def whole(array):
        return pl.BlockSpec(array.shape, lambda j, o: (0, 0))

    first = pl.BlockSpec((1, tok, cols), lambda j, o: (0, 0, 0))
    second = pl.BlockSpec((1, tok, cols), lambda j, o: (1, 0, 0))
    return pl.pallas_call(
        weight_kernel,
        grid_spec=pltpu.PrefetchScalarGridSpec(
            num_scalar_prefetch=1,
            grid=(1,),
            in_specs=[whole(own), whole(other), first, second, first, second] + [whole(e) for e in extra],
            out_specs=[pl.BlockSpec((512, wide), lambda j, o: (0, 0))] * 2,
            scratch_shapes=[pltpu.VMEM((1024, 4 * tok), BF16)],
        ),
        out_shape=[jax.ShapeDtypeStruct((512, wide), F32)] * 2,
        compiler_params=pltpu.CompilerParams(vmem_limit_bytes=WEIGHT_VMEM),
        cost_estimate=cost(S_weight_grad, 2 * 1024 * 4 * tok * cols, (1024 + 4 * tok) * wide * 4 + 1024 * tok * 12),
        name="weight_grad",
    )(order, own, other, here, here, there, there, *extra)


PLANES = [[chip * 2 + core for chip in range(16)] for core in range(2)]


def plane_sum(array):
    return lax.psum_scatter(array, "dp", scatter_dimension=0, axis_index_groups=PLANES, tiled=True)


class Piece:
    def __init__(self, stream, send, keep):
        self.perms, self.send, self.keep, self.step = STREAMS[stream], send, keep, 0

    def exchange(self):
        got = swap(self.send, self.perms[self.step])
        self.step += 1
        rows = self.keep.shape[0] // 2
        if self.step == 4:
            self.keep = self.keep + got
        else:
            self.send, self.keep = self.keep[:rows] + got[:rows], self.keep[rows:] + got[rows:]
        return got


def hold(value, pieces, when=True):
    if not when:
        return value
    value, *sends = tie(value, *[p.send for p in pieces])
    for p, send in zip(pieces, sends):
        p.send = send
    return value


def tie(*arrays):
    return lax.optimization_barrier(arrays)


def on_device(
    tokens,
    norm1_gain,
    w_query,
    w_key,
    w_value,
    w_output,
    norm2_gain,
    w_gate,
    w_up,
    w_down,
    cotangent,
    first_len,
    live_rows,
):
    dp = lax.axis_index("dp")
    y = lax.axis_index("tensor")
    z, x, c = dp // 8, (dp // 2) % 4, dp % 2
    slot = jnp.where(c == 0, low_bit(y), high_bit(y))
    orders = [block_order(s, z, x, c).astype(jnp.int32) for s in range(2)]
    tok, wide = tokens.shape
    gain_one = norm1_gain[None]
    gain_two = norm2_gain[None]
    tables = turn_tables(tok // 2)
    slot_k = jnp.reshape(slot, (1,)).astype(jnp.int32)
    slot_n = 1 - slot_k
    core = jnp.reshape(c, (1,)).astype(jnp.int32)
    plain = jnp.concatenate([core, jnp.array([0, 0, 1, 1], jnp.int32)])
    live = [(s < live_rows).astype(jnp.int32) for s in (slot_k, slot_n)]
    masked = jnp.concatenate([core, slot_k, slot_n, *live])

    weights = (w_query, w_key, w_value, w_output)
    part_n, one_n, attended, kept_n = attend(1, slot_n, first_len, tokens, gain_one, tables, None, *weights)
    got = swap(part_n, ALONG_Y[0])
    part_k, one_k, attended, kept_k = attend(0, slot_k, first_len, tokens, gain_one, tables, attended, *weights)
    if B1:
        masked, plain, part_k = tie(masked, plain, part_k)
    half = part_k + got
    x_k = lax.dynamic_slice_in_dim(tokens, slot * (tok // 2), tok // 2, 0).astype(F32)
    middle_k = x_k + half + swap(half, ALONG_Y[1])
    dy_own, dy_other = by_block(masked, cotangent, cotangent)
    dy_other = swap(dy_other, OTHER_CORE)
    one_own, one_other = by_block(plain, one_k, one_n)
    one_other = swap(one_other, OTHER_CORE)
    attended_other = swap(attended, OTHER_CORE)
    if B2:
        middle_k, dy_other, one_other, attended_other = tie(middle_k, dy_other, one_other, attended_other)

    feed = (w_gate, w_up, w_down)
    middle_n = swap(middle_k, ALONG_Y[0])
    back_k, hidden_k, act_k, two_k = mlp(slot_k, live_rows, middle_k, cotangent, gain_two, *feed, True)
    got = swap(back_k, ALONG_Y[0])
    hidden_k_other = swap(hidden_k, OTHER_CORE)
    act_k_other = swap(act_k, OTHER_CORE)
    slot_n, two_k = tie(slot_n, two_k)
    back_n, hidden_n, act_n, two_n = mlp(slot_n, live_rows, middle_n, cotangent, gain_two, *feed, True)
    hidden_n_other = swap(hidden_n, OTHER_CORE)
    act_n_other = swap(act_n, OTHER_CORE)
    plain, hidden_k_other, got = tie(plain, hidden_k_other, got)
    two_own, two_other = by_block(plain, two_k, two_n)
    two_other = swap(two_other, OTHER_CORE)

    half = back_n + got
    dy_own, half = tie(dy_own, half)
    got = swap(half, ALONG_Y[1])
    hidden = (hidden_k, hidden_n, hidden_k_other, hidden_n_other)
    grads = mlp_weight_grad(dy_own, dy_other, two_own, two_other, hidden, (act_k, act_n, act_k_other, act_n_other))
    if B4:
        got, grads = tie(got, grads)
    grad_2n = half + got
    slot_b = slot_n
    if I2:
        hidden_n, grads = tie(hidden_n, grads)
        out_k, out_n = layer_part(hidden_k, hidden_n, w_down)
        slot_b, out_k = tie(slot_b, out_k)

    grads = plane_sum(grads)
    grad_2k = swap(grad_2n, ALONG_Y[0])
    back_n, grad_mid_n, dm_n, lin, gain_2 = attend_back(
        1, slot_b, first_len, live_rows, (half, got), middle_n, cotangent, gain_two, kept_n, tables, None, *weights
    )
    if not I2:
        if D1:
            hidden_n, back_n = tie(hidden_n, back_n)
        out_k, out_n = layer_part(hidden_k, hidden_n, w_down)
    if I3:
        out_n, back_n = tie(out_n, back_n)
    got = swap(back_n, ALONG_Y[0])
    slot_b = slot_k
    if I1:
        slot_b, out_k = tie(slot_b, out_k)
    back_k, grad_mid_k, dm_k, lin, _ = attend_back(
        0, slot_b, first_len, live_rows, (grad_2k,), middle_k, cotangent, gain_two, kept_k, tables, lin, *weights
    )
    if E3:
        out_n, back_k = tie(out_n, back_k)
    out_got = swap(out_n, ALONG_Y[0])
    lin_other = swap(lin, OTHER_CORE)
    dm_own, dm_other = by_block(plain, dm_k, dm_n)
    order_0 = orders[0]
    if G1:
        order_0, got = tie(order_0, got)
    dm_other = swap(dm_other, OTHER_CORE)
    lin_grad = weight_grad(order_0, one_own, one_other, lin, lin_other)
    out_grad = weight_grad(orders[1], dm_own, dm_other, attended, attended_other)
    three = [Piece(0, *lin_grad), Piece(1, *out_grad)]
    back_k = hold(back_k, three, B7)
    half = back_k + got
    grad_1k = half + swap(half, ALONG_Y[1])
    out_half = out_k + out_got
    for p in three:
        p.exchange()
    if G2:
        grad_1k = hold(grad_1k, three)
    if G4:
        out_half = hold(out_half, three)
    out_sum = out_half + swap(out_half, ALONG_Y[1])
    out_other = swap(out_sum, ALONG_Y[0])
    out_kept = out_sum
    for p in three:
        p.exchange()

    grad_1n = swap(grad_1k, ALONG_Y[0])
    if G3:
        grad_1n = hold(grad_1n, three)
    if G5:
        out_kept = hold(out_sum, three)
    slot_t = slot_k
    grad_tokens, gain_1 = tokens_slot(slot_t, grad_1k, grad_mid_k, tokens, gain_one, None)

    gains = jnp.concatenate([gain_1, gain_2], axis=0)
    gains = gains + swap(gains, ALONG_Y[0])
    gains = jnp.transpose(gains.reshape(2, 16, 2, 64), (2, 1, 0, 3)).reshape(2, 16, 128)
    mine = lax.dynamic_index_in_dim(gains, c, keepdims=False)
    theirs = lax.dynamic_index_in_dim(gains, 1 - c, keepdims=False)
    mine = mine + swap(theirs, OTHER_CORE)
    picks = orders[0][:, None] == jnp.arange(16, dtype=jnp.int32)[None, :]
    mine = jnp.sum(jnp.where(picks[:, :, None], mine[None], 0.0), axis=1)
    for perm in STREAMS[0][:2]:
        rows = mine.shape[0] // 2
        mine = mine[rows:] + swap(mine[:rows], perm)
    mine = hold(mine, three, D8)
    for perm in STREAMS[0][2:]:
        rows = mine.shape[0] // 2
        mine = mine[rows:] + swap(mine[:rows], perm)
    for p in three:
        p.exchange()
    if H3:
        out_other = hold(out_other, three)
    for p in three:
        if p.step < 4:
            p.exchange()
    query_key_value, output = [p.keep for p in three]

    layer_out = layer_slot(slot_k, live_rows, middle_k, out_kept, None)
    layer_out = layer_slot(slot_n, live_rows, middle_n, out_other, layer_out)
    grad_tokens, _ = tokens_slot(slot_n, grad_1n, grad_mid_n, tokens, gain_one, grad_tokens)

    return (
        layer_out,
        grad_tokens,
        mine[0, :64],
        query_key_value[:, :512],
        query_key_value[:, 512:640],
        query_key_value[:, 640:],
        jnp.transpose(output),
        mine[0, 64:],
        grads[:, 2048:4096],
        grads[:, 4096:],
        jnp.transpose(grads[:, :2048]),
    )


def solution(mesh):
    placed = (
        P("dp", None),
        P(),
        P(None, "tensor"),
        P(None, "tensor"),
        P(None, "tensor"),
        P("tensor", None),
        P(),
        P(None, "tensor"),
        P(None, "tensor"),
        P("tensor", None),
        P("dp", None),
        P("dp"),
        P("dp"),
    )
    return jax.shard_map(
        on_device,
        mesh=mesh,
        in_specs=placed,
        out_specs=(
            P("dp", None),
            P("dp", None),
            P("dp"),
            P("dp", "tensor"),
            P("dp", "tensor"),
            P("dp", "tensor"),
            P("tensor", "dp"),
            P("dp"),
            P("dp", "tensor"),
            P("dp", "tensor"),
            P("tensor", "dp"),
        ),
        check_vma=False,
    )
```
